32 devices in a mesh: rep: 4 (over y, core), fsdp: 8 (over z, x).
Axes of the slice: x: 2, y: 2, z: 4, core: 2. Of those that a mesh axis runs over, the one named last changes fastest.
Arguments:
- activations: bfloat16 [4, 3072, 4096], P('rep', 'fsdp'), may hold values from -6 to 6
- kv_weight: bfloat16 [4, 4096, 1024], P('rep', 'fsdp'), may hold values from -0.09375 to 0.09375
- kv_cotangent: bfloat16 [4, 3072, 1024], P('rep', 'fsdp'), may hold values from -6 to 6
- first_moment: float32 [4, 4096, 1024], P('rep', 'fsdp'), may hold values from -48 to 48
- second_moment: float32 [4, 4096, 1024], P('rep', 'fsdp'), may hold values from 10 to 1000
- partner: int32 [4], replicated, may hold values from 0 to 3, as said below
- mix_numerator: int32 [4], replicated, may hold values from 8 to 56
Outputs:
- kv_out: bfloat16 [4, 3072, 1024], P('rep', 'fsdp')
- x_grad: bfloat16 [4, 3072, 4096], P('rep', 'fsdp')
- new_weight: bfloat16 [4, 4096, 1024], P('rep', 'fsdp')
- new_first: float32 [4, 4096, 1024], P('rep', 'fsdp')
- new_second: float32 [4, 4096, 1024], P('rep', 'fsdp')
The draws below stay inside these ranges and needn't reach their ends.
Inputs may be any that keep to these rules, and one draw needn't show every extreme that they name: partner[partner[r]] == r and partner[r] != r for every replica r.
All inputs are finite; a program needn't handle non-finite values.
Results may differ from the reference program's by a relative error of at most 0.018.
Values may be sent and summed in bfloat16 or wider, within the bound.
No kernel may reach another device: no remote copies, remote signals or barrier semaphores. Data moves between devices by JAX's collectives and lax.ppermute only.
A program may use at most 128 MiB of HBM per device.

```python
import math
import jax
import jax.numpy as jnp
from jax import lax

D = 4096
KV2 = 1024
TOK_DEV = 384
TOKENS = 3072
N_REP = 4
N_FSDP = 8


def draw_partner(key, part):
    shuffled = jax.random.permutation(jax.random.fold_in(key, 7), N_REP).astype(jnp.int32)
    leading = shuffled[0::2]
    trailing = shuffled[1::2]
    matches = jnp.zeros((N_REP,), jnp.int32).at[leading].set(trailing).at[trailing].set(leading)
    return matches


def with_ends(entries, stream_key, low, largest):
    spot = [jax.random.randint(jax.random.fold_in(stream_key, axis), (), 0, length) for axis, length in enumerate(entries.shape)]
    main_axis = entries.shape.index(max(entries.shape))
    neighbour = spot[:main_axis] + [(spot[main_axis] + 1) % entries.shape[main_axis]] + spot[main_axis + 1:]
    return entries.at[tuple(spot)].set(low).at[tuple(neighbour)].set(largest)


def spiked(result, rng, source, target, parts, factor):
    owner, partner = [(jnp.arange(result.shape[position]) // (result.shape[position] // parts)).reshape([-1 if axis == position else 1 for axis in range(result.ndim)]) for position in (source, target)]
    chosen = jax.random.permutation(rng, parts)[partner]
    strong = (owner == chosen) | (owner == (partner + parts // 2) % parts)
    return jnp.where(strong, factor * result, result)


def shard_levels(own_key, dims, pieces, least, top_value):
    def one(dim, parts):
        heights = jax.random.uniform(jax.random.fold_in(jax.random.fold_in(own_key, 6), dim), (parts,), jnp.float32, least / len(pieces), top_value / len(pieces))
        return jnp.repeat(jnp.exp(heights), dims[dim] // parts).reshape((-1,) + (1,) * (len(dims) - dim - 1))

    loudness = one(*pieces[0])
    for cut in pieces[1:]:
        loudness = loudness * one(*cut)
    return loudness


def noise(stream_key, extent, spread, bound, split=(), kind=jnp.bfloat16):
    values = jax.random.normal(stream_key, extent, jnp.float32) * spread
    if len(split) > 0:
        values = shard_levels(stream_key, extent, split, -0.22, 0.18) * values
    return jnp.clip(values, min=-bound, max=bound).astype(kind)


def heavy_noise(own_key, dims, scale, bound, shards, heavy, dtype=jnp.bfloat16):
    values = scale * jax.random.normal(own_key, dims, jnp.float32)
    if shards:
        values = values * shard_levels(own_key, dims, shards, -0.22, 0.18)
    return jnp.clip(spiked(values, jax.random.fold_in(own_key, 3), *heavy), -bound, bound).astype(dtype)


def setup_inputs(seed: int = 0) -> dict:
    splits = jax.random.split(jax.random.key(seed), 8)
    return {
        "activations": heavy_noise(splits[0], (N_REP, TOKENS, D), 1.0, 6.0, ((0, 4), (1, 8)), (1, 2, 8, 2.0)),
        "kv_weight": noise(splits[1], (N_REP, D, KV2), D ** -0.5, 0.09375, ((0, 4), (1, 8))),
        "kv_cotangent": noise(splits[2], (N_REP, TOKENS, KV2), 1.0, 6.0, ((0, 4), (1, 8))),
        "first_moment": noise(splits[3], (N_REP, D, KV2), 8.0, 48.0, ((0, 4), (1, 8)), jnp.float32),
        "second_moment": jnp.clip(jnp.exp(math.log(1000.0) - 4.6051702 * jax.random.uniform(splits[4], (N_REP, D, KV2), jnp.float32) ** shard_levels(splits[4], (N_REP, D, KV2), ((0, 4), (1, 8)), -0.2, 0.2)), 10.0, 1000.0),
        "partner": draw_partner(jax.random.fold_in(splits[7], 71), 0),
        "mix_numerator": with_ends(jax.random.randint(splits[6], (N_REP,), 8, 57), jax.random.fold_in(splits[6], 1), 8, 56).astype(jnp.int32),
    }


beta_one = 0.9
beta_two = 0.999
learn_rate = 0.02
weight_decay = 0.1
adam_eps = 1e-08
corr_one = 1.0 - beta_one ** 10
corr_two = 1.0 - beta_two ** 10
mix_denom = 64.0

def reference(activations, kv_weight, kv_cotangent, first_moment, second_moment, partner, mix_numerator):

    def per_replica(inputs):
        tokens_in, weights, cotangent, moment_a, moment_b = inputs
        keys_values = jnp.dot(tokens_in, weights, preferred_element_type=jnp.float32).astype(jnp.bfloat16)
        input_grad = jnp.dot(cotangent, weights.T, preferred_element_type=jnp.float32).astype(jnp.bfloat16)
        token_groups = tokens_in.reshape(N_FSDP, TOK_DEV, D)
        cot_groups = cotangent.reshape(N_FSDP, TOK_DEV, KV2)

        def add_group(running, couple):
            partial_term = jnp.dot(couple[0].T, couple[1], preferred_element_type=jnp.float32).astype(jnp.bfloat16)
            partial_term = lax.optimization_barrier(partial_term)
            return (running + partial_term.astype(jnp.float32), None)
        gradient, _ = lax.scan(add_group, jnp.zeros((D, KV2), jnp.float32), (token_groups, cot_groups))
        moment_new_a = beta_one * moment_a + (1.0 - beta_one) * gradient
        moment_new_b = beta_two * moment_b + (1.0 - beta_two) * gradient * gradient
        old_weight = weights.astype(jnp.float32)
        update = moment_new_a / corr_one / (jnp.sqrt(moment_new_b / corr_two) + adam_eps) + weight_decay * old_weight
        stepped = (old_weight - learn_rate * update).astype(jnp.bfloat16)
        return (keys_values, input_grad, stepped, moment_new_a, moment_new_b)
    kv_out, x_grad, stepped, new_first, new_second = lax.map(per_replica, (activations, kv_weight, kv_cotangent, first_moment, second_moment))
    mixing = mix_numerator.astype(jnp.float32) / mix_denom
    partner_rows = jnp.take(stepped, partner.astype(jnp.int32), axis=0)
    new_weight = ((1.0 - mixing)[:, None, None] * stepped.astype(jnp.float32) + mixing[:, None, None] * partner_rows.astype(jnp.float32)).astype(jnp.bfloat16)
    return (kv_out, x_grad, new_weight, new_first, new_second)
```

```python
import functools

import jax
import jax.numpy as jnp
import numpy as np
from jax import lax
from jax.experimental import pallas as pl
from jax.experimental.pallas import tpu as pltpu
from jax.sharding import PartitionSpec as P

beta_one = 0.9
beta_two = 0.999
learn_rate = 0.02
weight_decay = 0.1
adam_eps = 1e-08
corr_one = 1.0 - beta_one**10
corr_two = 1.0 - beta_two**10
mix_denom = 64.0

CHUNKS = 2
MIB = 1 << 20
ANY = pl.BlockSpec(memory_space=pl.ANY)

TN = (((0,), (0,)), ((), ()))
NT = (((1,), (1,)), ((), ()))


def dot(a, b, dims=(((1,), (0,)), ((), ()))):
    return lax.dot_general(a, b, dims, preferred_element_type=jnp.float32)


class Plan:
    def __init__(self, n):
        self.depth = depth = n // 2
        self.columns = {}
        self.rows = [[] for _ in range(n)]
        order = [
            sorted(range(depth), key=lambda q: (-abs(q - z), (q < z) != (2 * z >= depth)))
            for z in range(depth)
        ]
        self.sources = [set() for _ in range(depth)]
        arrivals = []
        for z in range(depth):
            ups = [(z - t, ("up", t)) for t in range(1, z + 1)]
            downs = [(z + t, ("dn", t)) for t in range(1, depth - z)]
            arrivals.append(downs + ups if 2 * z < depth else ups + downs)
            for j, (_, source) in enumerate(arrivals[z], 1):
                self.sources[j].add(source)
        self.sources = [sorted(s) for s in self.sources]
        for i in range(n):
            z, x = divmod(i, 2)
            put = functools.partial(self._put, i)
            put("own", i)
            for k in range(depth):
                put(f"pack{k}", 2 * order[z][k] + 1 - x)
            for s in range(2, depth + 1):
                for way, q in (("up", z + 1 + depth - s), ("dn", z - 1 - depth + s)):
                    add = 0 <= q < depth
                    put(f"add_{way}{s}", int(add))
                    put(f"blk_{way}{s}", 2 * q + x if add else 0)
                    put(f"pos_{way}{s}", order[z].index(q) if add else 0)
            for j in range(depth):
                q, source = (z, None) if j == 0 else arrivals[z][j - 1]
                put(f"mine{j}", 2 * q + x)
                put(f"theirs{j}", 2 * q + 1 - x)
                put(f"piece{j}", order[z].index(q))
                put(f"source{j}", 0 if j == 0 else self.sources[j].index(source))
        self.table = np.asarray(self.rows, np.int32)

    def _put(self, i, name, value):
        column = self.columns.setdefault(name, len(self.columns))
        assert column == len(self.rows[i])
        self.rows[i].append(value)

    def __getitem__(self, name):
        return self.columns[name]


def call(kernel, row, ins, outs, grid=(1,), aliases=None, scratch=(), flops=0, moved=0, vmem=24):
    return pl.pallas_call(
        kernel,
        grid_spec=pltpu.PrefetchScalarGridSpec(
            num_scalar_prefetch=1,
            grid=grid,
            in_specs=[spec for _, spec in ins],
            out_specs=[spec for _, spec in outs],
            scratch_shapes=list(scratch),
        ),
        out_shape=[shape for shape, _ in outs],
        input_output_aliases=aliases or {},
        compiler_params=pltpu.CompilerParams(vmem_limit_bytes=vmem * MIB),
        cost_estimate=pl.CostEstimate(flops=flops, bytes_accessed=moved, transcendentals=0),
    )(row, *[array for array, _ in ins])


def whole(array):
    rank = array.ndim
    return pl.BlockSpec(array.shape, lambda g, row: (0,) * rank)


def block(shape, column, scale=1, offset=0):
    return pl.BlockSpec(shape, lambda g, row: (0, row[column] * scale + offset))


def struct(shape, dtype):
    return jax.ShapeDtypeStruct(shape, dtype)


def pack(plan, row, act, width, k, after):
    def kernel(row_ref, act_ref, *refs):
        refs[-1][...] = act_ref[...]

    tokens = act.shape[0]
    return call(
        kernel,
        row,
        [(act, block((tokens, width), plan[f"pack{k}"]))] + [(a, ANY) for a in after],
        [(struct((tokens, width), act.dtype), pl.BlockSpec((tokens, width), lambda g, row: (0, 0)))],
        moved=4 * tokens * width,
    )[0]


def relay(plan, row, s, h, got, act, pieces, cot_own, cot_oth):
    tokens, columns = cot_own.shape
    rows = got["up"].shape[0]
    count = len(pieces)
    ways = ("up", "dn")

    def kernel(row_ref, *refs):
        got_refs, act_refs = refs[0:2], refs[2:4]
        piece_refs = refs[4 : 4 + count]
        own_ref, oth_ref = refs[4 + count : 6 + count]
        out_refs = refs[6 + count : 8 + count]
        held = refs[8 + count]
        for d, way in enumerate(ways):
            add = row_ref[plan[f"add_{way}{s}"]]
            pos = row_ref[plan[f"pos_{way}{s}"]]

            @pl.when(add == 0)
            def _():
                out_refs[d][...] = got_refs[d][...]

            @pl.when(add == 1)
            def _():
                for j in range(count):

                    @pl.when(pos == j)
                    def _():
                        held[...] = piece_refs[j][...]

                total = dot(act_refs[d][...], own_ref[...], TN)
                total = total + dot(held[...], oth_ref[...], TN)
                out_refs[d][...] = (total + got_refs[d][...].astype(jnp.float32)).astype(jnp.bfloat16)

    ins = [(got[way], whole(got[way])) for way in ways]
    ins += [
        (act, block((tokens, rows), plan[f"blk_{way}{s}"], CHUNKS, h)) for way in ways
    ]
    ins += [(p, pl.BlockSpec((tokens, rows), lambda g, row: (0, h))) for p in pieces]
    ins += [(cot_own, whole(cot_own)), (cot_oth, whole(cot_oth))]
    out = struct((rows, columns), jnp.bfloat16)
    up, dn = call(
        kernel,
        row,
        ins,
        [(out, whole(out)), (out, whole(out))],
        scratch=[pltpu.VMEM((tokens, rows), jnp.bfloat16)],
        flops=8 * tokens * rows * columns,
        moved=8 * rows * columns + 4 * tokens * columns,
    )
    return {"up": up, "dn": dn}


def own_gradient(plan, row, act, piece, cot_own, cot_oth):
    tokens, columns = cot_own.shape
    rows = piece.shape[1]

    def kernel(row_ref, act_ref, piece_ref, own_ref, oth_ref, out_ref):
        total = dot(act_ref[...], own_ref[...], TN)
        out_ref[...] = total + dot(piece_ref[...], oth_ref[...], TN)

    out = struct((rows, columns), jnp.float32)
    return call(
        kernel,
        row,
        [
            (act, block((tokens, rows), plan["own"])),
            (piece, whole(piece)),
            (cot_own, whole(cot_own)),
            (cot_oth, whole(cot_oth)),
        ],
        [(out, whole(out))],
        flops=4 * tokens * rows * columns,
        moved=4 * rows * columns + 4 * tokens * columns,
    )[0]


def project(plan, row, j, candidates, act, pieces, cot_own, cot_oth, kept):
    tokens, columns = cot_own.shape
    rows = pieces[0].shape[1]
    parts = len(candidates[0])
    last = j == plan.depth - 1
    flat = [c for candidate in candidates for c in candidate]
    n_w, n_p = len(flat), len(pieces)

    def kernel(row_ref, *refs):
        w_refs = refs[:n_w]
        piece_refs = refs[n_w : n_w + n_p]
        act_ref, own_ref, oth_ref = refs[n_w + n_p : n_w + n_p + 3]
        rest = refs[n_w + n_p + 3 :]
        if j > 0:
            _, kv_own_in, kv_oth_in = rest[:3]
            rest = rest[3:]
        xg_own, xg_oth, kv_own, kv_oth, w_buf, p_buf, sems = rest
        size = rows // parts
        for c in range(len(candidates)):

            @pl.when(row_ref[plan[f"source{j}"]] == c)
            def _():
                copies = [
                    pltpu.make_async_copy(
                        w_refs[c * parts + p], w_buf.at[pl.ds(p * size, size)], sems.at[p]
                    )
                    for p in range(parts)
                ]
                for copy in copies:
                    copy.start()
                for copy in copies:
                    copy.wait()

        for p in range(n_p):

            @pl.when(row_ref[plan[f"piece{j}"]] == p)
            def _():
                copy = pltpu.make_async_copy(piece_refs[p], p_buf, sems.at[parts])
                copy.start()
                copy.wait()

        xg_oth[...] = dot(oth_ref[...], w_buf[...], NT).astype(jnp.bfloat16)
        xg_own[...] = dot(own_ref[...], w_buf[...], NT).astype(jnp.bfloat16)
        oth = dot(p_buf[...], w_buf[...])
        own = dot(act_ref[...], w_buf[...])
        if j > 0:
            oth = oth + kv_oth_in[...]
            own = own + kv_own_in[...]
        kv_oth[...] = oth.astype(kv_oth.dtype)
        kv_own[...] = own

    ins = [(w, ANY) for w in flat] + [(p, ANY) for p in pieces]
    ins += [
        (act, block((tokens, rows), plan[f"mine{j}"])),
        (cot_own, whole(cot_own)),
        (cot_oth, whole(cot_oth)),
    ]
    xg = struct(act.shape, jnp.bfloat16)
    aliases = {}
    if j > 0:
        xg_before, kv_own_before, kv_oth_before = kept
        first = 1 + len(ins)
        ins += [(xg_before, ANY), (kv_own_before, whole(kv_own_before)), (kv_oth_before, whole(kv_oth_before))]
        aliases = {first: 0, first + 1: 2}
    kv_own = struct((tokens, columns), jnp.float32)
    kv_oth = struct((tokens, columns), jnp.bfloat16 if last else jnp.float32)
    piece_out = struct((tokens, rows), jnp.bfloat16)
    return call(
        kernel,
        row,
        ins,
        [
            (xg, block((tokens, rows), plan[f"mine{j}"])),
            (piece_out, whole(piece_out)),
            (kv_own, whole(kv_own)),
            (kv_oth, whole(kv_oth)),
        ],
        aliases=aliases,
        scratch=[
            pltpu.VMEM((rows, columns), jnp.bfloat16),
            pltpu.VMEM((tokens, rows), jnp.bfloat16),
            pltpu.SemaphoreType.DMA((parts + 1,)),
        ],
        flops=8 * tokens * rows * columns,
        moved=20 * tokens * columns,
        vmem=32,
    )


def place(plan, row, xg, arrived):
    count = len(arrived)
    tokens, width = arrived[0].shape

    def kernel(row_ref, _, *refs):
        out_ref, sems = refs[count:]
        copies = []
        for j in range(count):
            start = pl.multiple_of(row_ref[plan[f"theirs{j}"]] * width, width)
            copies.append(
                pltpu.make_async_copy(refs[j], out_ref.at[:, pl.ds(start, width)], sems.at[j])
            )
        for copy in copies:
            copy.start()
        for copy in copies:
            copy.wait()

    return call(
        kernel,
        row,
        [(xg, ANY)] + [(a, ANY) for a in arrived],
        [(struct(xg.shape, xg.dtype), ANY)],
        aliases={1: 0},
        scratch=[pltpu.SemaphoreType.DMA((count,))],
        moved=4 * count * tokens * width,
    )[0]


def adam(row, h, got, grad, weights, first, second, kept):
    rows, columns = got["up"].shape
    steps = 4 if rows % 64 == 0 else 1
    size = rows // steps

    def kernel(row_ref, up_ref, dn_ref, grad_ref, w_ref, a_ref, b_ref, *refs):
        a_out, b_out, stepped = refs[-3:]
        gradient = grad_ref[...] + up_ref[...].astype(jnp.float32) + dn_ref[...].astype(jnp.float32)
        moment_a = beta_one * a_ref[...] + (1.0 - beta_one) * gradient
        moment_b = beta_two * b_ref[...] + (1.0 - beta_two) * gradient * gradient
        old = w_ref[...].astype(jnp.float32)
        update = moment_a / corr_one / (jnp.sqrt(moment_b / corr_two) + adam_eps) + weight_decay * old
        a_out[...] = moment_a
        b_out[...] = moment_b
        stepped[...] = (old - learn_rate * update).astype(jnp.bfloat16)

    local = pl.BlockSpec((size, columns), lambda g, row: (g, 0))
    part = pl.BlockSpec((size, columns), lambda g, row: (g + h * steps, 0))
    ins = [(got["up"], local), (got["dn"], local)]
    ins += [(a, part) for a in (grad, weights, first, second)]
    aliases = {}
    if kept is not None:
        aliases = {1 + len(ins): 0, 2 + len(ins): 1}
        ins += [(a, ANY) for a in kept]
    return call(
        kernel,
        row,
        ins,
        [
            (struct(first.shape, jnp.float32), part),
            (struct(second.shape, jnp.float32), part),
            (struct((rows, columns), jnp.bfloat16), local),
        ],
        grid=(steps,),
        aliases=aliases,
        flops=16 * rows * columns,
        moved=28 * rows * columns,
    )


def average(mixing, h, stepped, chosen, kept, height):
    rows, columns = stepped.shape
    steps = 2 if rows % 32 == 0 else 1
    size = rows // steps

    def kernel(mix_ref, stepped_ref, chosen_ref, *refs):
        mix = mix_ref[0].astype(jnp.float32) / mix_denom
        refs[-1][...] = (
            (1.0 - mix) * stepped_ref[...].astype(jnp.float32)
            + mix * chosen_ref[...].astype(jnp.float32)
        ).astype(jnp.bfloat16)

    local = pl.BlockSpec((size, columns), lambda g, row: (g, 0))
    part = pl.BlockSpec((size, columns), lambda g, row: (g + h * steps, 0))
    ins = [(stepped, local), (chosen, local)]
    if kept is not None:
        ins.append((kept, ANY))
    return call(
        kernel,
        mixing,
        ins,
        [(struct((height, columns), jnp.bfloat16), part)],
        grid=(steps,),
        aliases={} if kept is None else {3: 0},
        moved=6 * rows * columns,
    )[0]


def partner_rows(stepped, partner, replica, n_rep):
    if n_rep != 4:
        gathered = lax.all_gather(stepped, "rep", axis=0, tiled=False)
        return lax.dynamic_index_in_dim(gathered, partner[replica], 0, keepdims=False)
    mask = partner[0]
    near = lax.ppermute(stepped, "rep", [(r, r ^ 1) for r in range(4)])
    far = lax.ppermute(
        jnp.where(mask == 3, near, stepped), "rep", [(r, r ^ 2) for r in range(4)]
    )
    return jnp.where(mask == 1, near, far)


def per_device(
    n_rep, n, activations, kv_weight, kv_cotangent, first_moment, second_moment, partner, mix_numerator
):
    act, weights, cot = activations[0], kv_weight[0], kv_cotangent[0]
    first, second = first_moment[0], second_moment[0]
    plan = Plan(n)
    depth = plan.depth
    rows = weights.shape[0]
    size = rows // CHUNKS
    row = lax.dynamic_index_in_dim(
        jnp.asarray(plan.table), lax.axis_index("fsdp"), 0, keepdims=False
    )
    climb = [(i, i + 2) for i in range(n - 2)]
    ways = {"up": climb, "dn": [(b, a) for a, b in climb]}
    swap = functools.partial(lax.ppermute, axis_name="fsdp", perm=[(i, i ^ 1) for i in range(n)])

    def shift(bufs):
        return {way: lax.ppermute(bufs[way], "fsdp", ways[way]) for way in ways}

    got = {}
    for h in range(CHUNKS):
        part = weights[h * size : (h + 1) * size]
        got[1, h] = shift({"up": part, "dn": part})

    cot_oth = swap(cot)
    pieces = []
    for k in range(depth):
        after = [cot_oth] if k == 1 else [pieces[k - 2]] if k > 1 else []
        pieces.append(swap(pack(plan, row, act, rows, k, after)))

    for s in range(2, depth + 1):
        for h in range(CHUNKS):
            bufs = relay(plan, row, s, h, got[s - 1, h], act, pieces[: s - 1], cot, cot_oth)
            got[s, h] = shift(bufs)

    kept = None
    arrived = []
    for j in range(depth):
        if j == 0:
            candidates = [[weights]]
        else:
            candidates = [
                [got[slot, h][way] for h in range(CHUNKS)] for way, slot in plan.sources[j]
            ]
        xg, xg_oth, kv_own, kv_oth = project(
            plan, row, j, candidates, act, pieces, cot, cot_oth, kept
        )
        kept = (xg, kv_own, kv_oth)
        arrived.append(swap(xg_oth))
    kv_out = (kept[1] + swap(kept[2]).astype(jnp.float32)).astype(jnp.bfloat16)
    x_grad = place(plan, row, kept[0], arrived)

    grad = own_gradient(plan, row, act, pieces[depth - 1], cot, cot_oth)
    replica = lax.axis_index("rep")
    mixing = lax.dynamic_slice(mix_numerator, (replica,), (1,))
    moments, averaged = None, None
    for h in range(CHUNKS):
        new_a, new_b, stepped = adam(row, h, got[depth, h], grad, weights, first, second, moments)
        moments = (new_a, new_b)
        chosen = partner_rows(stepped, partner, replica, n_rep)
        averaged = average(mixing, h, stepped, chosen, averaged, rows)
    return (
        kv_out[None],
        x_grad[None],
        averaged[None],
        moments[0][None],
        moments[1][None],
    )


def solution(mesh):
    placed = P("rep", "fsdp", None)
    return jax.shard_map(
        functools.partial(per_device, mesh.shape["rep"], mesh.shape["fsdp"]),
        mesh=mesh,
        in_specs=(placed,) * 5 + (P(), P()),
        out_specs=(placed,) * 5,
        check_vma=False,
    )
```

```python
import functools

import jax
import jax.numpy as jnp
import numpy as np
from jax import lax
from jax.experimental import pallas as pl
from jax.experimental.pallas import tpu as pltpu
from jax.sharding import PartitionSpec as P

beta_one = 0.9
beta_two = 0.999
learn_rate = 0.02
weight_decay = 0.1
adam_eps = 1e-08
corr_one = 1.0 - beta_one**10
corr_two = 1.0 - beta_two**10
mix_denom = 64.0

CHUNKS = 2
MIB = 1 << 20
ANY = pl.BlockSpec(memory_space=pl.ANY)

TN = (((0,), (0,)), ((), ()))
NT = (((1,), (1,)), ((), ()))


def dot(a, b, dims=(((1,), (0,)), ((), ()))):
    return lax.dot_general(a, b, dims, preferred_element_type=jnp.float32)


class Plan:
    def __init__(self, n):
        self.depth = depth = n // 2
        self.columns = {}
        self.rows = [[] for _ in range(n)]
        order = [
            sorted(range(depth), key=lambda q: (-abs(q - z), (q < z) != (2 * z >= depth)))
            for z in range(depth)
        ]
        self.sources = [set() for _ in range(depth)]
        arrivals = []
        for z in range(depth):
            below, above = ("b", "a") if z % 2 == 0 else ("a", "b")
            ups = [(z - t, (below, t)) for t in range(1, z + 1)]
            downs = [(z + t, (above, t)) for t in range(1, depth - z)]
            arrivals.append(downs + ups if 2 * z < depth else ups + downs)
            for j, (_, source) in enumerate(arrivals[z], 1):
                self.sources[j].add(source)
        self.sources = [sorted(s) for s in self.sources]
        for i in range(n):
            z, x = divmod(i, 2)
            put = functools.partial(self._put, i)
            put("own", i)
            for k in range(depth):
                put(f"pack{k}", 2 * order[z][k] + 1 - x)
            for s in range(2, depth + 1):
                up, down = z + 1 + depth - s, z - 1 - depth + s
                for link, q in zip("ab", (up, down) if z % 2 == 0 else (down, up)):
                    add = 0 <= q < depth
                    put(f"add_{link}{s}", int(add))
                    put(f"blk_{link}{s}", 2 * q + x if add else 0)
                    put(f"pos_{link}{s}", order[z].index(q) if add else 0)
            for j in range(depth):
                q, source = (z, None) if j == 0 else arrivals[z][j - 1]
                put(f"mine{j}", 2 * q + x)
                put(f"theirs{j}", 2 * q + 1 - x)
                put(f"piece{j}", order[z].index(q))
                put(f"source{j}", 0 if j == 0 else self.sources[j].index(source))
        self.table = np.asarray(self.rows, np.int32)

    def _put(self, i, name, value):
        column = self.columns.setdefault(name, len(self.columns))
        assert column == len(self.rows[i])
        self.rows[i].append(value)

    def __getitem__(self, name):
        return self.columns[name]


def call(kernel, row, ins, outs, grid=(1,), aliases=None, scratch=(), flops=0, moved=0, vmem=24):
    return pl.pallas_call(
        kernel,
        grid_spec=pltpu.PrefetchScalarGridSpec(
            num_scalar_prefetch=1,
            grid=grid,
            in_specs=[spec for _, spec in ins],
            out_specs=[spec for _, spec in outs],
            scratch_shapes=list(scratch),
        ),
        out_shape=[shape for shape, _ in outs],
        input_output_aliases=aliases or {},
        compiler_params=pltpu.CompilerParams(vmem_limit_bytes=vmem * MIB),
        cost_estimate=pl.CostEstimate(flops=flops, bytes_accessed=moved, transcendentals=0),
    )(row, *[array for array, _ in ins])


def whole(array):
    rank = array.ndim
    return pl.BlockSpec(array.shape, lambda g, row: (0,) * rank)


def block(shape, column, scale=1, offset=0):
    return pl.BlockSpec(shape, lambda g, row: (0, row[column] * scale + offset))


def struct(shape, dtype):
    return jax.ShapeDtypeStruct(shape, dtype)


class View:
    def __init__(self, array, start, count):
        assert start % count == 0
        self.array, self.start, self.count = array, start, count
        self.shape = (array.shape[0], count)

    def operand(self):
        at = self.start // self.count
        return self.array, pl.BlockSpec(self.shape, lambda g, row: (0, at))


def pack(plan, row, width, views, act=None, turns=(), after=()):
    count = len(views) + len(turns)
    ins = [v.operand() for v in views]
    tokens = views[0].shape[0] if views else act.shape[0]
    ins += [(act, block((tokens, width), plan[f"pack{k}"])) for k in turns]
    sizes = [v.count for v in views] + [width] * len(turns)

    def kernel(row_ref, *refs):
        at = 0
        for ref, size in zip(refs[:count], sizes):
            refs[-1][:, at : at + size] = ref[...]
            at += size

    out = struct((tokens, sum(sizes)), jnp.bfloat16)
    return call(
        kernel,
        row,
        ins + [(a, ANY) for a in after],
        [(out, whole(out))],
        moved=4 * tokens * sum(sizes),
    )[0]


def relay(plan, row, s, got, act, pieces, cot_own, cot_oth):
    (tokens, columns), rows = cot_own.shape, got["a"].shape[0]
    count = len(pieces)

    def kernel(row_ref, *refs):
        got_refs, act_refs = refs[0:2], refs[2:4]
        piece_refs = refs[4 : 4 + count]
        own_ref, oth_ref = refs[4 + count : 6 + count]
        out_refs = refs[6 + count : 8 + count]
        held = refs[8 + count]
        for d, link in enumerate("ab"):
            add = row_ref[plan[f"add_{link}{s}"]]
            pos = row_ref[plan[f"pos_{link}{s}"]]

            @pl.when(add == 0)
            def _():
                out_refs[d][...] = got_refs[d][...]

            @pl.when(add == 1)
            def _():
                for j in range(count):

                    @pl.when(pos == j)
                    def _():
                        held[...] = piece_refs[j][...]

                total = dot(act_refs[d][...], own_ref[...], TN)
                total = total + dot(held[...], oth_ref[...], TN)
                out_refs[d][...] = (total + got_refs[d][...].astype(jnp.float32)).astype(jnp.bfloat16)

    ins = [(got[link], whole(got[link])) for link in "ba"]
    ins += [(act, block((tokens, rows), plan[f"blk_{link}{s}"])) for link in "ab"]
    ins += [view.operand() for view in (*pieces, cot_own, cot_oth)]
    out = struct((rows, columns), jnp.bfloat16)
    a, b = call(
        kernel,
        row,
        ins,
        [(out, whole(out)), (out, whole(out))],
        scratch=[pltpu.VMEM((tokens, rows), jnp.bfloat16)],
        flops=8 * tokens * rows * columns,
        moved=8 * rows * columns + 4 * tokens * columns,
    )
    return {"a": a, "b": b}


def own_gradient(plan, row, act, piece, cot, cot_oth):
    tokens, columns = cot.shape
    rows = piece.shape[1]

    def kernel(row_ref, act_ref, piece_ref, own_ref, *refs):
        out_ref = refs[-1]
        at = 0
        for ref, view in zip(refs, cot_oth):
            part = slice(at, at + view.count)
            total = dot(act_ref[...], own_ref[:, part], TN)
            out_ref[:, part] = total + dot(piece_ref[...], ref[...], TN)
            at += view.count

    out = struct((rows, columns), jnp.float32)
    return call(
        kernel,
        row,
        [(act, block((tokens, rows), plan["own"])), piece.operand(), (cot, whole(cot))]
        + [view.operand() for view in cot_oth],
        [(out, whole(out))],
        flops=4 * tokens * rows * columns,
        moved=4 * rows * columns + 4 * tokens * columns,
    )[0]


def project(plan, row, j, candidates, act, cot, cot_oth, xg_before, turn=None, after=()):
    (tokens, columns), rows = cot.shape, candidates[0][0].shape[0]
    parts = len(candidates[0])
    flat = [c for candidate in candidates for c in candidate]
    n_w, n_c, extra = len(flat), len(cot_oth), turn is not None
    widths = [c.shape[1] for c in candidates[0]]
    starts = np.cumsum([0] + widths)

    def kernel(row_ref, *refs):
        w_refs, cot_refs = refs[:n_w], refs[n_w : n_w + n_c]
        own_ref = refs[n_w + n_c]
        xg_own, xg_oth, w_out, sems = refs[-4:]
        for c in range(len(candidates)):

            @pl.when(row_ref[plan[f"source{j}"]] == c)
            def _():
                copies = [
                    pltpu.make_async_copy(
                        w_refs[c * parts + p],
                        w_out.at[:, pl.ds(int(starts[p]), widths[p])],
                        sems.at[p],
                    )
                    for p in range(parts)
                ]
                for copy in copies:
                    copy.start()
                for copy in copies:
                    copy.wait()

        total, at = 0.0, 0
        for ref, view in zip(cot_refs, cot_oth):
            total = total + dot(ref[...], w_out[:, at : at + view.count], NT)
            at += view.count
        xg_oth[:, :rows] = total.astype(jnp.bfloat16)
        if extra:
            xg_oth[:, rows:] = refs[n_w + n_c + 1][...]
        xg_own[...] = dot(own_ref[...], w_out[...], NT).astype(jnp.bfloat16)

    ins = [(w, ANY) for w in flat] + [view.operand() for view in cot_oth] + [(cot, whole(cot))]
    if extra:
        ins.append((act, block((tokens, rows), plan[f"pack{turn}"])))
    aliases = {}
    if xg_before is not None:
        aliases = {1 + len(ins): 0}
        ins.append((xg_before, ANY))
    ins += [(a, ANY) for a in after]
    other = struct((tokens, rows * (1 + extra)), jnp.bfloat16)
    shard = struct((rows, columns), jnp.bfloat16)
    return call(
        kernel,
        row,
        ins,
        [
            (struct(act.shape, jnp.bfloat16), block((tokens, rows), plan[f"mine{j}"])),
            (other, whole(other)),
            (shard, whole(shard)),
        ],
        aliases=aliases,
        scratch=[pltpu.SemaphoreType.DMA((parts,))],
        flops=4 * tokens * rows * columns,
        moved=12 * tokens * columns,
    )


def values(plan, row, turns, shards, act, pieces, kept, last):
    rows, columns = shards[0].shape
    tokens = act.shape[0]
    count, n_p = len(turns), len(pieces)

    def kernel(row_ref, *refs):
        w_refs, act_refs = refs[:count], refs[count : 2 * count]
        piece_refs = refs[2 * count : 2 * count + n_p]
        own_out, oth_out, held = refs[-3:]
        own = oth = 0.0
        if kept is not None:
            own, oth = refs[2 * count + n_p][...], refs[2 * count + n_p + 1][...]
        for t, j in enumerate(turns):
            for p in range(n_p):

                @pl.when(row_ref[plan[f"piece{j}"]] == p)
                def _():
                    held[...] = piece_refs[p][...]

            oth = oth + dot(held[...], w_refs[t][...])
            own = own + dot(act_refs[t][...], w_refs[t][...])
        oth_out[...] = oth.astype(oth_out.dtype)
        own_out[...] = own

    ins = [(w, whole(w)) for w in shards]
    ins += [(act, block((tokens, rows), plan[f"mine{j}"])) for j in turns]
    ins += [p.operand() for p in pieces]
    if kept is not None:
        ins += [(k, whole(k)) for k in kept]
    own = struct((tokens, columns), jnp.float32)
    oth = struct((tokens, columns), jnp.bfloat16 if last else jnp.float32)
    return call(
        kernel,
        row,
        ins,
        [(own, whole(own)), (oth, whole(oth))],
        scratch=[pltpu.VMEM((tokens, rows), jnp.bfloat16)],
        flops=4 * tokens * rows * columns * count,
        moved=8 * tokens * columns,
        vmem=40,
    )


def finish(plan, row, xg, arrived, kv_own, kv_got, after):
    count = len(arrived)
    tokens, width = arrived[0].shape
    table = [plan[f"theirs{j}"] for j in range(count)]

    def kernel(row_ref, *refs):
        out_ref, kv_out = refs[-2:]
        g = pl.program_id(0)
        for j in range(count):

            @pl.when(g == j)
            def _():
                out_ref[...] = refs[j][...]

        kv_out[...] = (refs[count][...] + refs[count + 1][...].astype(jnp.float32)).astype(jnp.bfloat16)

    def place(g, row):
        at = row[table[0]]
        for j in range(1, count):
            at = jnp.where(g == j, row[table[j]], at)
        return (0, at)

    kv_block = pl.BlockSpec((tokens // count, kv_own.shape[1]), lambda g, row: (g, 0))
    ins = [view.operand() for view in arrived]
    ins += [(kv_own, kv_block), (kv_got, kv_block), (xg, ANY)] + [(a, ANY) for a in after]
    return call(
        kernel,
        row,
        ins,
        [
            (struct(xg.shape, xg.dtype), pl.BlockSpec((tokens, width), place)),
            (struct(kv_own.shape, jnp.bfloat16), kv_block),
        ],
        grid=(count,),
        aliases={count + 3: 0},
        moved=4 * count * tokens * width,
    )


def adam(row, h, got, grad, weights, first, second, kept):
    rows, columns = got["a"].shape
    steps = 4 if rows % 64 == 0 else 1
    size = rows // steps

    def kernel(row_ref, up_ref, dn_ref, grad_ref, w_ref, a_ref, b_ref, *refs):
        a_out, b_out, stepped = refs[-3:]
        gradient = grad_ref[...] + up_ref[...].astype(jnp.float32) + dn_ref[...].astype(jnp.float32)
        moment_a = beta_one * a_ref[...] + (1.0 - beta_one) * gradient
        moment_b = beta_two * b_ref[...] + (1.0 - beta_two) * gradient * gradient
        old = w_ref[...].astype(jnp.float32)
        update = moment_a / corr_one / (jnp.sqrt(moment_b / corr_two) + adam_eps) + weight_decay * old
        a_out[...] = moment_a
        b_out[...] = moment_b
        stepped[...] = (old - learn_rate * update).astype(jnp.bfloat16)

    local = pl.BlockSpec((size, columns), lambda g, row: (g, 0))
    part = pl.BlockSpec((size, columns), lambda g, row: (g, h))
    ins = [(got["a"], local), (got["b"], local)]
    ins += [(a, part) for a in (grad, weights, first, second)]
    aliases = {}
    if kept is not None:
        aliases = {1 + len(ins): 0, 2 + len(ins): 1}
        ins += [(a, ANY) for a in kept]
    return call(
        kernel,
        row,
        ins,
        [
            (struct(first.shape, jnp.float32), part),
            (struct(second.shape, jnp.float32), part),
            (struct((rows, columns), jnp.bfloat16), local),
        ],
        grid=(steps,),
        aliases=aliases,
        flops=16 * rows * columns,
        moved=28 * rows * columns,
    )


def average(mixing, h, stepped, chosen, kept, width):
    rows, columns = stepped.shape
    steps = 2 if rows % 32 == 0 else 1
    size = rows // steps

    def kernel(mix_ref, stepped_ref, chosen_ref, *refs):
        mix = mix_ref[0].astype(jnp.float32) / mix_denom
        refs[-1][...] = (
            (1.0 - mix) * stepped_ref[...].astype(jnp.float32)
            + mix * chosen_ref[...].astype(jnp.float32)
        ).astype(jnp.bfloat16)

    local = pl.BlockSpec((size, columns), lambda g, row: (g, 0))
    part = pl.BlockSpec((size, columns), lambda g, row: (g, h))
    ins = [(stepped, local), (chosen, local)]
    if kept is not None:
        ins.append((kept, ANY))
    return call(
        kernel,
        mixing,
        ins,
        [(struct((rows, width), jnp.bfloat16), part)],
        grid=(steps,),
        aliases={} if kept is None else {3: 0},
        moved=6 * rows * columns,
    )[0]


def partner_rows(stepped, partner, replica, n_rep):
    if n_rep != 4:
        gathered = lax.all_gather(stepped, "rep", axis=0, tiled=False)
        return lax.dynamic_index_in_dim(gathered, partner[replica], 0, keepdims=False)
    mask = partner[0]
    near = lax.ppermute(stepped, "rep", [(r, r ^ 1) for r in range(4)])
    far = lax.ppermute(
        jnp.where(mask == 3, near, stepped), "rep", [(r, r ^ 2) for r in range(4)]
    )
    return jnp.where(mask == 1, near, far)


def per_device(
    n_rep, n, activations, kv_weight, kv_cotangent, first_moment, second_moment, partner, mix_numerator
):
    act, weights, cot = activations[0], kv_weight[0], kv_cotangent[0]
    first, second = first_moment[0], second_moment[0]
    plan = Plan(n)
    depth = plan.depth
    rows, columns = weights.shape
    size = columns // CHUNKS
    row = lax.dynamic_index_in_dim(
        jnp.asarray(plan.table), lax.axis_index("fsdp"), 0, keepdims=False
    )
    links = {
        "a": [(i, i + 2 if i // 2 % 2 == 0 else i - 2) for i in range(n)],
        "b": [(i, i - 2 if i // 2 % 2 == 0 else i + 2) for i in range(n)],
    }
    links = {name: [p for p in pairs if 0 <= p[1] < n] for name, pairs in links.items()}
    swap = functools.partial(lax.ppermute, axis_name="fsdp", perm=[(i, i ^ 1) for i in range(n)])

    def exchange(bufs):
        return {name: lax.ppermute(bufs[name], "fsdp", links[name]) for name in links}

    def part(array, h):
        return View(array, h * size, size)

    got = {}
    for h in range(CHUNKS):
        own = weights[:, h * size : (h + 1) * size]
        got[1, h] = exchange({"a": own, "b": own})

    opening = swap(pack(plan, row, rows, [part(cot, 0)], act, [0]))
    cot_oth = [View(opening, 0, size)]
    pieces = [View(opening, size, rows)]
    for h in range(1, CHUNKS):
        cot_oth.append(part(swap(pack(plan, row, rows, [part(cot, h)], after=[opening])), 0))
    latest = cot_oth[-1].array
    for k in range(1, depth - 1, 2):
        turns = list(range(k, min(k + 2, depth - 1)))
        latest = swap(pack(plan, row, rows, [], act, turns, after=[latest]))
        pieces += [View(latest, t * rows, rows) for t in range(len(turns))]
    xg, both, shard = project(
        plan, row, 0, [[weights]], act, cot, cot_oth, None, turn=depth - 1, after=[latest]
    )
    both = swap(both)
    arrived, shards = [View(both, 0, rows)], [shard]
    pieces.append(View(both, rows, rows))

    for s in range(2, depth + 1):
        for h in range(CHUNKS):
            bufs = relay(
                plan, row, s, got[s - 1, h], act, pieces[: s - 1], part(cot, h), cot_oth[h]
            )
            got[s, h] = exchange(bufs)

    for j in range(1, depth):
        candidates = [
            [got[slot, h][link] for h in range(CHUNKS)] for link, slot in plan.sources[j]
        ]
        xg, xg_oth, shard = project(plan, row, j, candidates, act, cot, cot_oth, xg)
        arrived.append(View(swap(xg_oth), 0, rows))
        shards.append(shard)
    early = list(range(depth - 1))
    sums = values(plan, row, early, shards[:-1], act, pieces, None, False)
    kv_own, kv_oth = values(plan, row, [depth - 1], shards[-1:], act, pieces, sums, True)
    kv_got = swap(kv_oth)

    grad = own_gradient(plan, row, act, pieces[depth - 1], cot, cot_oth)
    replica = lax.axis_index("rep")
    mixing = lax.dynamic_slice(mix_numerator, (replica,), (1,))
    moments, averaged = None, None
    for h in range(CHUNKS):
        new_a, new_b, stepped = adam(row, h, got[depth, h], grad, weights, first, second, moments)
        moments = (new_a, new_b)
        chosen = partner_rows(stepped, partner, replica, n_rep)
        if h == CHUNKS - 1:
            x_grad, kv_out = finish(plan, row, xg, arrived, kv_own, kv_got, [averaged])
        averaged = average(mixing, h, stepped, chosen, averaged, columns)
    return (
        kv_out[None],
        x_grad[None],
        averaged[None],
        moments[0][None],
        moments[1][None],
    )


def solution(mesh):
    placed = P("rep", "fsdp", None)
    return jax.shard_map(
        functools.partial(per_device, mesh.shape["rep"], mesh.shape["fsdp"]),
        mesh=mesh,
        in_specs=(placed,) * 5 + (P(), P()),
        out_specs=(placed,) * 5,
        check_vma=False,
    )
```

```python
import functools

import jax
import jax.numpy as jnp
import numpy as np
from jax import lax
from jax.experimental import pallas as pl
from jax.experimental.pallas import tpu as pltpu
from jax.sharding import PartitionSpec as P

beta_one = 0.9
beta_two = 0.999
learn_rate = 0.02
weight_decay = 0.1
adam_eps = 1e-08
corr_one = 1.0 - beta_one**10
corr_two = 1.0 - beta_two**10
mix_denom = 64.0

CHUNKS = 2
MIB = 1 << 20
ANY = pl.BlockSpec(memory_space=pl.ANY)

TN = (((0,), (0,)), ((), ()))
NT = (((1,), (1,)), ((), ()))


def dot(a, b, dims=(((1,), (0,)), ((), ()))):
    return lax.dot_general(a, b, dims, preferred_element_type=jnp.float32)


class Plan:
    def __init__(self, n):
        self.depth = depth = n // 2
        self.columns = {}
        self.rows = [[] for _ in range(n)]
        order = [
            sorted(range(depth), key=lambda q: (-abs(q - z), (q < z) != (2 * z >= depth)))
            for z in range(depth)
        ]
        self.sources = [set() for _ in range(depth)]
        arrivals = []
        for z in range(depth):
            below, above = ("b", "a") if z % 2 == 0 else ("a", "b")
            ups = [(z - t, (below, t)) for t in range(1, z + 1)]
            downs = [(z + t, (above, t)) for t in range(1, depth - z)]
            arrivals.append(downs + ups if 2 * z < depth else ups + downs)
            for j, (_, source) in enumerate(arrivals[z], 1):
                self.sources[j].add(source)
        self.sources = [sorted(s) for s in self.sources]
        for i in range(n):
            z, x = divmod(i, 2)
            put = functools.partial(self._put, i)
            put("own", i)
            for k in range(depth):
                put(f"pack{k}", 2 * order[z][k] + 1 - x)
            for s in range(2, depth + 1):
                up, down = z + 1 + depth - s, z - 1 - depth + s
                for link, q in zip("ab", (up, down) if z % 2 == 0 else (down, up)):
                    add = 0 <= q < depth
                    put(f"add_{link}{s}", int(add))
                    put(f"blk_{link}{s}", 2 * q + x if add else 0)
                    put(f"pos_{link}{s}", order[z].index(q) if add else 0)
            for j in range(depth):
                q, source = (z, None) if j == 0 else arrivals[z][j - 1]
                put(f"mine{j}", 2 * q + x)
                put(f"theirs{j}", 2 * q + 1 - x)
                put(f"piece{j}", order[z].index(q))
                put(f"source{j}", 0 if j == 0 else self.sources[j].index(source))
        self.table = np.asarray(self.rows, np.int32)

    def _put(self, i, name, value):
        column = self.columns.setdefault(name, len(self.columns))
        assert column == len(self.rows[i])
        self.rows[i].append(value)

    def __getitem__(self, name):
        return self.columns[name]


def call(kernel, row, ins, outs, grid=(1,), aliases=None, scratch=(), flops=0, moved=0, vmem=24):
    return pl.pallas_call(
        kernel,
        grid_spec=pltpu.PrefetchScalarGridSpec(
            num_scalar_prefetch=1,
            grid=grid,
            in_specs=[spec for _, spec in ins],
            out_specs=[spec for _, spec in outs],
            scratch_shapes=list(scratch),
        ),
        out_shape=[shape for shape, _ in outs],
        input_output_aliases=aliases or {},
        compiler_params=pltpu.CompilerParams(vmem_limit_bytes=vmem * MIB),
        cost_estimate=pl.CostEstimate(flops=flops, bytes_accessed=moved, transcendentals=0),
    )(row, *[array for array, _ in ins])


def whole(array):
    rank = array.ndim
    return pl.BlockSpec(array.shape, lambda g, row: (0,) * rank)


def block(shape, column, scale=1, offset=0):
    return pl.BlockSpec(shape, lambda g, row: (0, row[column] * scale + offset))


def struct(shape, dtype):
    return jax.ShapeDtypeStruct(shape, dtype)


class View:
    def __init__(self, array, start, count):
        assert start % count == 0
        self.array, self.start, self.count = array, start, count
        self.shape = (array.shape[0], count)

    def operand(self):
        at = self.start // self.count
        return self.array, pl.BlockSpec(self.shape, lambda g, row: (0, at))


def pack(plan, row, width, views, act=None, turns=(), after=()):
    count = len(views) + len(turns)
    ins = [v.operand() for v in views]
    tokens = views[0].shape[0] if views else act.shape[0]
    ins += [(act, block((tokens, width), plan[f"pack{k}"])) for k in turns]
    sizes = [v.count for v in views] + [width] * len(turns)

    def kernel(row_ref, *refs):
        at = 0
        for ref, size in zip(refs[:count], sizes):
            refs[-1][:, at : at + size] = ref[...]
            at += size

    out = struct((tokens, sum(sizes)), jnp.bfloat16)
    return call(
        kernel,
        row,
        ins + [(a, ANY) for a in after],
        [(out, whole(out))],
        moved=4 * tokens * sum(sizes),
    )[0]


def relay(plan, row, s, got, act, pieces, cot_own, cot_oth, after=()):
    (tokens, columns), rows = cot_own.shape, got["a"].shape[0]
    count = len(pieces)

    def kernel(row_ref, *refs):
        got_refs, act_refs = refs[0:2], refs[2:4]
        piece_refs = refs[4 : 4 + count]
        own_ref, oth_ref = refs[4 + count : 6 + count]
        out_refs, held = refs[-3:-1], refs[-1]
        for d, link in enumerate("ab"):
            add = row_ref[plan[f"add_{link}{s}"]]
            pos = row_ref[plan[f"pos_{link}{s}"]]

            @pl.when(add == 0)
            def _():
                out_refs[d][...] = got_refs[d][...]

            @pl.when(add == 1)
            def _():
                for j in range(count):

                    @pl.when(pos == j)
                    def _():
                        held[...] = piece_refs[j][...]

                total = dot(act_refs[d][...], own_ref[...], TN)
                total = total + dot(held[...], oth_ref[...], TN)
                out_refs[d][...] = (total + got_refs[d][...].astype(jnp.float32)).astype(jnp.bfloat16)

    ins = [got[link].operand() for link in "ba"]
    ins += [(act, block((tokens, rows), plan[f"blk_{link}{s}"])) for link in "ab"]
    ins += [view.operand() for view in (*pieces, cot_own, cot_oth)]
    ins += [(a, ANY) for a in after]
    out = struct((rows, columns), jnp.bfloat16)
    a, b = call(
        kernel,
        row,
        ins,
        [(out, whole(out)), (out, whole(out))],
        scratch=[pltpu.VMEM((tokens, rows), jnp.bfloat16)],
        flops=8 * tokens * rows * columns,
        moved=8 * rows * columns + 4 * tokens * columns,
    )
    return {"a": a, "b": b}


def own_gradient(plan, row, act, piece, cot, cot_oth):
    tokens, columns = cot.shape
    rows = piece.shape[1]

    def kernel(row_ref, act_ref, piece_ref, own_ref, *refs):
        out_ref = refs[-1]
        at = 0
        for ref, view in zip(refs, cot_oth):
            part = slice(at, at + view.count)
            total = dot(act_ref[...], own_ref[:, part], TN)
            out_ref[:, part] = total + dot(piece_ref[...], ref[...], TN)
            at += view.count

    out = struct((rows, columns), jnp.float32)
    return call(
        kernel,
        row,
        [(act, block((tokens, rows), plan["own"])), piece.operand(), (cot, whole(cot))]
        + [view.operand() for view in cot_oth],
        [(out, whole(out))],
        flops=4 * tokens * rows * columns,
        moved=4 * rows * columns + 4 * tokens * columns,
    )[0]


def project(plan, row, j, candidates, act, cot, cot_oth, xg_before, turn=None, front=None, after=()):
    (tokens, columns), rows = cot.shape, candidates[0][0].shape[0]
    flat = [c for candidate in candidates for c in candidate]
    starts = np.cumsum([0] + [len(candidate) for candidate in candidates])
    parts = max(len(candidate) for candidate in candidates)
    n_w, n_c = len(flat), len(cot_oth)
    ahead = 0 if front is None else front.count
    width = ahead + rows + (0 if turn is None else rows)

    def kernel(row_ref, *refs):
        w_refs, cot_refs = refs[:n_w], refs[n_w : n_w + n_c]
        own_ref = refs[n_w + n_c]
        xg_own, xg_oth, w_out, sems = refs[-4:]
        for c in range(len(candidates)):

            @pl.when(row_ref[plan[f"source{j}"]] == c)
            def _():
                copies, at = [], 0
                for p in range(starts[c], starts[c + 1]):
                    to = w_out.at[:, pl.ds(at, flat[p].shape[1])]
                    copies.append(pltpu.make_async_copy(w_refs[p], to, sems.at[len(copies)]))
                    at += flat[p].shape[1]
                for copy in copies:
                    copy.start()
                for copy in copies:
                    copy.wait()

        total, at = 0.0, 0
        for ref, view in zip(cot_refs, cot_oth):
            total = total + dot(ref[...], w_out[:, at : at + view.count], NT)
            at += view.count
        xg_oth[:, ahead : ahead + rows] = total.astype(jnp.bfloat16)
        rest = list(refs[n_w + n_c + 1 :])
        if front is not None:
            xg_oth[:, :ahead] = rest.pop(0)[...]
        if turn is not None:
            xg_oth[:, ahead + rows :] = rest.pop(0)[...]
        xg_own[...] = dot(own_ref[...], w_out[...], NT).astype(jnp.bfloat16)

    ins = [(w, ANY) for w in flat] + [view.operand() for view in cot_oth] + [(cot, whole(cot))]
    if front is not None:
        ins.append(front.operand())
    if turn is not None:
        ins.append((act, block((tokens, rows), plan[f"pack{turn}"])))
    aliases = {}
    if xg_before is not None:
        aliases = {1 + len(ins): 0}
        ins.append((xg_before, ANY))
    ins += [(a, ANY) for a in after]
    other = struct((tokens, width), jnp.bfloat16)
    shard = struct((rows, columns), jnp.bfloat16)
    return call(
        kernel,
        row,
        ins,
        [
            (struct(act.shape, jnp.bfloat16), block((tokens, rows), plan[f"mine{j}"])),
            (other, whole(other)),
            (shard, whole(shard)),
        ],
        aliases=aliases,
        scratch=[pltpu.SemaphoreType.DMA((parts,))],
        flops=4 * tokens * rows * columns,
        moved=12 * tokens * columns,
    )


def values(plan, row, turns, shards, act, pieces, kept, last):
    rows, columns = shards[0].shape
    tokens = act.shape[0]
    count, n_p = len(turns), len(pieces)

    def kernel(row_ref, *refs):
        w_refs, act_refs = refs[:count], refs[count : 2 * count]
        piece_refs = refs[2 * count : 2 * count + n_p]
        own_out, oth_out, held = refs[-3:]
        own = oth = 0.0
        if kept is not None:
            own, oth = refs[2 * count + n_p][...], refs[2 * count + n_p + 1][...]
        for t, j in enumerate(turns):
            for p in range(n_p):

                @pl.when(row_ref[plan[f"piece{j}"]] == p)
                def _():
                    held[...] = piece_refs[p][...]

            oth = oth + dot(held[...], w_refs[t][...])
            own = own + dot(act_refs[t][...], w_refs[t][...])
        oth_out[...] = oth.astype(oth_out.dtype)
        own_out[...] = own

    ins = [(w, whole(w)) for w in shards]
    ins += [(act, block((tokens, rows), plan[f"mine{j}"])) for j in turns]
    ins += [p.operand() for p in pieces]
    if kept is not None:
        ins += [(k, whole(k)) for k in kept]
    own = struct((tokens, columns), jnp.float32)
    oth = struct((tokens, columns), jnp.bfloat16 if last else jnp.float32)
    return call(
        kernel,
        row,
        ins,
        [(own, whole(own)), (oth, whole(oth))],
        scratch=[pltpu.VMEM((tokens, rows), jnp.bfloat16)],
        flops=4 * tokens * rows * columns * count,
        moved=8 * tokens * columns,
        vmem=40,
    )


def finish(plan, row, xg, arrived, kv_own, kv_got, after):
    count = len(arrived)
    tokens, width = arrived[0].shape
    table = [plan[f"theirs{j}"] for j in range(count)]

    def kernel(row_ref, *refs):
        out_ref, kv_out = refs[-2:]
        g = pl.program_id(0)
        for j in range(count):

            @pl.when(g == j)
            def _():
                out_ref[...] = refs[j][...]

        kv_out[...] = (refs[count][...] + refs[count + 1][...].astype(jnp.float32)).astype(jnp.bfloat16)

    def place(g, row):
        at = row[table[0]]
        for j in range(1, count):
            at = jnp.where(g == j, row[table[j]], at)
        return (0, at)

    kv_block = pl.BlockSpec((tokens // count, kv_own.shape[1]), lambda g, row: (g, 0))
    ins = [view.operand() for view in arrived]
    ins += [(kv_own, kv_block), (kv_got, kv_block), (xg, ANY)] + [(a, ANY) for a in after]
    return call(
        kernel,
        row,
        ins,
        [
            (struct(xg.shape, xg.dtype), pl.BlockSpec((tokens, width), place)),
            (struct(kv_own.shape, jnp.bfloat16), kv_block),
        ],
        grid=(count,),
        aliases={count + 3: 0},
        moved=4 * count * tokens * width,
    )


def adam(row, h, got, grad, weights, first, second, kept, after=()):
    rows, columns = got["a"].shape
    assert got["a"].start == 0
    steps = 4 if rows % 64 == 0 else 1
    size = rows // steps

    def kernel(row_ref, up_ref, dn_ref, grad_ref, w_ref, a_ref, b_ref, *refs):
        a_out, b_out, stepped = refs[-3:]
        gradient = grad_ref[...] + up_ref[...].astype(jnp.float32) + dn_ref[...].astype(jnp.float32)
        moment_a = beta_one * a_ref[...] + (1.0 - beta_one) * gradient
        moment_b = beta_two * b_ref[...] + (1.0 - beta_two) * gradient * gradient
        old = w_ref[...].astype(jnp.float32)
        update = moment_a / corr_one / (jnp.sqrt(moment_b / corr_two) + adam_eps) + weight_decay * old
        a_out[...] = moment_a
        b_out[...] = moment_b
        stepped[...] = (old - learn_rate * update).astype(jnp.bfloat16)

    local = pl.BlockSpec((size, columns), lambda g, row: (g, 0))
    part = pl.BlockSpec((size, columns), lambda g, row: (g, h))
    ins = [(got["a"].array, local), (got["b"].array, local)]
    ins += [(a, part) for a in (grad, weights, first, second)]
    aliases = {}
    if kept is not None:
        aliases = {1 + len(ins): 0, 2 + len(ins): 1}
        ins += [(a, ANY) for a in kept]
    ins += [(a, ANY) for a in after]
    return call(
        kernel,
        row,
        ins,
        [
            (struct(first.shape, jnp.float32), part),
            (struct(second.shape, jnp.float32), part),
            (struct((rows, columns), jnp.bfloat16), local),
        ],
        grid=(steps,),
        aliases=aliases,
        flops=16 * rows * columns,
        moved=28 * rows * columns,
    )


def average(scalars, h, stepped, others, kept, width, after):
    rows, columns = stepped.shape
    steps = 2 if rows % 32 == 0 else 1
    size = rows // steps
    count = len(others)

    def kernel(scalar_ref, stepped_ref, *refs):
        mix = scalar_ref[0].astype(jnp.float32) / mix_denom
        for j in range(count):

            @pl.when(scalar_ref[1] == j)
            def _():
                refs[-1][...] = (
                    (1.0 - mix) * stepped_ref[...].astype(jnp.float32)
                    + mix * refs[j][...].astype(jnp.float32)
                ).astype(jnp.bfloat16)

    local = pl.BlockSpec((size, columns), lambda g, row: (g, 0))
    part = pl.BlockSpec((size, columns), lambda g, row: (g, h))
    ins = [(a, local) for a in (stepped, *others)]
    if kept is not None:
        ins.append((kept, ANY))
    ins += [(a, ANY) for a in after]
    return call(
        kernel,
        scalars,
        ins,
        [(struct((rows, width), jnp.bfloat16), part)],
        grid=(steps,),
        aliases={} if kept is None else {count + 2: 0},
        moved=6 * rows * columns,
    )[0]


def partner_rows(stepped, partner, replica, n_rep):
    if n_rep != 4:
        gathered = lax.all_gather(stepped, "rep", axis=0, tiled=False)
        return [lax.dynamic_index_in_dim(gathered, partner[replica], 0, keepdims=False)]
    far = lax.ppermute(stepped, "rep", [(r, r ^ 2) for r in range(4)])
    core = [(r, r ^ 1) for r in range(4)]
    return [lax.ppermute(stepped, "rep", core), far, lax.ppermute(far, "rep", core)]


def per_device(
    n_rep, n, activations, kv_weight, kv_cotangent, first_moment, second_moment, partner, mix_numerator
):
    act, weights, cot = activations[0], kv_weight[0], kv_cotangent[0]
    first, second = first_moment[0], second_moment[0]
    plan = Plan(n)
    depth = plan.depth
    rows, columns = weights.shape
    size = columns // CHUNKS
    row = lax.dynamic_index_in_dim(
        jnp.asarray(plan.table), lax.axis_index("fsdp"), 0, keepdims=False
    )
    links = {
        "a": [(i, i + 2 if i // 2 % 2 == 0 else i - 2) for i in range(n)],
        "b": [(i, i - 2 if i // 2 % 2 == 0 else i + 2) for i in range(n)],
    }
    links = {name: [p for p in pairs if 0 <= p[1] < n] for name, pairs in links.items()}
    swap = functools.partial(lax.ppermute, axis_name="fsdp", perm=[(i, i ^ 1) for i in range(n)])

    def exchange(bufs):
        return {name: lax.ppermute(bufs[name], "fsdp", links[name]) for name in links}

    def part(array, h):
        return View(array, h * size, size)

    opening = exchange({"a": weights, "b": weights})
    got = {(1, h): {link: part(opening[link], h) for link in links} for h in range(CHUNKS)}

    def arrivals(link, slot):
        if slot == 1:
            return [opening[link]]
        return [got[slot, h][link].array for h in range(CHUNKS)]

    def send(views, *turns, after=()):
        return swap(pack(plan, row, rows, views, act, turns, after))

    parcel = send([part(cot, 0)], 0)
    cot_oth = [View(parcel, 0, size)]
    pieces = [View(parcel, size, rows)]
    for h in range(1, CHUNKS):
        cot_oth.append(part(send([part(cot, h)]), 0))
    parcel = send([], *range(1, depth - 1), after=[parcel])
    pieces += [View(parcel, k * rows, rows) for k in range(depth - 2)]

    arrived, shards = [], []
    xg, held = None, None

    def shard_step(j, xg, held):
        candidates = [[weights]]
        if j > 0:
            candidates = [arrivals(*source) for source in plan.sources[j]]
        turn = depth - 1 if j == depth - 3 else None
        xg, parcel, shard = project(plan, row, j, candidates, act, cot, cot_oth, xg, turn, held)
        shards.append(shard)
        if turn is None and j < depth - 1:
            return xg, View(parcel, 0, parcel.shape[1])
        parcel = swap(parcel)
        arrived.extend(View(parcel, t * rows, rows) for t in range(j + 1 - len(arrived)))
        if turn is not None:
            pieces.append(View(parcel, parcel.shape[1] - rows, rows))
        return xg, None

    xg, held = shard_step(0, xg, held)
    for s in range(2, depth + 1):
        if s > 2:
            xg, held = shard_step(s - 2, xg, held)
        if s == depth:
            grad = own_gradient(plan, row, act, pieces[depth - 1], cot, cot_oth)
        for h in range(CHUNKS):
            after = [bufs["a"]] if h > 0 else []
            bufs = relay(
                plan, row, s, got[s - 1, h], act, pieces[: s - 1], part(cot, h), cot_oth[h], after
            )
            got[s, h] = {link: part(array, 0) for link, array in exchange(bufs).items()}
    xg, held = shard_step(depth - 1, xg, held)
    early = list(range(depth - 1))
    sums = values(plan, row, early, shards[:-1], act, pieces, None, False)
    kv_own, kv_oth = values(plan, row, [depth - 1], shards[-1:], act, pieces, sums, True)
    kv_got = swap(kv_oth)

    replica = lax.axis_index("rep")
    choice = (partner[0] if n_rep == 4 else jnp.int32(1)) - 1
    scalars = jnp.stack([mix_numerator[replica], choice])
    moments, averaged = None, None
    for h in range(CHUNKS):
        after = [arrived[-1].array, kv_oth] if h == CHUNKS - 1 else []
        *moments, stepped = adam(
            row, h, got[depth, h], grad, weights, first, second, moments, after
        )
        others = partner_rows(stepped, partner, replica, n_rep)
        if h == CHUNKS - 1:
            x_grad, kv_out = finish(plan, row, xg, arrived, kv_own, kv_got, [averaged])
        averaged = average(
            scalars, h, stepped, others, averaged, columns, []
        )
    return (
        kv_out[None],
        x_grad[None],
        averaged[None],
        moments[0][None],
        moments[1][None],
    )


def solution(mesh):
    placed = P("rep", "fsdp", None)
    return jax.shard_map(
        functools.partial(per_device, mesh.shape["rep"], mesh.shape["fsdp"]),
        mesh=mesh,
        in_specs=(placed,) * 5 + (P(), P()),
        out_specs=(placed,) * 5,
        check_vma=False,
    )
```

```python
import functools

import jax
import jax.numpy as jnp
import numpy as np
from jax import lax
from jax.experimental import pallas as pl
from jax.experimental.pallas import tpu as pltpu
from jax.sharding import PartitionSpec as P

beta_one = 0.9
beta_two = 0.999
learn_rate = 0.02
weight_decay = 0.1
adam_eps = 1e-08
corr_one = 1.0 - beta_one**10
corr_two = 1.0 - beta_two**10
mix_denom = 64.0

CHUNKS = 2
MIB = 1 << 20
ANY = pl.BlockSpec(memory_space=pl.ANY)

TN = (((0,), (0,)), ((), ()))
NT = (((1,), (1,)), ((), ()))


def dot(a, b, dims=(((1,), (0,)), ((), ()))):
    return lax.dot_general(a, b, dims, preferred_element_type=jnp.float32)


class Plan:
    def __init__(self, n_rep, n):
        self.depth = depth = n // 2
        self.columns = {}
        self.rows = [[] for _ in range(n_rep * n)]
        order = [
            sorted(range(depth), key=lambda q: (-abs(q - z), (q < z) != (2 * z >= depth)))
            for z in range(depth)
        ]
        self.sources = [set() for _ in range(depth)]
        arrivals = []
        for z in range(depth):
            below, above = ("b", "a") if z % 2 == 0 else ("a", "b")
            ups = [(z - t, (below, t)) for t in range(1, z + 1)]
            downs = [(z + t, (above, t)) for t in range(1, depth - z)]
            arrivals.append(downs + ups if 2 * z < depth else ups + downs)
            for j, (_, source) in enumerate(arrivals[z], 1):
                self.sources[j].add(source)
        self.sources = [sorted(s) for s in self.sources]
        for device in range(n_rep * n):
            replica, i = divmod(device, n)
            z, x = divmod(i, 2)
            put = functools.partial(self._put, device)
            put("replica", replica)
            put("own", i)
            for k in range(depth):
                put(f"pack{k}", 2 * order[z][k] + 1 - x)
            for s in range(2, depth + 1):
                up, down = z + 1 + depth - s, z - 1 - depth + s
                for link, q in zip("ab", (up, down) if z % 2 == 0 else (down, up)):
                    add = 0 <= q < depth
                    put(f"add_{link}{s}", int(add))
                    put(f"blk_{link}{s}", 2 * q + x if add else 0)
                    put(f"pos_{link}{s}", order[z].index(q) if add else 0)
            for j in range(depth):
                q, source = (z, None) if j == 0 else arrivals[z][j - 1]
                put(f"mine{j}", 2 * q + x)
                put(f"theirs{j}", 2 * q + 1 - x)
                put(f"piece{j}", order[z].index(q))
                put(f"source{j}", 0 if j == 0 else self.sources[j].index(source))
        self.table = np.asarray(self.rows, np.int32)

    def _put(self, i, name, value):
        column = self.columns.setdefault(name, len(self.columns))
        assert column == len(self.rows[i])
        self.rows[i].append(value)

    def __getitem__(self, name):
        return self.columns[name]


def call(kernel, row, ins, outs, grid=(1,), aliases=None, scratch=(), flops=0, moved=0, vmem=16):
    scalars = row if isinstance(row, tuple) else (row,)
    return pl.pallas_call(
        kernel,
        grid_spec=pltpu.PrefetchScalarGridSpec(
            num_scalar_prefetch=len(scalars),
            grid=grid,
            in_specs=[spec for _, spec in ins],
            out_specs=[spec for _, spec in outs],
            scratch_shapes=list(scratch),
        ),
        out_shape=[shape for shape, _ in outs],
        input_output_aliases=aliases or {},
        compiler_params=pltpu.CompilerParams(vmem_limit_bytes=vmem * MIB),
        cost_estimate=pl.CostEstimate(flops=flops, bytes_accessed=moved, transcendentals=0),
    )(*scalars, *[array for array, _ in ins])


def whole(array):
    rank = array.ndim
    return pl.BlockSpec(array.shape, lambda g, row: (0,) * rank)


def block(shape, column, scale=1, offset=0):
    return pl.BlockSpec(shape, lambda g, row: (0, row[column] * scale + offset))


def struct(shape, dtype):
    return jax.ShapeDtypeStruct(shape, dtype)


class View:
    def __init__(self, array, start, count):
        assert start % count == 0
        self.array, self.start, self.count = array, start, count
        self.shape = (array.shape[0], count)

    def operand(self):
        at = self.start // self.count
        return self.array, pl.BlockSpec(self.shape, lambda g, row: (0, at))


def pack(plan, row, width, views, act=None, turns=(), after=()):
    count = len(views) + len(turns)
    ins = [v.operand() for v in views]
    tokens = views[0].shape[0] if views else act.shape[0]
    ins += [(act, block((tokens, width), plan[f"pack{k}"])) for k in turns]
    sizes = [v.count for v in views] + [width] * len(turns)

    def kernel(row_ref, *refs):
        at = 0
        for ref, size in zip(refs[:count], sizes):
            refs[-1][:, at : at + size] = ref[...]
            at += size

    out = struct((tokens, sum(sizes)), jnp.bfloat16)
    return call(
        kernel,
        row,
        ins + [(a, ANY) for a in after],
        [(out, whole(out))],
        moved=4 * tokens * sum(sizes),
    )[0]


def relay(plan, row, s, got, act, pieces, cot_own, cot_oth, after=()):
    (tokens, columns), rows = cot_own.shape, got["a"].shape[0]
    count = len(pieces)

    def kernel(row_ref, *refs):
        got_refs, act_refs = refs[0:2], refs[2:4]
        piece_refs = refs[4 : 4 + count]
        own_ref, oth_ref = refs[4 + count : 6 + count]
        out_refs, held = refs[-3:-1], refs[-1]
        for d, link in enumerate("ab"):
            add = row_ref[plan[f"add_{link}{s}"]]
            pos = row_ref[plan[f"pos_{link}{s}"]]

            @pl.when(add == 0)
            def _():
                out_refs[d][...] = got_refs[d][...]

            @pl.when(add == 1)
            def _():
                for j in range(count):

                    @pl.when(pos == j)
                    def _():
                        held[...] = piece_refs[j][...]

                total = dot(act_refs[d][...], own_ref[...], TN)
                total = total + dot(held[...], oth_ref[...], TN)
                out_refs[d][...] = (total + got_refs[d][...].astype(jnp.float32)).astype(jnp.bfloat16)

    ins = [got[link].operand() for link in "ba"]
    ins += [(act, block((tokens, rows), plan[f"blk_{link}{s}"])) for link in "ab"]
    ins += [view.operand() for view in (*pieces, cot_own, cot_oth)]
    ins += [(a, ANY) for a in after]
    out = struct((rows, columns), jnp.bfloat16)
    a, b = call(
        kernel,
        row,
        ins,
        [(out, whole(out)), (out, whole(out))],
        scratch=[pltpu.VMEM((tokens, rows), jnp.bfloat16)],
        flops=8 * tokens * rows * columns,
        moved=8 * rows * columns + 4 * tokens * columns,
    )
    return {"a": a, "b": b}


def own_gradient(plan, row, act, piece, cot, cot_oth):
    tokens, columns = cot.shape
    rows = piece.shape[1]

    def kernel(row_ref, act_ref, piece_ref, own_ref, *refs):
        out_ref = refs[-1]
        at = 0
        for ref, view in zip(refs, cot_oth):
            part = slice(at, at + view.count)
            total = dot(act_ref[...], own_ref[:, part], TN)
            out_ref[:, part] = total + dot(piece_ref[...], ref[...], TN)
            at += view.count

    out = struct((rows, columns), jnp.float32)
    return call(
        kernel,
        row,
        [(act, block((tokens, rows), plan["own"])), piece.operand(), (cot, whole(cot))]
        + [view.operand() for view in cot_oth],
        [(out, whole(out))],
        flops=4 * tokens * rows * columns,
        moved=4 * rows * columns + 4 * tokens * columns,
    )[0]


def project(plan, row, j, candidates, act, cot, cot_oth, xg_before, turn=None, front=None, after=()):
    (tokens, columns), rows = cot.shape, candidates[0][0].shape[0]
    flat = [c for candidate in candidates for c in candidate]
    starts = np.cumsum([0] + [len(candidate) for candidate in candidates])
    parts = max(len(candidate) for candidate in candidates)
    n_w, n_c = len(flat), len(cot_oth)
    ahead = 0 if front is None else front.count
    width = ahead + rows + (0 if turn is None else rows)

    def kernel(row_ref, *refs):
        w_refs, cot_refs = refs[:n_w], refs[n_w : n_w + n_c]
        own_ref = refs[n_w + n_c]
        xg_own, xg_oth, w_out, sems = refs[-4:]
        for c in range(len(candidates)):

            @pl.when(row_ref[plan[f"source{j}"]] == c)
            def _():
                copies, at = [], 0
                for p in range(starts[c], starts[c + 1]):
                    to = w_out.at[:, pl.ds(at, flat[p].shape[1])]
                    copies.append(pltpu.make_async_copy(w_refs[p], to, sems.at[len(copies)]))
                    at += flat[p].shape[1]
                for copy in copies:
                    copy.start()
                for copy in copies:
                    copy.wait()

        total, at = 0.0, 0
        for ref, view in zip(cot_refs, cot_oth):
            total = total + dot(ref[...], w_out[:, at : at + view.count], NT)
            at += view.count
        xg_oth[:, ahead : ahead + rows] = total.astype(jnp.bfloat16)
        rest = list(refs[n_w + n_c + 1 :])
        if front is not None:
            xg_oth[:, :ahead] = rest.pop(0)[...]
        if turn is not None:
            xg_oth[:, ahead + rows :] = rest.pop(0)[...]
        xg_own[...] = dot(own_ref[...], w_out[...], NT).astype(jnp.bfloat16)

    ins = [(w, ANY) for w in flat] + [view.operand() for view in cot_oth] + [(cot, whole(cot))]
    if front is not None:
        ins.append(front.operand())
    if turn is not None:
        ins.append((act, block((tokens, rows), plan[f"pack{turn}"])))
    aliases = {}
    if xg_before is not None:
        aliases = {1 + len(ins): 0}
        ins.append((xg_before, ANY))
    ins += [(a, ANY) for a in after]
    other = struct((tokens, width), jnp.bfloat16)
    shard = struct((rows, columns), jnp.bfloat16)
    return call(
        kernel,
        row,
        ins,
        [
            (struct(act.shape, jnp.bfloat16), block((tokens, rows), plan[f"mine{j}"])),
            (other, whole(other)),
            (shard, whole(shard)),
        ],
        aliases=aliases,
        scratch=[pltpu.SemaphoreType.DMA((parts,))],
        flops=4 * tokens * rows * columns,
        moved=12 * tokens * columns,
        vmem=20,
    )


def values(plan, row, turns, shards, act, pieces, kept, behind=None):
    rows, columns = shards[0].shape
    tokens = act.shape[0]
    count, n_p = len(turns), len(pieces)
    extra = 0 if behind is None else behind.count

    def kernel(row_ref, *refs):
        w_refs, act_refs = refs[:count], refs[count : 2 * count]
        piece_refs = refs[2 * count : 2 * count + n_p]
        rest = list(refs[2 * count + n_p : -3])
        own_out, oth_out, held = refs[-3:]
        own = oth = 0.0
        if kept is not None:
            own, oth = rest.pop(0)[...], rest.pop(0)[...]
        for t, j in enumerate(turns):
            for p in range(n_p):

                @pl.when(row_ref[plan[f"piece{j}"]] == p)
                def _():
                    held[...] = piece_refs[p][...]

            oth = oth + dot(held[...], w_refs[t][...])
            own = own + dot(act_refs[t][...], w_refs[t][...])
        oth_out[:, :columns] = oth.astype(oth_out.dtype)
        if behind is not None:
            oth_out[:, columns:] = rest.pop(0)[...]
        own_out[...] = own

    ins = [(w, whole(w)) for w in shards]
    ins += [(act, block((tokens, rows), plan[f"mine{j}"])) for j in turns]
    ins += [p.operand() for p in pieces]
    if kept is not None:
        ins += [(k, whole(k)) for k in kept]
    if behind is not None:
        ins.append(behind.operand())
    own = struct((tokens, columns), jnp.float32)
    oth = struct((tokens, columns + extra), jnp.float32 if behind is None else jnp.bfloat16)
    return call(
        kernel,
        row,
        ins,
        [(own, whole(own)), (oth, whole(oth))],
        scratch=[pltpu.VMEM((tokens, rows), jnp.bfloat16)],
        flops=4 * tokens * rows * columns * count,
        moved=8 * tokens * columns,
        vmem=28,
    )


def place(plan, row, xg, arrived, first, sums=None):
    count = len(arrived)
    tokens, width = arrived[0].shape
    table = [plan[f"theirs{first + j}"] for j in range(count)]

    def kernel(row_ref, *refs):
        g = pl.program_id(0)
        out_ref = refs[-1] if sums is None else refs[-2]
        for j in range(count):

            @pl.when(g == j)
            def _():
                out_ref[...] = refs[j][...]

        if sums is not None:
            total = refs[count][...] + refs[count + 1][...].astype(jnp.float32)
            refs[-1][...] = total.astype(jnp.bfloat16)

    def column(g, row):
        at = row[table[0]]
        for j in range(1, count):
            at = jnp.where(g == j, row[table[j]], at)
        return (0, at)

    ins = [view.operand() for view in arrived]
    outs = [(struct(xg.shape, xg.dtype), pl.BlockSpec((tokens, width), column))]
    if sums is not None:
        own, other = sums
        kv_block = pl.BlockSpec((tokens // count, own.shape[1]), lambda g, row: (g, 0))
        assert other.start == 0
        ins += [(own, kv_block), (other.array, kv_block)]
        outs.append((struct(own.shape, jnp.bfloat16), kv_block))
    aliases = {1 + len(ins): 0}
    return call(
        kernel,
        row,
        ins + [(xg, ANY)],
        outs,
        grid=(count,),
        aliases=aliases,
        moved=4 * count * tokens * width,
    )


def adam(row, h, got, grad, weights, first, second, kept, after=()):
    rows, columns = got["a"].shape
    assert got["a"].start == 0
    steps = 4 if rows % 64 == 0 else 1
    size = rows // steps

    def kernel(row_ref, up_ref, dn_ref, grad_ref, w_ref, a_ref, b_ref, *refs):
        a_out, b_out, stepped = refs[-3:]
        gradient = grad_ref[...] + up_ref[...].astype(jnp.float32) + dn_ref[...].astype(jnp.float32)
        moment_a = beta_one * a_ref[...] + (1.0 - beta_one) * gradient
        moment_b = beta_two * b_ref[...] + (1.0 - beta_two) * gradient * gradient
        old = w_ref[...].astype(jnp.float32)
        update = moment_a / corr_one / (jnp.sqrt(moment_b / corr_two) + adam_eps) + weight_decay * old
        a_out[...] = moment_a
        b_out[...] = moment_b
        stepped[...] = (old - learn_rate * update).astype(jnp.bfloat16)

    local = pl.BlockSpec((size, columns), lambda g, row: (g, 0))
    part = pl.BlockSpec((size, columns), lambda g, row: (g, h))
    ins = [(got["a"].array, local), (got["b"].array, local)]
    ins += [(a, part) for a in (grad, weights, first, second)]
    aliases = {}
    if kept is not None:
        aliases = {1 + len(ins): 0, 2 + len(ins): 1}
        ins += [(a, ANY) for a in kept]
    ins += [(a, ANY) for a in after]
    return call(
        kernel,
        row,
        ins,
        [
            (struct(first.shape, jnp.float32), part),
            (struct(second.shape, jnp.float32), part),
            (struct((rows, columns), jnp.bfloat16), local),
        ],
        grid=(steps,),
        aliases=aliases,
        flops=16 * rows * columns,
        moved=28 * rows * columns,
    )


def average(plan, scalars, h, stepped, others, kept, width, after=()):
    rows, columns = stepped.shape
    steps = 2 if rows % 32 == 0 else 1
    size = rows // steps
    count = len(others)

    def kernel(row_ref, numerator_ref, partner_ref, stepped_ref, *refs):
        mix = numerator_ref[row_ref[plan["replica"]]].astype(jnp.float32) / mix_denom
        for j in range(count):

            @pl.when((partner_ref[0] == j + 1) | (count == 1))
            def _():
                refs[-1][...] = (
                    (1.0 - mix) * stepped_ref[...].astype(jnp.float32)
                    + mix * refs[j][...].astype(jnp.float32)
                ).astype(jnp.bfloat16)

    local = pl.BlockSpec((size, columns), lambda g, *scalars: (g, 0))
    part = pl.BlockSpec((size, columns), lambda g, *scalars: (g, h))
    ins = [(a, local) for a in (stepped, *others)]
    if kept is not None:
        ins.append((kept, ANY))
    ins += [(a, ANY) for a in after]
    return call(
        kernel,
        scalars,
        ins,
        [(struct((rows, width), jnp.bfloat16), part)],
        grid=(steps,),
        aliases={} if kept is None else {count + 4: 0},
        moved=6 * rows * columns,
    )[0]


def partner_rows(stepped, partner, replica, n_rep):
    if n_rep != 4:
        gathered = lax.all_gather(stepped, "rep", axis=0, tiled=False)
        return [lax.dynamic_index_in_dim(gathered, partner[replica], 0, keepdims=False)]
    far = lax.ppermute(stepped, "rep", [(r, r ^ 2) for r in range(4)])
    core = [(r, r ^ 1) for r in range(4)]
    return [lax.ppermute(stepped, "rep", core), far, lax.ppermute(far, "rep", core)]


def per_device(
    n_rep, n, activations, kv_weight, kv_cotangent, first_moment, second_moment, partner, mix_numerator
):
    act, weights, cot = activations[0], kv_weight[0], kv_cotangent[0]
    first, second = first_moment[0], second_moment[0]
    plan = Plan(n_rep, n)
    depth = plan.depth
    rows, columns = weights.shape
    size = columns // CHUNKS
    row = lax.dynamic_index_in_dim(
        jnp.asarray(plan.table), lax.axis_index(("rep", "fsdp")), 0, keepdims=False
    )
    links = {
        "a": [(i, i + 2 if i // 2 % 2 == 0 else i - 2) for i in range(n)],
        "b": [(i, i - 2 if i // 2 % 2 == 0 else i + 2) for i in range(n)],
    }
    links = {name: [p for p in pairs if 0 <= p[1] < n] for name, pairs in links.items()}
    swap = functools.partial(lax.ppermute, axis_name="fsdp", perm=[(i, i ^ 1) for i in range(n)])

    def exchange(bufs):
        return {name: lax.ppermute(bufs[name], "fsdp", links[name]) for name in links}

    def part(array, h):
        return View(array, h * size, size)

    opening = exchange({"a": weights, "b": weights})
    got = {(1, h): {link: part(opening[link], h) for link in links} for h in range(CHUNKS)}

    def arrivals(link, slot):
        if slot == 1:
            return [opening[link]]
        return [got[slot, h][link].array for h in range(CHUNKS)]

    def send(*turns, after=()):
        return swap(pack(plan, row, rows, [], act, turns, after))

    parcel = swap(cot)
    cot_oth = [part(parcel, h) for h in range(CHUNKS)]
    pieces = [View(send(0), 0, rows)]
    parcel = send(*range(1, depth - 1), after=[parcel])
    pieces += [View(parcel, k * rows, rows) for k in range(depth - 2)]

    arrived, shards, sent = [], [], []
    xg, held = None, None

    def shard_step(j, xg, held):
        candidates = [[weights]]
        if j > 0:
            candidates = [arrivals(*source) for source in plan.sources[j]]
        turn = depth - 1 if j == depth - 3 else None
        after = [sent[-1]] if j == depth - 2 else []
        xg, parcel, shard = project(
            plan, row, j, candidates, act, cot, cot_oth, xg, turn, held, after
        )
        shards.append(shard)
        if j < depth - 3 or j == depth - 1:
            return xg, View(parcel, 0, parcel.shape[1])
        sent.append(swap(parcel))
        arrived.extend(View(sent[-1], t * rows, rows) for t in range(j + 1 - len(arrived)))
        if turn is not None:
            pieces.append(View(sent[-1], parcel.shape[1] - rows, rows))
        return xg, None

    xg, held = shard_step(0, xg, held)
    for s in range(2, depth + 1):
        if s > 2:
            xg, held = shard_step(s - 2, xg, held)
        if s == depth:
            grad = own_gradient(plan, row, act, pieces[depth - 1], cot, cot_oth)
            sums = values(plan, row, list(range(depth - 1)), shards, act, pieces, None)
        for h in range(CHUNKS):
            after = [bufs["a"]] if h > 0 else []
            if s == depth and h == CHUNKS - 1:
                after.append(sums[0])
            bufs = relay(
                plan, row, s, got[s - 1, h], act, pieces[: s - 1], part(cot, h), cot_oth[h], after
            )
            got[s, h] = {link: part(array, 0) for link, array in exchange(bufs).items()}
    xg, held = shard_step(depth - 1, xg, held)
    kv_own, parcel = values(plan, row, [depth - 1], shards[-1:], act, pieces, sums, held)
    final = swap(parcel)

    scalars = (row, mix_numerator, partner)
    moments, averaged, placed = None, None, None
    for h in range(CHUNKS):
        last = h == CHUNKS - 1
        after = [] if h == 0 else [sent[-1]]
        *moments, stepped = adam(
            row, h, got[depth, h], grad, weights, first, second, moments, after + [parcel]
        )
        if placed is None:
            placed = place(plan, row, xg, arrived, 0)[0]
        others = partner_rows(stepped, partner, row[plan["replica"]], n_rep)
        if last:
            views = [View(final, columns, rows)]
            kv_views = (kv_own, View(final, 0, columns))
            x_grad, kv_out = place(plan, row, placed, views, depth - 1, kv_views)
        averaged = average(
            plan, scalars, h, stepped, others, averaged, columns, [kv_out] if last else [final]
        )
    return (
        kv_out[None],
        x_grad[None],
        averaged[None],
        moments[0][None],
        moments[1][None],
    )


def solution(mesh):
    placed = P("rep", "fsdp", None)
    return jax.shard_map(
        functools.partial(per_device, mesh.shape["rep"], mesh.shape["fsdp"]),
        mesh=mesh,
        in_specs=(placed,) * 5 + (P(), P()),
        out_specs=(placed,) * 5,
        check_vma=False,
    )
```

```python
import functools

import jax
import jax.numpy as jnp
import numpy as np
from jax import lax
from jax.experimental import pallas as pl
from jax.experimental.pallas import tpu as pltpu
from jax.sharding import PartitionSpec as P

beta_one = 0.9
beta_two = 0.999
learn_rate = 0.02
weight_decay = 0.1
adam_eps = 1e-08
corr_one = 1.0 - beta_one**10
corr_two = 1.0 - beta_two**10
mix_denom = 64.0

CHUNKS = 2
MIB = 1 << 20
ANY = pl.BlockSpec(memory_space=pl.ANY)

TN = (((0,), (0,)), ((), ()))
NT = (((1,), (1,)), ((), ()))


def dot(a, b, dims=(((1,), (0,)), ((), ()))):
    return lax.dot_general(a, b, dims, preferred_element_type=jnp.float32)


class Plan:
    def __init__(self, n_rep, n):
        self.depth = depth = n // 2
        self.columns = {}
        self.rows = [[] for _ in range(n_rep * n)]
        order = [
            sorted(range(depth), key=lambda q: (-abs(q - z), (q < z) != (2 * z >= depth)))
            for z in range(depth)
        ]
        self.sources = [set() for _ in range(depth)]
        arrivals = []
        for z in range(depth):
            below, above = ("b", "a") if z % 2 == 0 else ("a", "b")
            ups = [(z - t, (below, t)) for t in range(1, z + 1)]
            downs = [(z + t, (above, t)) for t in range(1, depth - z)]
            arrivals.append(downs + ups if 2 * z < depth else ups + downs)
            for j, (_, source) in enumerate(arrivals[z], 1):
                self.sources[j].add(source)
        self.sources = [sorted(s) for s in self.sources]
        for device in range(n_rep * n):
            replica, i = divmod(device, n)
            z, x = divmod(i, 2)
            put = functools.partial(self._put, device)
            put("replica", replica)
            put("own", i)
            for k in range(depth):
                put(f"pack{k}", 2 * order[z][k] + 1 - x)
            for s in range(2, depth + 1):
                up, down = z + 1 + depth - s, z - 1 - depth + s
                for link, q in zip("ab", (up, down) if z % 2 == 0 else (down, up)):
                    add = 0 <= q < depth
                    put(f"add_{link}{s}", int(add))
                    put(f"blk_{link}{s}", 2 * q + x if add else 0)
                    put(f"pos_{link}{s}", order[z].index(q) if add else 0)
            for j in range(depth):
                q, source = (z, None) if j == 0 else arrivals[z][j - 1]
                put(f"mine{j}", 2 * q + x)
                put(f"theirs{j}", 2 * q + 1 - x)
                put(f"piece{j}", order[z].index(q))
                put(f"source{j}", 0 if j == 0 else self.sources[j].index(source))
        self.table = np.asarray(self.rows, np.int32)

    def _put(self, i, name, value):
        column = self.columns.setdefault(name, len(self.columns))
        assert column == len(self.rows[i])
        self.rows[i].append(value)

    def __getitem__(self, name):
        return self.columns[name]


def call(kernel, row, ins, outs, grid=(1,), aliases=None, scratch=(), vmem=16):
    scalars = row if isinstance(row, tuple) else (row,)
    return pl.pallas_call(
        kernel,
        grid_spec=pltpu.PrefetchScalarGridSpec(
            num_scalar_prefetch=len(scalars),
            grid=grid,
            in_specs=[spec for _, spec in ins],
            out_specs=[spec for _, spec in outs],
            scratch_shapes=list(scratch),
        ),
        out_shape=[shape for shape, _ in outs],
        input_output_aliases=aliases or {},
        compiler_params=pltpu.CompilerParams(vmem_limit_bytes=vmem * MIB),
        cost_estimate=pl.CostEstimate(flops=0, bytes_accessed=0, transcendentals=0),
    )(*scalars, *[array for array, _ in ins])


def whole(array):
    rank = array.ndim
    return pl.BlockSpec(array.shape, lambda g, row: (0,) * rank)


def block(shape, column, scale=1, offset=0):
    return pl.BlockSpec(shape, lambda g, row: (0, row[column] * scale + offset))


def struct(shape, dtype):
    return jax.ShapeDtypeStruct(shape, dtype)


class View:
    def __init__(self, array, start, count):
        assert start % count == 0
        self.array, self.start, self.count = array, start, count
        self.shape = (array.shape[0], count)

    def operand(self):
        at = self.start // self.count
        return self.array, pl.BlockSpec(self.shape, lambda g, row: (0, at))


def pack(plan, row, width, views, act=None, turns=(), after=()):
    count = len(views) + len(turns)
    ins = [v.operand() for v in views]
    tokens = views[0].shape[0] if views else act.shape[0]
    ins += [(act, block((tokens, width), plan[f"pack{k}"])) for k in turns]
    sizes = [v.count for v in views] + [width] * len(turns)

    def kernel(row_ref, *refs):
        at = 0
        for ref, size in zip(refs[:count], sizes):
            refs[-1][:, at : at + size] = ref[...]
            at += size

    out = struct((tokens, sum(sizes)), jnp.bfloat16)
    return call(
        kernel,
        row,
        ins + [(a, ANY) for a in after],
        [(out, whole(out))],
    )[0]


def relay(plan, row, s, got, act, pieces, cot_own, cot_oth, after=()):
    (tokens, columns), rows = cot_own.shape, got["a"].shape[0]
    count = len(pieces)

    def kernel(row_ref, *refs):
        got_refs, act_refs = refs[0:2], refs[2:4]
        piece_refs = refs[4 : 4 + count]
        own_ref, oth_ref = refs[4 + count : 6 + count]
        out_refs, held = refs[-3:-1], refs[-1]
        for d, link in enumerate("ab"):
            add = row_ref[plan[f"add_{link}{s}"]]
            pos = row_ref[plan[f"pos_{link}{s}"]]

            @pl.when(add == 0)
            def _():
                out_refs[d][...] = got_refs[d][...]

            @pl.when(add == 1)
            def _():
                for j in range(count):

                    @pl.when(pos == j)
                    def _():
                        held[...] = piece_refs[j][...]

                total = dot(act_refs[d][...], own_ref[...], TN)
                total = total + dot(held[...], oth_ref[...], TN)
                out_refs[d][...] = (total + got_refs[d][...].astype(jnp.float32)).astype(jnp.bfloat16)

    ins = [got[link].operand() for link in "ba"]
    ins += [(act, block((tokens, rows), plan[f"blk_{link}{s}"])) for link in "ab"]
    ins += [view.operand() for view in (*pieces, cot_own, cot_oth)]
    ins += [(a, ANY) for a in after]
    out = struct((rows, columns), jnp.bfloat16)
    a, b = call(
        kernel,
        row,
        ins,
        [(out, whole(out)), (out, whole(out))],
        scratch=[pltpu.VMEM((tokens, rows), jnp.bfloat16)],
    )
    return {"a": a, "b": b}


def own_gradient(plan, row, act, piece, cot, cot_oth):
    tokens, columns = cot.shape
    rows = piece.shape[1]

    def kernel(row_ref, act_ref, piece_ref, own_ref, *refs):
        out_ref = refs[-1]
        at = 0
        for ref, view in zip(refs, cot_oth):
            part = slice(at, at + view.count)
            total = dot(act_ref[...], own_ref[:, part], TN)
            out_ref[:, part] = total + dot(piece_ref[...], ref[...], TN)
            at += view.count

    out = struct((rows, columns), jnp.float32)
    return call(
        kernel,
        row,
        [(act, block((tokens, rows), plan["own"])), piece.operand(), (cot, whole(cot))]
        + [view.operand() for view in cot_oth],
        [(out, whole(out))],
    )[0]


def project(plan, row, j, candidates, act, cot, cot_oth, xg_before, turn=None, front=None, after=()):
    (tokens, columns), rows = cot.shape, candidates[0][0].shape[0]
    flat = [c for candidate in candidates for c in candidate]
    starts = np.cumsum([0] + [len(candidate) for candidate in candidates])
    parts = max(len(candidate) for candidate in candidates)
    n_w, n_c = len(flat), len(cot_oth)
    ahead = 0 if front is None else front.count
    width = ahead + rows + (0 if turn is None else rows)

    def kernel(row_ref, *refs):
        w_refs, cot_refs = refs[:n_w], refs[n_w : n_w + n_c]
        own_ref = refs[n_w + n_c]
        xg_own, xg_oth, w_out, sems = refs[-4:]
        for c in range(len(candidates)):

            @pl.when(row_ref[plan[f"source{j}"]] == c)
            def _():
                copies, at = [], 0
                for p in range(starts[c], starts[c + 1]):
                    to = w_out.at[:, pl.ds(at, flat[p].shape[1])]
                    copies.append(pltpu.make_async_copy(w_refs[p], to, sems.at[len(copies)]))
                    at += flat[p].shape[1]
                for copy in copies:
                    copy.start()
                for copy in copies:
                    copy.wait()

        total, at = 0.0, 0
        for ref, view in zip(cot_refs, cot_oth):
            total = total + dot(ref[...], w_out[:, at : at + view.count], NT)
            at += view.count
        xg_oth[:, ahead : ahead + rows] = total.astype(jnp.bfloat16)
        rest = list(refs[n_w + n_c + 1 :])
        if front is not None:
            xg_oth[:, :ahead] = rest.pop(0)[...]
        if turn is not None:
            xg_oth[:, ahead + rows :] = rest.pop(0)[...]
        xg_own[...] = dot(own_ref[...], w_out[...], NT).astype(jnp.bfloat16)

    ins = [(w, ANY) for w in flat] + [view.operand() for view in cot_oth] + [(cot, whole(cot))]
    if front is not None:
        ins.append(front.operand())
    if turn is not None:
        ins.append((act, block((tokens, rows), plan[f"pack{turn}"])))
    aliases = {}
    if xg_before is not None:
        aliases = {1 + len(ins): 0}
        ins.append((xg_before, ANY))
    ins += [(a, ANY) for a in after]
    other = struct((tokens, width), jnp.bfloat16)
    shard = struct((rows, columns), jnp.bfloat16)
    return call(
        kernel,
        row,
        ins,
        [
            (struct(act.shape, jnp.bfloat16), block((tokens, rows), plan[f"mine{j}"])),
            (other, whole(other)),
            (shard, whole(shard)),
        ],
        aliases=aliases,
        scratch=[pltpu.SemaphoreType.DMA((parts,))],
        vmem=20,
    )


def values(plan, row, turns, shards, act, pieces, kept, behind=None):
    rows, columns = shards[0].shape
    tokens = act.shape[0]
    count, n_p = len(turns), len(pieces)
    extra = 0 if behind is None else behind.count

    def kernel(row_ref, *refs):
        w_refs, act_refs = refs[:count], refs[count : 2 * count]
        piece_refs = refs[2 * count : 2 * count + n_p]
        rest = list(refs[2 * count + n_p : -3])
        own_out, oth_out, held = refs[-3:]
        own = oth = 0.0
        if kept is not None:
            own, oth = rest.pop(0)[...], rest.pop(0)[...]
        for t, j in enumerate(turns):
            for p in range(n_p):

                @pl.when(row_ref[plan[f"piece{j}"]] == p)
                def _():
                    held[...] = piece_refs[p][...]

            oth = oth + dot(held[...], w_refs[t][...])
            own = own + dot(act_refs[t][...], w_refs[t][...])
        oth_out[:, :columns] = oth.astype(oth_out.dtype)
        if behind is not None:
            oth_out[:, columns:] = rest.pop(0)[...]
        own_out[...] = own

    ins = [(w, whole(w)) for w in shards]
    ins += [(act, block((tokens, rows), plan[f"mine{j}"])) for j in turns]
    ins += [p.operand() for p in pieces]
    if kept is not None:
        ins += [(k, whole(k)) for k in kept]
    if behind is not None:
        ins.append(behind.operand())
    own = struct((tokens, columns), jnp.float32)
    oth = struct((tokens, columns + extra), jnp.float32 if behind is None else jnp.bfloat16)
    return call(
        kernel,
        row,
        ins,
        [(own, whole(own)), (oth, whole(oth))],
        scratch=[pltpu.VMEM((tokens, rows), jnp.bfloat16)],
        vmem=28,
    )


def place(plan, row, xg, arrived, first, sums=None):
    count = len(arrived)
    tokens, width = arrived[0].shape
    table = [plan[f"theirs{first + j}"] for j in range(count)]

    def kernel(row_ref, *refs):
        g = pl.program_id(0)
        out_ref = refs[-1] if sums is None else refs[-2]
        for j in range(count):

            @pl.when(g == j)
            def _():
                out_ref[...] = refs[j][...]

        if sums is not None:
            total = refs[count][...] + refs[count + 1][...].astype(jnp.float32)
            refs[-1][...] = total.astype(jnp.bfloat16)

    def column(g, row):
        at = row[table[0]]
        for j in range(1, count):
            at = jnp.where(g == j, row[table[j]], at)
        return (0, at)

    ins = [view.operand() for view in arrived]
    outs = [(struct(xg.shape, xg.dtype), pl.BlockSpec((tokens, width), column))]
    if sums is not None:
        own, other = sums
        kv_block = pl.BlockSpec((tokens // count, own.shape[1]), lambda g, row: (g, 0))
        assert other.start == 0
        ins += [(own, kv_block), (other.array, kv_block)]
        outs.append((struct(own.shape, jnp.bfloat16), kv_block))
    aliases = {1 + len(ins): 0}
    return call(
        kernel,
        row,
        ins + [(xg, ANY)],
        outs,
        grid=(count,),
        aliases=aliases,
    )


def adam(row, h, got, grad, weights, first, second, kept, after=()):
    rows, columns = got["a"].shape
    assert got["a"].start == 0
    steps = 4 if rows % 64 == 0 else 1
    size = rows // steps

    def kernel(row_ref, up_ref, dn_ref, grad_ref, w_ref, a_ref, b_ref, *refs):
        a_out, b_out, stepped = refs[-3:]
        gradient = grad_ref[...] + up_ref[...].astype(jnp.float32) + dn_ref[...].astype(jnp.float32)
        moment_a = beta_one * a_ref[...] + (1.0 - beta_one) * gradient
        moment_b = beta_two * b_ref[...] + (1.0 - beta_two) * gradient * gradient
        old = w_ref[...].astype(jnp.float32)
        update = moment_a / corr_one / (jnp.sqrt(moment_b / corr_two) + adam_eps) + weight_decay * old
        a_out[...] = moment_a
        b_out[...] = moment_b
        stepped[...] = (old - learn_rate * update).astype(jnp.bfloat16)

    local = pl.BlockSpec((size, columns), lambda g, row: (g, 0))
    part = pl.BlockSpec((size, columns), lambda g, row: (g, h))
    ins = [(got["a"].array, local), (got["b"].array, local)]
    ins += [(a, part) for a in (grad, weights, first, second)]
    aliases = {}
    if kept is not None:
        aliases = {1 + len(ins): 0, 2 + len(ins): 1}
        ins += [(a, ANY) for a in kept]
    ins += [(a, ANY) for a in after]
    return call(
        kernel,
        row,
        ins,
        [
            (struct(first.shape, jnp.float32), part),
            (struct(second.shape, jnp.float32), part),
            (struct((rows, columns), jnp.bfloat16), local),
        ],
        grid=(steps,),
        aliases=aliases,
    )


def average(plan, scalars, h, stepped, others, kept, width, after=()):
    rows, columns = stepped.shape
    steps = 2 if rows % 32 == 0 else 1
    size = rows // steps
    count = len(others)

    def kernel(row_ref, numerator_ref, partner_ref, stepped_ref, *refs):
        mix = numerator_ref[row_ref[plan["replica"]]].astype(jnp.float32) / mix_denom
        for j in range(count):

            @pl.when((partner_ref[0] == j + 1) | (count == 1))
            def _():
                refs[-1][...] = (
                    (1.0 - mix) * stepped_ref[...].astype(jnp.float32)
                    + mix * refs[j][...].astype(jnp.float32)
                ).astype(jnp.bfloat16)

    local = pl.BlockSpec((size, columns), lambda g, *scalars: (g, 0))
    part = pl.BlockSpec((size, columns), lambda g, *scalars: (g, h))
    ins = [(a, local) for a in (stepped, *others)]
    if kept is not None:
        ins.append((kept, ANY))
    ins += [(a, ANY) for a in after]
    return call(
        kernel,
        scalars,
        ins,
        [(struct((rows, width), jnp.bfloat16), part)],
        grid=(steps,),
        aliases={} if kept is None else {count + 4: 0},
    )[0]


def partner_rows(stepped, partner, replica, n_rep):
    if n_rep != 4:
        gathered = lax.all_gather(stepped, "rep", axis=0, tiled=False)
        return [lax.dynamic_index_in_dim(gathered, partner[replica], 0, keepdims=False)]
    far = lax.ppermute(stepped, "rep", [(r, r ^ 2) for r in range(4)])
    core = [(r, r ^ 1) for r in range(4)]
    return [lax.ppermute(stepped, "rep", core), far, lax.ppermute(far, "rep", core)]


def per_device(
    n_rep, n, activations, kv_weight, kv_cotangent, first_moment, second_moment, partner, mix_numerator
):
    act, weights, cot = activations[0], kv_weight[0], kv_cotangent[0]
    first, second = first_moment[0], second_moment[0]
    plan = Plan(n_rep, n)
    depth = plan.depth
    rows, columns = weights.shape
    size = columns // CHUNKS
    row = lax.dynamic_index_in_dim(
        jnp.asarray(plan.table), lax.axis_index(("rep", "fsdp")), 0, keepdims=False
    )
    links = {
        "a": [(i, i + 2 if i // 2 % 2 == 0 else i - 2) for i in range(n)],
        "b": [(i, i - 2 if i // 2 % 2 == 0 else i + 2) for i in range(n)],
    }
    links = {name: [p for p in pairs if 0 <= p[1] < n] for name, pairs in links.items()}
    swap = functools.partial(lax.ppermute, axis_name="fsdp", perm=[(i, i ^ 1) for i in range(n)])

    def exchange(bufs):
        return {name: lax.ppermute(bufs[name], "fsdp", links[name]) for name in links}

    def part(array, h):
        return View(array, h * size, size)

    opening = exchange({"a": weights, "b": weights})
    got = {(1, h): {link: part(opening[link], h) for link in links} for h in range(CHUNKS)}

    def arrivals(link, slot):
        if slot == 1:
            return [opening[link]]
        return [got[slot, h][link].array for h in range(CHUNKS)]

    def send(*turns, after=()):
        return swap(pack(plan, row, rows, [], act, turns, after))

    parcel = swap(cot)
    cot_oth = [part(parcel, h) for h in range(CHUNKS)]
    pieces = [View(send(0), 0, rows)]
    parcel = send(*range(1, depth - 1), after=[parcel])
    pieces += [View(parcel, k * rows, rows) for k in range(depth - 2)]

    arrived, shards, sent = [], [], []
    xg, held = None, None

    def shard_step(j, xg, held):
        candidates = [[weights]]
        if j > 0:
            candidates = [arrivals(*source) for source in plan.sources[j]]
        turn = depth - 1 if j == 0 else None
        after = [sent[0]] if j == depth - 2 else list(bufs.values()) if j == 0 else []
        xg, parcel, shard = project(
            plan, row, j, candidates, act, cot, cot_oth, xg, turn, held, after
        )
        shards.append(shard)
        if 0 < j < depth - 2 or j == depth - 1:
            return xg, View(parcel, 0, parcel.shape[1])
        sent.append(swap(parcel))
        arrived.extend(View(sent[-1], t * rows, rows) for t in range(j + 1 - len(arrived)))
        if turn is not None:
            pieces.append(View(sent[-1], parcel.shape[1] - rows, rows))
        return xg, None

    bufs = {}
    for s in range(2, depth + 1):
        if s == depth:
            for j in range(1, depth - 1):
                xg, held = shard_step(j, xg, held)
            grad = own_gradient(plan, row, act, pieces[depth - 1], cot, cot_oth)
            sums = values(plan, row, list(range(depth - 1)), shards, act, pieces, None)
        for h in range(CHUNKS):
            after = list(bufs.values())[:1]
            if s == depth and h == CHUNKS - 1:
                after += [sums[0], grad]
            bufs = relay(
                plan, row, s, got[s - 1, h], act, pieces[: s - 1], part(cot, h), cot_oth[h], after
            )
            got[s, h] = {link: part(array, 0) for link, array in exchange(bufs).items()}
            if s == 3 and h == 0:
                xg, held = shard_step(0, xg, held)
    xg, held = shard_step(depth - 1, xg, held)
    kv_own, parcel = values(plan, row, [depth - 1], shards[-1:], act, pieces, sums, held)
    final = swap(parcel)

    scalars = (row, mix_numerator, partner)
    moments, averaged, placed = None, None, None
    for h in range(CHUNKS):
        last = h == CHUNKS - 1
        after = [] if h == 0 else [placed]
        *moments, stepped = adam(
            row, h, got[depth, h], grad, weights, first, second, moments, after + [parcel]
        )
        if placed is None:
            placed = place(plan, row, xg, arrived, 0)[0]
        others = partner_rows(stepped, partner, row[plan["replica"]], n_rep)
        if last:
            views = [View(final, columns, rows)]
            kv_views = (kv_own, View(final, 0, columns))
            x_grad, kv_out = place(plan, row, placed, views, depth - 1, kv_views)
        averaged = average(
            plan, scalars, h, stepped, others, averaged, columns, [kv_out] if last else [final]
        )
    return (
        kv_out[None],
        x_grad[None],
        averaged[None],
        moments[0][None],
        moments[1][None],
    )


def solution(mesh):
    placed = P("rep", "fsdp", None)
    return jax.shard_map(
        functools.partial(per_device, mesh.shape["rep"], mesh.shape["fsdp"]),
        mesh=mesh,
        in_specs=(placed,) * 5 + (P(), P()),
        out_specs=(placed,) * 5,
        check_vma=False,
    )
```

```python
import functools

import jax
import jax.numpy as jnp
import numpy as np
from jax import lax
from jax.experimental import pallas as pl
from jax.experimental.pallas import tpu as pltpu
from jax.sharding import PartitionSpec as P

beta_one = 0.9
beta_two = 0.999
learn_rate = 0.02
weight_decay = 0.1
adam_eps = 1e-08
corr_one = 1.0 - beta_one**10
corr_two = 1.0 - beta_two**10
mix_denom = 64.0

CHUNKS = 2
MIB = 1 << 20
ANY = pl.BlockSpec(memory_space=pl.ANY)

TN = (((0,), (0,)), ((), ()))
NT = (((1,), (1,)), ((), ()))


def dot(a, b, dims=(((1,), (0,)), ((), ()))):
    return lax.dot_general(a, b, dims, preferred_element_type=jnp.float32)


class Plan:
    def __init__(self, n_rep, n):
        self.depth = depth = n // 2
        self.columns = {}
        self.rows = [[] for _ in range(n_rep * n)]
        order = [
            sorted(range(depth), key=lambda q: (-abs(q - z), (q < z) != (2 * z >= depth)))
            for z in range(depth)
        ]
        self.sources = [set() for _ in range(depth)]
        arrivals = []
        for z in range(depth):
            below, above = ("b", "a") if z % 2 == 0 else ("a", "b")
            ups = [(z - t, (below, t)) for t in range(1, z + 1)]
            downs = [(z + t, (above, t)) for t in range(1, depth - z)]
            arrivals.append(downs + ups if 2 * z < depth else ups + downs)
            for j, (_, source) in enumerate(arrivals[z], 1):
                self.sources[j].add(source)
        self.sources = [sorted(s) for s in self.sources]
        for device in range(n_rep * n):
            replica, i = divmod(device, n)
            z, x = divmod(i, 2)
            put = functools.partial(self._put, device)
            put("replica", replica)
            put("own", i)
            for k in range(depth):
                put(f"pack{k}", 2 * order[z][k] + 1 - x)
            for s in range(2, depth + 1):
                up, down = z + 1 + depth - s, z - 1 - depth + s
                for link, q in zip("ab", (up, down) if z % 2 == 0 else (down, up)):
                    add = 0 <= q < depth
                    put(f"add_{link}{s}", int(add))
                    put(f"blk_{link}{s}", 2 * q + x if add else 0)
                    put(f"pos_{link}{s}", order[z].index(q) if add else 0)
            for j in range(depth):
                q, source = (z, None) if j == 0 else arrivals[z][j - 1]
                put(f"mine{j}", 2 * q + x)
                put(f"theirs{j}", 2 * q + 1 - x)
                put(f"piece{j}", order[z].index(q))
                put(f"source{j}", 0 if j == 0 else self.sources[j].index(source))
        self.table = np.asarray(self.rows, np.int32)

    def _put(self, i, name, value):
        column = self.columns.setdefault(name, len(self.columns))
        assert column == len(self.rows[i])
        self.rows[i].append(value)

    def __getitem__(self, name):
        return self.columns[name]


def call(kernel, row, ins, outs, grid=(1,), aliases=None, scratch=(), vmem=16):
    scalars = row if isinstance(row, tuple) else (row,)
    return pl.pallas_call(
        kernel,
        grid_spec=pltpu.PrefetchScalarGridSpec(
            num_scalar_prefetch=len(scalars),
            grid=grid,
            in_specs=[spec for _, spec in ins],
            out_specs=[spec for _, spec in outs],
            scratch_shapes=list(scratch),
        ),
        out_shape=[shape for shape, _ in outs],
        input_output_aliases=aliases or {},
        compiler_params=pltpu.CompilerParams(vmem_limit_bytes=vmem * MIB),
        cost_estimate=pl.CostEstimate(flops=0, bytes_accessed=0, transcendentals=0),
    )(*scalars, *[array for array, _ in ins])


def whole(array):
    rank = array.ndim
    return pl.BlockSpec(array.shape, lambda g, row: (0,) * rank)


def block(shape, column, scale=1, offset=0):
    return pl.BlockSpec(shape, lambda g, row: (0, row[column] * scale + offset))


def struct(shape, dtype):
    return jax.ShapeDtypeStruct(shape, dtype)


class View:
    def __init__(self, array, start, count):
        assert start % count == 0
        self.array, self.start, self.count = array, start, count
        self.shape = (array.shape[0], count)

    def operand(self):
        at = self.start // self.count
        return self.array, pl.BlockSpec(self.shape, lambda g, row: (0, at))


def pack(plan, row, width, views, act=None, turns=(), after=()):
    count = len(views) + len(turns)
    ins = [v.operand() for v in views]
    tokens = views[0].shape[0] if views else act.shape[0]
    ins += [(act, block((tokens, width), plan[f"pack{k}"])) for k in turns]
    sizes = [v.count for v in views] + [width] * len(turns)

    def kernel(row_ref, *refs):
        at = 0
        for ref, size in zip(refs[:count], sizes):
            refs[-1][:, at : at + size] = ref[...]
            at += size

    out = struct((tokens, sum(sizes)), jnp.bfloat16)
    return call(
        kernel,
        row,
        ins + [(a, ANY) for a in after],
        [(out, whole(out))],
    )[0]


def relay(plan, row, s, got, act, pieces, cot_own, cot_oth, after=()):
    (tokens, columns), rows = cot_own.shape, got["a"].shape[0]
    count = len(pieces)

    def kernel(row_ref, *refs):
        got_refs, act_refs = refs[0:2], refs[2:4]
        piece_refs = refs[4 : 4 + count]
        own_ref, oth_ref = refs[4 + count : 6 + count]
        out_refs, held = refs[-3:-1], refs[-1]
        for d, link in enumerate("ab"):
            add = row_ref[plan[f"add_{link}{s}"]]
            pos = row_ref[plan[f"pos_{link}{s}"]]

            @pl.when(add == 0)
            def _():
                out_refs[d][...] = got_refs[d][...]

            @pl.when(add == 1)
            def _():
                for j in range(count):

                    @pl.when(pos == j)
                    def _():
                        held[...] = piece_refs[j][...]

                total = dot(act_refs[d][...], own_ref[...], TN)
                total = total + dot(held[...], oth_ref[...], TN)
                out_refs[d][...] = (total + got_refs[d][...].astype(jnp.float32)).astype(jnp.bfloat16)

    ins = [got[link].operand() for link in "ba"]
    ins += [(act, block((tokens, rows), plan[f"blk_{link}{s}"])) for link in "ab"]
    ins += [view.operand() for view in (*pieces, cot_own, cot_oth)]
    ins += [(a, ANY) for a in after]
    out = struct((rows, columns), jnp.bfloat16)
    a, b = call(
        kernel,
        row,
        ins,
        [(out, whole(out)), (out, whole(out))],
        scratch=[pltpu.VMEM((tokens, rows), jnp.bfloat16)],
    )
    return {"a": a, "b": b}


def own_gradient(plan, row, act, piece, cot, cot_oth):
    tokens, columns = cot.shape
    rows = piece.shape[1]

    def kernel(row_ref, act_ref, piece_ref, own_ref, *refs):
        out_ref = refs[-1]
        at = 0
        for ref, view in zip(refs, cot_oth):
            part = slice(at, at + view.count)
            total = dot(act_ref[...], own_ref[:, part], TN)
            out_ref[:, part] = total + dot(piece_ref[...], ref[...], TN)
            at += view.count

    out = struct((rows, columns), jnp.float32)
    return call(
        kernel,
        row,
        [(act, block((tokens, rows), plan["own"])), piece.operand(), (cot, whole(cot))]
        + [view.operand() for view in cot_oth],
        [(out, whole(out))],
    )[0]


def project(plan, row, j, candidates, act, cot, cot_oth, xg_before, turns=(), after=()):
    (tokens, columns), rows = cot.shape, candidates[0][0].shape[0]
    flat = [c for candidate in candidates for c in candidate]
    starts = np.cumsum([0] + [len(candidate) for candidate in candidates])
    parts = max(len(candidate) for candidate in candidates)
    n_w, n_c = len(flat), len(cot_oth)
    width = rows * (1 + len(turns))

    def kernel(row_ref, *refs):
        w_refs, cot_refs = refs[:n_w], refs[n_w : n_w + n_c]
        own_ref = refs[n_w + n_c]
        xg_own, xg_oth, w_out, sems = refs[-4:]
        for c in range(len(candidates)):

            @pl.when(row_ref[plan[f"source{j}"]] == c)
            def _():
                copies, at = [], 0
                for p in range(starts[c], starts[c + 1]):
                    to = w_out.at[:, pl.ds(at, flat[p].shape[1])]
                    copies.append(pltpu.make_async_copy(w_refs[p], to, sems.at[len(copies)]))
                    at += flat[p].shape[1]
                for copy in copies:
                    copy.start()
                for copy in copies:
                    copy.wait()

        total, at = 0.0, 0
        for ref, view in zip(cot_refs, cot_oth):
            total = total + dot(ref[...], w_out[:, at : at + view.count], NT)
            at += view.count
        xg_oth[:, :rows] = total.astype(jnp.bfloat16)
        for t in range(len(turns)):
            ref = refs[n_w + n_c + 1 + t]
            xg_oth[:, (t + 1) * rows : (t + 2) * rows] = ref[...]
        xg_own[...] = dot(own_ref[...], w_out[...], NT).astype(jnp.bfloat16)

    ins = [(w, ANY) for w in flat] + [view.operand() for view in cot_oth] + [(cot, whole(cot))]
    ins += [(act, block((tokens, rows), plan[f"pack{turn}"])) for turn in turns]
    aliases = {}
    if xg_before is not None:
        aliases = {1 + len(ins): 0}
        ins.append((xg_before, ANY))
    ins += [(a, ANY) for a in after]
    other = struct((tokens, width), jnp.bfloat16)
    shard = struct((rows, columns), jnp.bfloat16)
    return call(
        kernel,
        row,
        ins,
        [
            (struct(act.shape, jnp.bfloat16), block((tokens, rows), plan[f"mine{j}"])),
            (other, whole(other)),
            (shard, whole(shard)),
        ],
        aliases=aliases,
        scratch=[pltpu.SemaphoreType.DMA((parts,))],
        vmem=20,
    )


def values(plan, row, turns, shards, act, pieces, kept, behind=None):
    rows, columns = shards[0].shape
    tokens = act.shape[0]
    count, n_p = len(turns), len(pieces)
    extra = 0 if behind is None else behind.count

    def kernel(row_ref, *refs):
        w_refs, act_refs = refs[:count], refs[count : 2 * count]
        piece_refs = refs[2 * count : 2 * count + n_p]
        rest = list(refs[2 * count + n_p : -3])
        own_out, oth_out, held = refs[-3:]
        own = oth = 0.0
        if kept is not None:
            own, oth = rest.pop(0)[...], rest.pop(0)[...]
        for t, j in enumerate(turns):
            for p in range(n_p):

                @pl.when(row_ref[plan[f"piece{j}"]] == p)
                def _():
                    held[...] = piece_refs[p][...]

            oth = oth + dot(held[...], w_refs[t][...])
            own = own + dot(act_refs[t][...], w_refs[t][...])
        oth_out[:, :columns] = oth.astype(oth_out.dtype)
        if behind is not None:
            oth_out[:, columns:] = rest.pop(0)[...]
        own_out[...] = own

    ins = [(w, whole(w)) for w in shards]
    ins += [(act, block((tokens, rows), plan[f"mine{j}"])) for j in turns]
    ins += [p.operand() for p in pieces]
    if kept is not None:
        ins += [(k, whole(k)) for k in kept]
    if behind is not None:
        ins.append(behind.operand())
    own = struct((tokens, columns), jnp.float32)
    oth = struct((tokens, columns + extra), jnp.float32 if behind is None else jnp.bfloat16)
    return call(
        kernel,
        row,
        ins,
        [(own, whole(own)), (oth, whole(oth))],
        scratch=[pltpu.VMEM((tokens, rows), jnp.bfloat16)],
        vmem=28,
    )


def place(plan, row, xg, arrived, first, sums=None):
    count = len(arrived)
    tokens, width = arrived[0].shape
    table = [plan[f"theirs{first + j}"] for j in range(count)]

    def kernel(row_ref, *refs):
        g = pl.program_id(0)
        out_ref = refs[-1] if sums is None else refs[-2]
        for j in range(count):

            @pl.when(g == j)
            def _():
                out_ref[...] = refs[j][...]

        if sums is not None:
            total = refs[count][...] + refs[count + 1][...].astype(jnp.float32)
            refs[-1][...] = total.astype(jnp.bfloat16)

    def column(g, row):
        at = row[table[0]]
        for j in range(1, count):
            at = jnp.where(g == j, row[table[j]], at)
        return (0, at)

    ins = [view.operand() for view in arrived]
    outs = [(struct(xg.shape, xg.dtype), pl.BlockSpec((tokens, width), column))]
    if sums is not None:
        own, other = sums
        kv_block = pl.BlockSpec((tokens // count, own.shape[1]), lambda g, row: (g, 0))
        assert other.start == 0
        ins += [(own, kv_block), (other.array, kv_block)]
        outs.append((struct(own.shape, jnp.bfloat16), kv_block))
    aliases = {1 + len(ins): 0}
    return call(
        kernel,
        row,
        ins + [(xg, ANY)],
        outs,
        grid=(count,),
        aliases=aliases,
    )


def adam(row, h, got, grad, weights, first, second, kept, after=()):
    rows, columns = got["a"].shape
    assert got["a"].start == 0
    steps = 4 if rows % 64 == 0 else 1
    size = rows // steps

    def kernel(row_ref, up_ref, dn_ref, grad_ref, w_ref, a_ref, b_ref, *refs):
        a_out, b_out, stepped = refs[-3:]
        gradient = grad_ref[...] + up_ref[...].astype(jnp.float32) + dn_ref[...].astype(jnp.float32)
        moment_a = beta_one * a_ref[...] + (1.0 - beta_one) * gradient
        moment_b = beta_two * b_ref[...] + (1.0 - beta_two) * gradient * gradient
        old = w_ref[...].astype(jnp.float32)
        update = moment_a / corr_one / (jnp.sqrt(moment_b / corr_two) + adam_eps) + weight_decay * old
        a_out[...] = moment_a
        b_out[...] = moment_b
        stepped[...] = (old - learn_rate * update).astype(jnp.bfloat16)

    local = pl.BlockSpec((size, columns), lambda g, row: (g, 0))
    part = pl.BlockSpec((size, columns), lambda g, row: (g, h))
    ins = [(got["a"].array, local), (got["b"].array, local)]
    ins += [(a, part) for a in (grad, weights, first, second)]
    aliases = {}
    if kept is not None:
        aliases = {1 + len(ins): 0, 2 + len(ins): 1}
        ins += [(a, ANY) for a in kept]
    ins += [(a, ANY) for a in after]
    return call(
        kernel,
        row,
        ins,
        [
            (struct(first.shape, jnp.float32), part),
            (struct(second.shape, jnp.float32), part),
            (struct((rows, columns), jnp.bfloat16), local),
        ],
        grid=(steps,),
        aliases=aliases,
    )


def average(plan, scalars, h, stepped, others, kept, width, after=()):
    rows, columns = stepped.shape
    steps = 2 if rows % 32 == 0 else 1
    size = rows // steps
    count = len(others)

    def kernel(row_ref, numerator_ref, partner_ref, stepped_ref, *refs):
        mix = numerator_ref[row_ref[plan["replica"]]].astype(jnp.float32) / mix_denom
        for j in range(count):

            @pl.when((partner_ref[0] == j + 1) | (count == 1))
            def _():
                refs[-1][...] = (
                    (1.0 - mix) * stepped_ref[...].astype(jnp.float32)
                    + mix * refs[j][...].astype(jnp.float32)
                ).astype(jnp.bfloat16)

    local = pl.BlockSpec((size, columns), lambda g, *scalars: (g, 0))
    part = pl.BlockSpec((size, columns), lambda g, *scalars: (g, h))
    ins = [(a, local) for a in (stepped, *others)]
    if kept is not None:
        ins.append((kept, ANY))
    ins += [(a, ANY) for a in after]
    return call(
        kernel,
        scalars,
        ins,
        [(struct((rows, width), jnp.bfloat16), part)],
        grid=(steps,),
        aliases={} if kept is None else {count + 4: 0},
    )[0]


def partner_rows(stepped, partner, replica, n_rep):
    if n_rep != 4:
        gathered = lax.all_gather(stepped, "rep", axis=0, tiled=False)
        return [lax.dynamic_index_in_dim(gathered, partner[replica], 0, keepdims=False)]
    far = lax.ppermute(stepped, "rep", [(r, r ^ 2) for r in range(4)])
    core = [(r, r ^ 1) for r in range(4)]
    return [lax.ppermute(stepped, "rep", core), far, lax.ppermute(far, "rep", core)]


def per_device(
    n_rep, n, activations, kv_weight, kv_cotangent, first_moment, second_moment, partner, mix_numerator
):
    act, weights, cot = activations[0], kv_weight[0], kv_cotangent[0]
    first, second = first_moment[0], second_moment[0]
    plan = Plan(n_rep, n)
    depth = plan.depth
    rows, columns = weights.shape
    size = columns // CHUNKS
    row = lax.dynamic_index_in_dim(
        jnp.asarray(plan.table), lax.axis_index(("rep", "fsdp")), 0, keepdims=False
    )
    links = {
        "a": [(i, i + 2 if i // 2 % 2 == 0 else i - 2) for i in range(n)],
        "b": [(i, i - 2 if i // 2 % 2 == 0 else i + 2) for i in range(n)],
    }
    links = {name: [p for p in pairs if 0 <= p[1] < n] for name, pairs in links.items()}
    swap = functools.partial(lax.ppermute, axis_name="fsdp", perm=[(i, i ^ 1) for i in range(n)])

    def exchange(bufs):
        return {name: lax.ppermute(bufs[name], "fsdp", links[name]) for name in links}

    def part(array, h):
        return View(array, h * size, size)

    opening = exchange({"a": weights, "b": weights})
    got = {(1, h): {link: part(opening[link], h) for link in links} for h in range(CHUNKS)}

    def arrivals(link, slot):
        if slot == 1:
            return [opening[link]]
        return [got[slot, h][link].array for h in range(CHUNKS)]

    def send(*turns, after=()):
        return swap(pack(plan, row, rows, [], act, turns, after))

    parcel = swap(cot)
    cot_oth = [part(parcel, h) for h in range(CHUNKS)]
    pieces = [View(send(0), 0, rows)]

    arrived, shards = [], []

    def shard_step(j, xg, turns, after=()):
        candidates = [[weights]]
        if j > 0:
            candidates = [arrivals(*source) for source in plan.sources[j]]
        ahead = turns if j > 0 else []
        xg, parcel, shard = project(plan, row, j, candidates, act, cot, cot_oth, xg, ahead, after)
        shards.append(shard)
        if j == 0:
            front = View(parcel, 0, rows)
            parcel = pack(plan, row, rows, [front], act, turns, [pieces[0].array])
        if j == depth - 1:
            return xg, View(parcel, 0, rows)
        parcel = swap(parcel)
        arrived.append(View(parcel, 0, rows))
        pieces.extend(View(parcel, (t + 1) * rows, rows) for t in range(len(turns)))
        return xg, None

    xg, _ = shard_step(0, None, range(1, depth - 1))
    bufs = {}
    for s in range(2, depth + 1):
        if s == depth:
            for j in range(1, depth - 1):
                turns = [depth - 1] if j == 1 else []
                xg, _ = shard_step(j, xg, turns, [arrived[-1].array])
            grad = own_gradient(plan, row, act, pieces[depth - 1], cot, cot_oth)
            sums = values(plan, row, list(range(depth - 1)), shards, act, pieces, None)
        for h in range(CHUNKS):
            after = list(bufs.values())[:1]
            if s == depth and h == CHUNKS - 1:
                after += [sums[0], grad]
            bufs = relay(
                plan, row, s, got[s - 1, h], act, pieces[: s - 1], part(cot, h), cot_oth[h], after
            )
            got[s, h] = {link: part(array, 0) for link, array in exchange(bufs).items()}
    xg, held = shard_step(depth - 1, xg, [])
    kv_own, parcel = values(plan, row, [depth - 1], shards[-1:], act, pieces, sums, held)
    final = swap(parcel)

    scalars = (row, mix_numerator, partner)
    moments, averaged, placed = None, None, None
    for h in range(CHUNKS):
        last = h == CHUNKS - 1
        after = [] if h == 0 else [placed]
        *moments, stepped = adam(
            row, h, got[depth, h], grad, weights, first, second, moments, after + [parcel]
        )
        if placed is None:
            placed = place(plan, row, xg, arrived, 0)[0]
        others = partner_rows(stepped, partner, row[plan["replica"]], n_rep)
        if last:
            views = [View(final, columns, rows)]
            kv_views = (kv_own, View(final, 0, columns))
            x_grad, kv_out = place(plan, row, placed, views, depth - 1, kv_views)
        averaged = average(
            plan, scalars, h, stepped, others, averaged, columns, [kv_out] if last else [final]
        )
    return (
        kv_out[None],
        x_grad[None],
        averaged[None],
        moments[0][None],
        moments[1][None],
    )


def solution(mesh):
    placed = P("rep", "fsdp", None)
    return jax.shard_map(
        functools.partial(per_device, mesh.shape["rep"], mesh.shape["fsdp"]),
        mesh=mesh,
        in_specs=(placed,) * 5 + (P(), P()),
        out_specs=(placed,) * 5,
        check_vma=False,
    )
```

```python
import functools

import jax
import jax.numpy as jnp
import numpy as np
from jax import lax
from jax.experimental import pallas as pl
from jax.experimental.pallas import tpu as pltpu
from jax.sharding import PartitionSpec as P

beta_one = 0.9
beta_two = 0.999
learn_rate = 0.02
weight_decay = 0.1
adam_eps = 1e-08
corr_one = 1.0 - beta_one**10
corr_two = 1.0 - beta_two**10
mix_denom = 64.0

CHUNKS = 2
MIB = 1 << 20
ANY = pl.BlockSpec(memory_space=pl.ANY)
HBM = pl.BlockSpec(memory_space=pltpu.HBM)

TN = (((0,), (0,)), ((), ()))
NT = (((1,), (1,)), ((), ()))


def dot(a, b, dims=(((1,), (0,)), ((), ()))):
    return lax.dot_general(a, b, dims, preferred_element_type=jnp.float32)


class Plan:
    def __init__(self, n_rep, n):
        self.depth = depth = n // 2
        self.columns = {}
        self.rows = [[] for _ in range(n_rep * n)]
        order = [
            sorted(range(depth), key=lambda q: (-abs(q - z), (q < z) != (2 * z >= depth)))
            for z in range(depth)
        ]
        self.sources = [set() for _ in range(depth)]
        arrivals = []
        for z in range(depth):
            below, above = ("b", "a") if z % 2 == 0 else ("a", "b")
            ups = [(z - t, (below, t)) for t in range(1, z + 1)]
            downs = [(z + t, (above, t)) for t in range(1, depth - z)]
            arrivals.append(downs + ups if 2 * z < depth else ups + downs)
            for j, (_, source) in enumerate(arrivals[z], 1):
                self.sources[j].add(source)
        self.sources = [sorted(s) for s in self.sources]
        for device in range(n_rep * n):
            replica, i = divmod(device, n)
            z, x = divmod(i, 2)
            put = functools.partial(self._put, device)
            put("replica", replica)
            put("own", i)
            for k in range(depth):
                put(f"pack{k}", 2 * order[z][k] + 1 - x)
            for s in range(2, depth + 1):
                up, down = z + 1 + depth - s, z - 1 - depth + s
                for link, q in zip("ab", (up, down) if z % 2 == 0 else (down, up)):
                    add = 0 <= q < depth
                    put(f"add_{link}{s}", int(add))
                    put(f"blk_{link}{s}", 2 * q + x if add else 0)
                    put(f"pos_{link}{s}", order[z].index(q) if add else 0)
            for j in range(depth):
                q, source = (z, None) if j == 0 else arrivals[z][j - 1]
                put(f"mine{j}", 2 * q + x)
                put(f"theirs{j}", 2 * q + 1 - x)
                put(f"piece{j}", order[z].index(q))
                put(f"source{j}", 0 if j == 0 else self.sources[j].index(source))
        self.table = np.asarray(self.rows, np.int32)

    def _put(self, i, name, value):
        column = self.columns.setdefault(name, len(self.columns))
        assert column == len(self.rows[i])
        self.rows[i].append(value)

    def __getitem__(self, name):
        return self.columns[name]


def call(kernel, row, ins, outs, grid=(1,), aliases=None, scratch=(), vmem=16):
    scalars = row if isinstance(row, tuple) else (row,)
    return pl.pallas_call(
        kernel,
        grid_spec=pltpu.PrefetchScalarGridSpec(
            num_scalar_prefetch=len(scalars),
            grid=grid,
            in_specs=[spec for _, spec in ins],
            out_specs=[spec for _, spec in outs],
            scratch_shapes=list(scratch),
        ),
        out_shape=[shape for shape, _ in outs],
        input_output_aliases=aliases or {},
        compiler_params=pltpu.CompilerParams(vmem_limit_bytes=vmem * MIB),
        cost_estimate=pl.CostEstimate(flops=0, bytes_accessed=0, transcendentals=0),
    )(*scalars, *[array for array, _ in ins])


def whole(array):
    rank = array.ndim
    return pl.BlockSpec(array.shape, lambda g, row: (0,) * rank)


def block(shape, column, scale=1, offset=0):
    return pl.BlockSpec(shape, lambda g, row: (0, row[column] * scale + offset))


def struct(shape, dtype):
    return jax.ShapeDtypeStruct(shape, dtype)


class View:
    def __init__(self, array, start, count):
        assert start % count == 0
        self.array, self.start, self.count = array, start, count
        self.shape = (array.shape[0], count)

    def operand(self):
        at = self.start // self.count
        return self.array, pl.BlockSpec(self.shape, lambda g, row: (0, at))


def pack(plan, row, width, views, act=None, turns=(), after=()):
    count = len(views) + len(turns)
    ins = [v.operand() for v in views]
    tokens = views[0].shape[0] if views else act.shape[0]
    ins += [(act, block((tokens, width), plan[f"pack{k}"])) for k in turns]
    sizes = [v.count for v in views] + [width] * len(turns)

    def kernel(row_ref, *refs):
        at = 0
        for ref, size in zip(refs[:count], sizes):
            refs[-1][:, at : at + size] = ref[...]
            at += size

    out = struct((tokens, sum(sizes)), jnp.bfloat16)
    return call(
        kernel,
        row,
        ins + [(a, ANY) for a in after],
        [(out, whole(out))],
    )[0]


def relay(plan, row, s, got, act, pieces, cot_own, cot_oth, after=()):
    (tokens, columns), rows = cot_own.shape, got["a"].shape[0]
    count = len(pieces)

    def kernel(row_ref, *refs):
        got_refs, act_refs = refs[0:2], refs[2:4]
        piece_refs = refs[4 : 4 + count]
        own_ref, oth_ref = refs[4 + count : 6 + count]
        out_refs, held = refs[-3:-1], refs[-1]
        for d, link in enumerate("ab"):
            add = row_ref[plan[f"add_{link}{s}"]]
            pos = row_ref[plan[f"pos_{link}{s}"]]

            @pl.when(add == 0)
            def _():
                out_refs[d][...] = got_refs[d][...]

            @pl.when(add == 1)
            def _():
                for j in range(count):

                    @pl.when(pos == j)
                    def _():
                        held[...] = piece_refs[j][...]

                total = dot(act_refs[d][...], own_ref[...], TN)
                total = total + dot(held[...], oth_ref[...], TN)
                out_refs[d][...] = (total + got_refs[d][...].astype(jnp.float32)).astype(jnp.bfloat16)

    ins = [got[link].operand() for link in "ba"]
    ins += [(act, block((tokens, rows), plan[f"blk_{link}{s}"])) for link in "ab"]
    ins += [view.operand() for view in (*pieces, cot_own, cot_oth)]
    ins += [(a, ANY) for a in after]
    out = struct((rows, columns), jnp.bfloat16)
    a, b = call(
        kernel,
        row,
        ins,
        [(out, whole(out)), (out, whole(out))],
        scratch=[pltpu.VMEM((tokens, rows), jnp.bfloat16)],
    )
    return {"a": a, "b": b}


def own_gradient(plan, row, act, piece, cot, cot_oth):
    tokens, columns = cot.shape
    rows = piece.shape[1]

    def kernel(row_ref, act_ref, piece_ref, own_ref, *refs):
        out_ref = refs[-1]
        at = 0
        for ref, view in zip(refs, cot_oth):
            part = slice(at, at + view.count)
            total = dot(act_ref[...], own_ref[:, part], TN)
            out_ref[:, part] = total + dot(piece_ref[...], ref[...], TN)
            at += view.count

    out = struct((rows, columns), jnp.float32)
    return call(
        kernel,
        row,
        [(act, block((tokens, rows), plan["own"])), piece.operand(), (cot, whole(cot))]
        + [view.operand() for view in cot_oth],
        [(out, whole(out))],
    )[0]


def project(plan, row, j, candidates, act, cot, cot_oth, xg_before):
    (tokens, columns), rows = cot.shape, candidates[0][0].shape[0]
    flat = [c for candidate in candidates for c in candidate]
    starts = np.cumsum([0] + [len(candidate) for candidate in candidates])
    parts = max(len(candidate) for candidate in candidates)
    n_w, n_c = len(flat), len(cot_oth)

    def kernel(row_ref, *refs):
        w_refs, cot_refs = refs[:n_w], refs[n_w : n_w + n_c]
        own_ref = refs[n_w + n_c]
        xg_own, xg_oth, w_out, sems = refs[-4:]
        for c in range(len(candidates)):

            @pl.when(row_ref[plan[f"source{j}"]] == c)
            def _():
                copies, at = [], 0
                for p in range(starts[c], starts[c + 1]):
                    to = w_out.at[:, pl.ds(at, flat[p].shape[1])]
                    copies.append(pltpu.make_async_copy(w_refs[p], to, sems.at[len(copies)]))
                    at += flat[p].shape[1]
                for copy in copies:
                    copy.start()
                for copy in copies:
                    copy.wait()

        total, at = 0.0, 0
        for ref, view in zip(cot_refs, cot_oth):
            total = total + dot(ref[...], w_out[:, at : at + view.count], NT)
            at += view.count
        xg_oth[...] = total.astype(jnp.bfloat16)
        xg_own[...] = dot(own_ref[...], w_out[...], NT).astype(jnp.bfloat16)

    ins = [(w, ANY) for w in flat] + [view.operand() for view in cot_oth] + [(cot, whole(cot))]
    aliases = {}
    if xg_before is not None:
        aliases = {1 + len(ins): 0}
        ins.append((xg_before, HBM))
    other = struct((tokens, rows), jnp.bfloat16)
    shard = struct((rows, columns), jnp.bfloat16)
    return call(
        kernel,
        row,
        ins,
        [
            (struct(act.shape, jnp.bfloat16), block((tokens, rows), plan[f"mine{j}"])),
            (other, whole(other)),
            (shard, whole(shard)),
        ],
        aliases=aliases,
        scratch=[pltpu.SemaphoreType.DMA((parts,))],
        vmem=20,
    )


def values(plan, row, turns, shards, act, pieces, kept, behind=None):
    rows, columns = shards[0].shape
    tokens = act.shape[0]
    count, n_p = len(turns), len(pieces)
    extra = 0 if behind is None else behind.count

    def kernel(row_ref, *refs):
        w_refs, act_refs = refs[:count], refs[count : 2 * count]
        piece_refs = refs[2 * count : 2 * count + n_p]
        rest = list(refs[2 * count + n_p : -3])
        own_out, oth_out, held = refs[-3:]
        own = oth = 0.0
        if kept is not None:
            own, oth = rest.pop(0)[...], rest.pop(0)[...]
        for t, j in enumerate(turns):
            for p in range(n_p):

                @pl.when(row_ref[plan[f"piece{j}"]] == p)
                def _():
                    held[...] = piece_refs[p][...]

            oth = oth + dot(held[...], w_refs[t][...])
            own = own + dot(act_refs[t][...], w_refs[t][...])
        oth_out[:, :columns] = oth.astype(oth_out.dtype)
        if behind is not None:
            oth_out[:, columns:] = rest.pop(0)[...]
        own_out[...] = own

    ins = [(w, whole(w)) for w in shards]
    ins += [(act, block((tokens, rows), plan[f"mine{j}"])) for j in turns]
    ins += [p.operand() for p in pieces]
    if kept is not None:
        ins += [(k, whole(k)) for k in kept]
    if behind is not None:
        ins.append(behind.operand())
    own = struct((tokens, columns), jnp.float32)
    oth = struct((tokens, columns + extra), jnp.float32 if behind is None else jnp.bfloat16)
    return call(
        kernel,
        row,
        ins,
        [(own, whole(own)), (oth, whole(oth))],
        scratch=[pltpu.VMEM((tokens, rows), jnp.bfloat16)],
        vmem=28,
    )


def place(plan, row, xg, arrived, first, sums=None):
    count = len(arrived)
    tokens, width = arrived[0].shape
    table = [plan[f"theirs{first + j}"] for j in range(count)]

    def kernel(row_ref, *refs):
        g = pl.program_id(0)
        out_ref = refs[-1] if sums is None else refs[-2]
        for j in range(count):

            @pl.when(g == j)
            def _():
                out_ref[...] = refs[j][...]

        if sums is not None:
            total = refs[count][...] + refs[count + 1][...].astype(jnp.float32)
            refs[-1][...] = total.astype(jnp.bfloat16)

    def column(g, row):
        at = row[table[0]]
        for j in range(1, count):
            at = jnp.where(g == j, row[table[j]], at)
        return (0, at)

    ins = [view.operand() for view in arrived]
    outs = [(struct(xg.shape, xg.dtype), pl.BlockSpec((tokens, width), column))]
    if sums is not None:
        own, other = sums
        kv_block = pl.BlockSpec((tokens // count, own.shape[1]), lambda g, row: (g, 0))
        assert other.start == 0
        ins += [(own, kv_block), (other.array, kv_block)]
        outs.append((struct(own.shape, jnp.bfloat16), kv_block))
    aliases = {1 + len(ins): 0}
    return call(
        kernel,
        row,
        ins + [(xg, HBM)],
        outs,
        grid=(count,),
        aliases=aliases,
    )


def adam(row, h, got, grad, weights, first, second, kept, after=()):
    rows, columns = got["a"].shape
    assert got["a"].start == 0
    steps = 4 if rows % 64 == 0 else 1
    size = rows // steps

    def kernel(row_ref, up_ref, dn_ref, grad_ref, w_ref, a_ref, b_ref, *refs):
        a_out, b_out, stepped = refs[-3:]
        gradient = grad_ref[...] + up_ref[...].astype(jnp.float32) + dn_ref[...].astype(jnp.float32)
        moment_a = beta_one * a_ref[...] + (1.0 - beta_one) * gradient
        moment_b = beta_two * b_ref[...] + (1.0 - beta_two) * gradient * gradient
        old = w_ref[...].astype(jnp.float32)
        update = moment_a / corr_one / (jnp.sqrt(moment_b / corr_two) + adam_eps) + weight_decay * old
        a_out[...] = moment_a
        b_out[...] = moment_b
        stepped[...] = (old - learn_rate * update).astype(jnp.bfloat16)

    local = pl.BlockSpec((size, columns), lambda g, row: (g, 0))
    part = pl.BlockSpec((size, columns), lambda g, row: (g, h))
    ins = [(got["a"].array, local), (got["b"].array, local)]
    ins += [(a, part) for a in (grad, weights, first, second)]
    aliases = {}
    if kept is not None:
        aliases = {1 + len(ins): 0, 2 + len(ins): 1}
        ins += [(a, HBM) for a in kept]
    ins += [(a, ANY) for a in after]
    return call(
        kernel,
        row,
        ins,
        [
            (struct(first.shape, jnp.float32), part),
            (struct(second.shape, jnp.float32), part),
            (struct((rows, columns), jnp.bfloat16), local),
        ],
        grid=(steps,),
        aliases=aliases,
    )


def average(plan, scalars, h, stepped, others, kept, width, after=()):
    rows, columns = stepped.shape
    steps = 2 if rows % 32 == 0 else 1
    size = rows // steps
    count = len(others)

    def kernel(row_ref, numerator_ref, partner_ref, stepped_ref, *refs):
        mix = numerator_ref[row_ref[plan["replica"]]].astype(jnp.float32) / mix_denom
        for j in range(count):

            @pl.when((partner_ref[0] == j + 1) | (count == 1))
            def _():
                refs[-1][...] = (
                    (1.0 - mix) * stepped_ref[...].astype(jnp.float32)
                    + mix * refs[j][...].astype(jnp.float32)
                ).astype(jnp.bfloat16)

    local = pl.BlockSpec((size, columns), lambda g, *scalars: (g, 0))
    part = pl.BlockSpec((size, columns), lambda g, *scalars: (g, h))
    ins = [(a, local) for a in (stepped, *others)]
    if kept is not None:
        ins.append((kept, HBM))
    ins += [(a, ANY) for a in after]
    return call(
        kernel,
        scalars,
        ins,
        [(struct((rows, width), jnp.bfloat16), part)],
        grid=(steps,),
        aliases={} if kept is None else {count + 4: 0},
    )[0]


def partner_rows(stepped, partner, replica, n_rep):
    if n_rep != 4:
        gathered = lax.all_gather(stepped, "rep", axis=0, tiled=False)
        return [lax.dynamic_index_in_dim(gathered, partner[replica], 0, keepdims=False)]
    far = lax.ppermute(stepped, "rep", [(r, r ^ 2) for r in range(4)])
    core = [(r, r ^ 1) for r in range(4)]
    return [lax.ppermute(stepped, "rep", core), far, lax.ppermute(far, "rep", core)]


def per_device(
    n_rep, n, activations, kv_weight, kv_cotangent, first_moment, second_moment, partner, mix_numerator
):
    act, weights, cot = activations[0], kv_weight[0], kv_cotangent[0]
    first, second = first_moment[0], second_moment[0]
    plan = Plan(n_rep, n)
    depth = plan.depth
    rows, columns = weights.shape
    size = columns // CHUNKS
    row = lax.dynamic_index_in_dim(
        jnp.asarray(plan.table), lax.axis_index(("rep", "fsdp")), 0, keepdims=False
    )
    links = {
        "a": [(i, i + 2 if i // 2 % 2 == 0 else i - 2) for i in range(n)],
        "b": [(i, i - 2 if i // 2 % 2 == 0 else i + 2) for i in range(n)],
    }
    links = {name: [p for p in pairs if 0 <= p[1] < n] for name, pairs in links.items()}
    swap = functools.partial(lax.ppermute, axis_name="fsdp", perm=[(i, i ^ 1) for i in range(n)])

    def exchange(bufs):
        return {name: lax.ppermute(bufs[name], "fsdp", links[name]) for name in links}

    def part(array, h):
        return View(array, h * size, size)

    opening = exchange({"a": weights, "b": weights})
    got = {(1, h): {link: part(opening[link], h) for link in links} for h in range(CHUNKS)}

    def arrivals(link, slot):
        if slot == 1:
            return [opening[link]]
        return [got[slot, h][link].array for h in range(CHUNKS)]

    def send(*turns, after=()):
        return swap(pack(plan, row, rows, [], act, turns, after))

    parcel = swap(cot)
    cot_oth = [part(parcel, h) for h in range(CHUNKS)]
    pieces = [View(send(0), 0, rows)]

    parcel = send(*range(1, depth - 1), after=[parcel, pieces[0].array])
    pieces += [View(parcel, k * rows, rows) for k in range(depth - 2)]

    arrived, shards, parts = [], [], []

    def shard_step(j, xg):
        candidates = [[weights]]
        if j > 0:
            candidates = [arrivals(*source) for source in plan.sources[j]]
        xg, parcel, shard = project(plan, row, j, candidates, act, cot, cot_oth, xg)
        shards.append(shard)
        parts.append(View(parcel, 0, rows))
        return xg

    def send_parts(views, turns, after):
        parcel = swap(pack(plan, row, rows, views, act, turns, after))
        arrived.extend(View(parcel, t * rows, rows) for t in range(len(views)))
        return parcel

    xg = shard_step(0, None)
    parcel = send_parts(parts, [depth - 1], [parcel])
    pieces.append(View(parcel, rows, rows))
    bufs = {}
    for s in range(2, depth + 1):
        if s == depth:
            for j in range(1, depth - 1):
                xg = shard_step(j, xg)
            send_parts(parts[1:], [], [parcel])
            grad = own_gradient(plan, row, act, pieces[depth - 1], cot, cot_oth)
            sums = values(plan, row, list(range(depth - 1)), shards, act, pieces, None)
        for h in range(CHUNKS):
            after = list(bufs.values())[:1]
            if s == depth:
                after.append(grad if h == 0 else sums[0])
            bufs = relay(
                plan, row, s, got[s - 1, h], act, pieces[: s - 1], part(cot, h), cot_oth[h], after
            )
            got[s, h] = {link: part(array, 0) for link, array in exchange(bufs).items()}
    xg = shard_step(depth - 1, xg)
    kv_own, parcel = values(plan, row, [depth - 1], shards[-1:], act, pieces, sums, parts[-1])
    final = swap(parcel)

    scalars = (row, mix_numerator, partner)
    moments, averaged, placed = None, None, None
    for h in range(CHUNKS):
        last = h == CHUNKS - 1
        after = [] if h == 0 else [placed]
        *moments, stepped = adam(
            row, h, got[depth, h], grad, weights, first, second, moments, after + [parcel]
        )
        if placed is None:
            placed = place(plan, row, xg, arrived, 0)[0]
        others = partner_rows(stepped, partner, row[plan["replica"]], n_rep)
        if last:
            views = [View(final, columns, rows)]
            kv_views = (kv_own, View(final, 0, columns))
            x_grad, kv_out = place(plan, row, placed, views, depth - 1, kv_views)
        averaged = average(
            plan, scalars, h, stepped, others, averaged, columns, [kv_out] if last else [final]
        )
    return (
        kv_out[None],
        x_grad[None],
        averaged[None],
        moments[0][None],
        moments[1][None],
    )


def solution(mesh):
    placed = P("rep", "fsdp", None)
    return jax.shard_map(
        functools.partial(per_device, mesh.shape["rep"], mesh.shape["fsdp"]),
        mesh=mesh,
        in_specs=(placed,) * 5 + (P(), P()),
        out_specs=(placed,) * 5,
        check_vma=False,
    )
```

```python
import functools

import jax
import jax.numpy as jnp
import numpy as np
from jax import lax
from jax.experimental import pallas as pl
from jax.experimental.pallas import tpu as pltpu
from jax.sharding import PartitionSpec as P

beta_one = 0.9
beta_two = 0.999
learn_rate = 0.02
weight_decay = 0.1
adam_eps = 1e-08
corr_one = 1.0 - beta_one**10
corr_two = 1.0 - beta_two**10
mix_denom = 64.0

CHUNKS = 2
MIB = 1 << 20
ANY = pl.BlockSpec(memory_space=pl.ANY)
HBM = pl.BlockSpec(memory_space=pltpu.HBM)

TN = (((0,), (0,)), ((), ()))
NT = (((1,), (1,)), ((), ()))


def dot(a, b, dims=(((1,), (0,)), ((), ()))):
    return lax.dot_general(a, b, dims, preferred_element_type=jnp.float32)


class Plan:
    def __init__(self, n_rep, n):
        self.depth = depth = n // 2
        self.columns = {}
        self.rows = [[] for _ in range(n_rep * n)]
        order = [
            sorted(range(depth), key=lambda q: (-abs(q - z), (q < z) != (2 * z >= depth)))
            for z in range(depth)
        ]
        self.sources = [set() for _ in range(depth)]
        arrivals = []
        for z in range(depth):
            below, above = ("b", "a") if z % 2 == 0 else ("a", "b")
            ups = [(z - t, (below, t)) for t in range(1, z + 1)]
            downs = [(z + t, (above, t)) for t in range(1, depth - z)]
            arrivals.append(downs + ups if 2 * z < depth else ups + downs)
            for j, (_, source) in enumerate(arrivals[z], 1):
                self.sources[j].add(source)
        self.sources = [sorted(s) for s in self.sources]
        for device in range(n_rep * n):
            replica, i = divmod(device, n)
            z, x = divmod(i, 2)
            put = functools.partial(self._put, device)
            put("replica", replica)
            put("own", i)
            for k in range(depth):
                put(f"pack{k}", 2 * order[z][k] + 1 - x)
            for s in range(2, depth + 1):
                up, down = z + 1 + depth - s, z - 1 - depth + s
                for link, q in zip("ab", (up, down) if z % 2 == 0 else (down, up)):
                    add = 0 <= q < depth
                    put(f"add_{link}{s}", int(add))
                    put(f"blk_{link}{s}", 2 * q + x if add else 0)
                    put(f"pos_{link}{s}", order[z].index(q) if add else 0)
            for j in range(depth):
                q, source = (z, None) if j == 0 else arrivals[z][j - 1]
                put(f"mine{j}", 2 * q + x)
                put(f"theirs{j}", 2 * q + 1 - x)
                put(f"piece{j}", order[z].index(q))
                put(f"source{j}", 0 if j == 0 else self.sources[j].index(source))
        self.table = np.asarray(self.rows, np.int32)

    def _put(self, i, name, value):
        column = self.columns.setdefault(name, len(self.columns))
        assert column == len(self.rows[i])
        self.rows[i].append(value)

    def __getitem__(self, name):
        return self.columns[name]


def call(kernel, row, ins, outs, grid=(1,), aliases=None, scratch=(), vmem=16):
    scalars = row if isinstance(row, tuple) else (row,)
    return pl.pallas_call(
        kernel,
        grid_spec=pltpu.PrefetchScalarGridSpec(
            num_scalar_prefetch=len(scalars),
            grid=grid,
            in_specs=[spec for _, spec in ins],
            out_specs=[spec for _, spec in outs],
            scratch_shapes=list(scratch),
        ),
        out_shape=[shape for shape, _ in outs],
        input_output_aliases=aliases or {},
        compiler_params=pltpu.CompilerParams(vmem_limit_bytes=vmem * MIB),
        cost_estimate=pl.CostEstimate(flops=0, bytes_accessed=0, transcendentals=0),
    )(*scalars, *[array for array, _ in ins])


def whole(array):
    rank = array.ndim
    return pl.BlockSpec(array.shape, lambda g, row: (0,) * rank)


def block(shape, column, scale=1, offset=0):
    return pl.BlockSpec(shape, lambda g, row: (0, row[column] * scale + offset))


def struct(shape, dtype):
    return jax.ShapeDtypeStruct(shape, dtype)


class View:
    def __init__(self, array, start, count):
        assert start % count == 0
        self.array, self.start, self.count = array, start, count
        self.shape = (array.shape[0], count)

    def operand(self):
        at = self.start // self.count
        return self.array, pl.BlockSpec(self.shape, lambda g, row: (0, at))


def pack(plan, row, width, views, act=None, turns=(), after=()):
    count = len(views) + len(turns)
    ins = [v.operand() for v in views]
    tokens = views[0].shape[0] if views else act.shape[0]
    ins += [(act, block((tokens, width), plan[f"pack{k}"])) for k in turns]
    sizes = [v.count for v in views] + [width] * len(turns)

    def kernel(row_ref, *refs):
        at = 0
        for ref, size in zip(refs[:count], sizes):
            refs[-1][:, at : at + size] = ref[...]
            at += size

    out = struct((tokens, sum(sizes)), jnp.bfloat16)
    return call(
        kernel,
        row,
        ins + [(a, ANY) for a in after],
        [(out, whole(out))],
    )[0]


def relay(plan, row, s, got, act, pieces, cot_own, cot_oth, after=()):
    (tokens, columns), rows = cot_own.shape, got["a"].shape[0]
    count = len(pieces)

    def kernel(row_ref, *refs):
        got_refs, act_refs = refs[0:2], refs[2:4]
        piece_refs = refs[4 : 4 + count]
        own_ref, oth_ref = refs[4 + count : 6 + count]
        out_refs, held = refs[-3:-1], refs[-1]
        for d, link in enumerate("ab"):
            add = row_ref[plan[f"add_{link}{s}"]]
            pos = row_ref[plan[f"pos_{link}{s}"]]

            @pl.when(add == 0)
            def _():
                out_refs[d][...] = got_refs[d][...]

            @pl.when(add == 1)
            def _():
                for j in range(count):

                    @pl.when(pos == j)
                    def _():
                        held[...] = piece_refs[j][...]

                total = dot(act_refs[d][...], own_ref[...], TN)
                total = total + dot(held[...], oth_ref[...], TN)
                out_refs[d][...] = (total + got_refs[d][...].astype(jnp.float32)).astype(jnp.bfloat16)

    ins = [got[link].operand() for link in "ba"]
    ins += [(act, block((tokens, rows), plan[f"blk_{link}{s}"])) for link in "ab"]
    ins += [view.operand() for view in (*pieces, cot_own, cot_oth)]
    ins += [(a, ANY) for a in after]
    out = struct((rows, columns), jnp.bfloat16)
    a, b = call(
        kernel,
        row,
        ins,
        [(out, whole(out)), (out, whole(out))],
        scratch=[pltpu.VMEM((tokens, rows), jnp.bfloat16)],
    )
    return {"a": a, "b": b}


def own_gradient(plan, row, act, piece, cot, cot_oth):
    tokens, columns = cot.shape
    rows = piece.shape[1]

    def kernel(row_ref, act_ref, piece_ref, own_ref, *refs):
        out_ref = refs[-1]
        at = 0
        for ref, view in zip(refs, cot_oth):
            part = slice(at, at + view.count)
            total = dot(act_ref[...], own_ref[:, part], TN)
            out_ref[:, part] = total + dot(piece_ref[...], ref[...], TN)
            at += view.count

    out = struct((rows, columns), jnp.float32)
    return call(
        kernel,
        row,
        [(act, block((tokens, rows), plan["own"])), piece.operand(), (cot, whole(cot))]
        + [view.operand() for view in cot_oth],
        [(out, whole(out))],
    )[0]


def project(plan, row, j, candidates, act, cot, cot_oth, xg_before):
    (tokens, columns), rows = cot.shape, candidates[0][0].shape[0]
    flat = [c for candidate in candidates for c in candidate]
    starts = np.cumsum([0] + [len(candidate) for candidate in candidates])
    parts = max(len(candidate) for candidate in candidates)
    n_w, n_c = len(flat), len(cot_oth)

    def kernel(row_ref, *refs):
        w_refs, cot_refs = refs[:n_w], refs[n_w : n_w + n_c]
        own_ref = refs[n_w + n_c]
        xg_own, xg_oth, w_out, sems = refs[-4:]
        for c in range(len(candidates)):

            @pl.when(row_ref[plan[f"source{j}"]] == c)
            def _():
                copies, at = [], 0
                for p in range(starts[c], starts[c + 1]):
                    to = w_out.at[:, pl.ds(at, flat[p].shape[1])]
                    copies.append(pltpu.make_async_copy(w_refs[p], to, sems.at[len(copies)]))
                    at += flat[p].shape[1]
                for copy in copies:
                    copy.start()
                for copy in copies:
                    copy.wait()

        total, at = 0.0, 0
        for ref, view in zip(cot_refs, cot_oth):
            total = total + dot(ref[...], w_out[:, at : at + view.count], NT)
            at += view.count
        xg_oth[...] = total.astype(jnp.bfloat16)
        xg_own[...] = dot(own_ref[...], w_out[...], NT).astype(jnp.bfloat16)

    ins = [(w, ANY) for w in flat] + [view.operand() for view in cot_oth] + [(cot, whole(cot))]
    aliases = {}
    if xg_before is not None:
        aliases = {1 + len(ins): 0}
        ins.append((xg_before, HBM))
    other = struct((tokens, rows), jnp.bfloat16)
    shard = struct((rows, columns), jnp.bfloat16)
    return call(
        kernel,
        row,
        ins,
        [
            (struct(act.shape, jnp.bfloat16), block((tokens, rows), plan[f"mine{j}"])),
            (other, whole(other)),
            (shard, whole(shard)),
        ],
        aliases=aliases,
        scratch=[pltpu.SemaphoreType.DMA((parts,))],
        vmem=20,
    )


def values(plan, row, turns, shards, act, pieces, kept, behind=None):
    rows, columns = shards[0].shape
    tokens = act.shape[0]
    count, n_p = len(turns), len(pieces)
    extra = 0 if behind is None else behind.count

    def kernel(row_ref, *refs):
        w_refs, act_refs = refs[:count], refs[count : 2 * count]
        piece_refs = refs[2 * count : 2 * count + n_p]
        rest = list(refs[2 * count + n_p : -3])
        own_out, oth_out, held = refs[-3:]
        own = oth = 0.0
        if kept is not None:
            own, oth = rest.pop(0)[...], rest.pop(0)[...]
        for t, j in enumerate(turns):
            for p in range(n_p):

                @pl.when(row_ref[plan[f"piece{j}"]] == p)
                def _():
                    held[...] = piece_refs[p][...]

            oth = oth + dot(held[...], w_refs[t][...])
            own = own + dot(act_refs[t][...], w_refs[t][...])
        oth_out[:, :columns] = oth.astype(oth_out.dtype)
        if behind is not None:
            oth_out[:, columns:] = rest.pop(0)[...]
        own_out[...] = own

    ins = [(w, whole(w)) for w in shards]
    ins += [(act, block((tokens, rows), plan[f"mine{j}"])) for j in turns]
    ins += [p.operand() for p in pieces]
    if kept is not None:
        ins += [(k, whole(k)) for k in kept]
    if behind is not None:
        ins.append(behind.operand())
    own = struct((tokens, columns), jnp.float32)
    oth = struct((tokens, columns + extra), jnp.float32 if behind is None else jnp.bfloat16)
    return call(
        kernel,
        row,
        ins,
        [(own, whole(own)), (oth, whole(oth))],
        scratch=[pltpu.VMEM((tokens, rows), jnp.bfloat16)],
        vmem=28,
    )


def place(plan, row, xg, arrived, first, sums=None, after=()):
    count = len(arrived)
    tokens, width = arrived[0].shape
    table = [plan[f"theirs{first + j}"] for j in range(count)]

    def kernel(row_ref, *refs):
        g = pl.program_id(0)
        out_ref = refs[-2]
        for j in range(count):

            @pl.when(g == j)
            def _():
                out_ref[...] = refs[j][...]

        if sums is None:
            refs[-1][...] = jnp.zeros_like(refs[-1])
        else:
            total = refs[count][...] + refs[count + 1][...].astype(jnp.float32)
            refs[-1][...] = total.astype(jnp.bfloat16)

    def column(g, row):
        at = row[table[0]]
        for j in range(1, count):
            at = jnp.where(g == j, row[table[j]], at)
        return (0, at)

    ins = [view.operand() for view in arrived]
    outs = [(struct(xg.shape, xg.dtype), pl.BlockSpec((tokens, width), column))]
    if sums is None:
        tile = struct((8, 128), jnp.float32)
        outs.append((tile, whole(tile)))
    else:
        own, other = sums
        kv_block = pl.BlockSpec((tokens // count, own.shape[1]), lambda g, row: (g, 0))
        assert other.start == 0
        ins += [(own, kv_block), (other.array, kv_block)]
        outs.append((struct(own.shape, jnp.bfloat16), kv_block))
    aliases = {1 + len(ins): 0}
    return call(
        kernel,
        row,
        ins + [(xg, HBM)] + [(a, ANY) for a in after],
        outs,
        grid=(count,),
        aliases=aliases,
    )


def adam(row, h, got, grad, weights, first, second, kept, after=()):
    rows, columns = got["a"].shape
    assert got["a"].start == 0
    steps = 4 if rows % 64 == 0 else 1
    size = rows // steps

    def kernel(row_ref, up_ref, dn_ref, grad_ref, w_ref, a_ref, b_ref, *refs):
        a_out, b_out, stepped = refs[-3:]
        gradient = grad_ref[...] + up_ref[...].astype(jnp.float32) + dn_ref[...].astype(jnp.float32)
        moment_a = beta_one * a_ref[...] + (1.0 - beta_one) * gradient
        moment_b = beta_two * b_ref[...] + (1.0 - beta_two) * gradient * gradient
        old = w_ref[...].astype(jnp.float32)
        update = moment_a / corr_one / (jnp.sqrt(moment_b / corr_two) + adam_eps) + weight_decay * old
        a_out[...] = moment_a
        b_out[...] = moment_b
        stepped[...] = (old - learn_rate * update).astype(jnp.bfloat16)

    local = pl.BlockSpec((size, columns), lambda g, row: (g, 0))
    part = pl.BlockSpec((size, columns), lambda g, row: (g, h))
    ins = [(got["a"].array, local), (got["b"].array, local)]
    ins += [(a, part) for a in (grad, weights, first, second)]
    aliases = {}
    if kept is not None:
        aliases = {1 + len(ins): 0, 2 + len(ins): 1}
        ins += [(a, HBM) for a in kept]
    ins += after
    return call(
        kernel,
        row,
        ins,
        [
            (struct(first.shape, jnp.float32), part),
            (struct(second.shape, jnp.float32), part),
            (struct((rows, columns), jnp.bfloat16), local),
        ],
        grid=(steps,),
        aliases=aliases,
    )


def average(plan, scalars, h, stepped, others, kept, width, after=()):
    rows, columns = stepped.shape
    steps = 2 if rows % 32 == 0 else 1
    size = rows // steps
    count = len(others)

    def kernel(row_ref, numerator_ref, partner_ref, stepped_ref, *refs):
        mix = numerator_ref[row_ref[plan["replica"]]].astype(jnp.float32) / mix_denom
        for j in range(count):

            @pl.when((partner_ref[0] == j + 1) | (count == 1))
            def _():
                refs[-2][...] = (
                    (1.0 - mix) * stepped_ref[...].astype(jnp.float32)
                    + mix * refs[j][...].astype(jnp.float32)
                ).astype(jnp.bfloat16)

        refs[-1][...] = jnp.zeros_like(refs[-1])

    tile = struct((8, 128), jnp.float32)
    local = pl.BlockSpec((size, columns), lambda g, *scalars: (g, 0))
    part = pl.BlockSpec((size, columns), lambda g, *scalars: (g, h))
    ins = [(a, local) for a in (stepped, *others)]
    if kept is not None:
        ins.append((kept, HBM))
    ins += [(a, ANY) for a in after]
    return call(
        kernel,
        scalars,
        ins,
        [
            (struct((rows, width), jnp.bfloat16), part),
            (tile, pl.BlockSpec(tile.shape, lambda g, *scalars: (0, 0))),
        ],
        grid=(steps,),
        aliases={} if kept is None else {count + 4: 0},
    )


def partner_rows(stepped, partner, replica, n_rep):
    if n_rep != 4:
        gathered = lax.all_gather(stepped, "rep", axis=0, tiled=False)
        return [lax.dynamic_index_in_dim(gathered, partner[replica], 0, keepdims=False)]
    far = lax.ppermute(stepped, "rep", [(r, r ^ 2) for r in range(4)])
    core = [(r, r ^ 1) for r in range(4)]
    return [lax.ppermute(stepped, "rep", core), far, lax.ppermute(far, "rep", core)]


def per_device(
    n_rep, n, activations, kv_weight, kv_cotangent, first_moment, second_moment, partner, mix_numerator
):
    act, weights, cot = activations[0], kv_weight[0], kv_cotangent[0]
    first, second = first_moment[0], second_moment[0]
    plan = Plan(n_rep, n)
    depth = plan.depth
    rows, columns = weights.shape
    size = columns // CHUNKS
    row = lax.dynamic_index_in_dim(
        jnp.asarray(plan.table), lax.axis_index(("rep", "fsdp")), 0, keepdims=False
    )
    links = {
        "a": [(i, i + 2 if i // 2 % 2 == 0 else i - 2) for i in range(n)],
        "b": [(i, i - 2 if i // 2 % 2 == 0 else i + 2) for i in range(n)],
    }
    links = {name: [p for p in pairs if 0 <= p[1] < n] for name, pairs in links.items()}
    swap = functools.partial(lax.ppermute, axis_name="fsdp", perm=[(i, i ^ 1) for i in range(n)])

    def exchange(bufs):
        return {name: lax.ppermute(bufs[name], "fsdp", links[name]) for name in links}

    def part(array, h):
        return View(array, h * size, size)

    opening = exchange({"a": weights, "b": weights})
    got = {(1, h): {link: part(opening[link], h) for link in links} for h in range(CHUNKS)}

    def arrivals(link, slot):
        if slot == 1:
            return [opening[link]]
        return [got[slot, h][link].array for h in range(CHUNKS)]

    def send(*turns, after=()):
        return swap(pack(plan, row, rows, [], act, turns, after))

    parcel = swap(cot)
    cot_oth = [part(parcel, h) for h in range(CHUNKS)]
    pieces = [View(send(0), 0, rows)]

    parcel = send(*range(1, depth - 1), after=[parcel, pieces[0].array])
    pieces += [View(parcel, k * rows, rows) for k in range(depth - 2)]

    arrived, shards, parts = [], [], []

    def shard_step(j, xg):
        candidates = [[weights]]
        if j > 0:
            candidates = [arrivals(*source) for source in plan.sources[j]]
        xg, parcel, shard = project(plan, row, j, candidates, act, cot, cot_oth, xg)
        shards.append(shard)
        parts.append(View(parcel, 0, rows))
        return xg

    def send_parts(views, turns, after):
        parcel = swap(pack(plan, row, rows, views, act, turns, after))
        arrived.extend(View(parcel, t * rows, rows) for t in range(len(views)))
        return parcel

    xg = shard_step(0, None)
    parcel = send_parts(parts, [depth - 1], [parcel])
    pieces.append(View(parcel, rows, rows))
    bufs = {}
    for s in range(2, depth + 1):
        if s == depth:
            for j in range(2, depth - 1):
                xg = shard_step(j, xg)
            send_parts(parts[1:], [], [parcel])
            grad = own_gradient(plan, row, act, pieces[depth - 1], cot, cot_oth)
            sums = values(plan, row, list(range(depth - 1)), shards, act, pieces, None)
        for h in range(CHUNKS):
            after = list(bufs.values())[:1]
            if s == 3 and h == 0:
                xg = shard_step(1, xg)
                after.append(parts[1].array)
            if s == depth and h == CHUNKS - 1:
                after.append(sums[0])
            bufs = relay(
                plan, row, s, got[s - 1, h], act, pieces[: s - 1], part(cot, h), cot_oth[h], after
            )
            got[s, h] = {link: part(array, 0) for link, array in exchange(bufs).items()}
    xg = shard_step(depth - 1, xg)
    kv_own, parcel = values(plan, row, [depth - 1], shards[-1:], act, pieces, sums, parts[-1])
    final = swap(parcel)

    scalars = (row, mix_numerator, partner)
    moments, averaged, placed = None, None, None
    for h in range(CHUNKS):
        last = h == CHUNKS - 1
        after = [] if h == 0 else [(tile, ANY)]
        *moments, stepped = adam(
            row, h, got[depth, h], grad, weights, first, second, moments, after + [(parcel, ANY)]
        )
        if placed is None:
            placed, tile = place(plan, row, xg, arrived, 0)
        others = partner_rows(stepped, partner, row[plan["replica"]], n_rep)
        if last:
            views = [View(final, columns, rows)]
            kv_views = (kv_own, View(final, 0, columns))
            x_grad, kv_out = place(plan, row, placed, views, depth - 1, kv_views, [tile])
        averaged, tile = average(
            plan, scalars, h, stepped, others, averaged, columns, [kv_out] if last else []
        )
    return (
        kv_out[None],
        x_grad[None],
        averaged[None],
        moments[0][None],
        moments[1][None],
    )


def solution(mesh):
    placed = P("rep", "fsdp", None)
    return jax.shard_map(
        functools.partial(per_device, mesh.shape["rep"], mesh.shape["fsdp"]),
        mesh=mesh,
        in_specs=(placed,) * 5 + (P(), P()),
        out_specs=(placed,) * 5,
        check_vma=False,
    )
```

```python
import functools

import jax
import jax.numpy as jnp
import numpy as np
from jax import lax
from jax.experimental import pallas as pl
from jax.experimental.pallas import tpu as pltpu
from jax.sharding import PartitionSpec as P

beta_one = 0.9
beta_two = 0.999
learn_rate = 0.02
weight_decay = 0.1
adam_eps = 1e-08
corr_one = 1.0 - beta_one**10
corr_two = 1.0 - beta_two**10
mix_denom = 64.0

CHUNKS = 2
MIB = 1 << 20
ANY = pl.BlockSpec(memory_space=pl.ANY)
HBM = pl.BlockSpec(memory_space=pltpu.HBM)

TN = (((0,), (0,)), ((), ()))
NT = (((1,), (1,)), ((), ()))


def dot(a, b, dims=(((1,), (0,)), ((), ()))):
    return lax.dot_general(a, b, dims, preferred_element_type=jnp.float32)


class Plan:
    def __init__(self, n_rep, n):
        self.depth = depth = n // 2
        self.columns = {}
        self.rows = [[] for _ in range(n_rep * n)]
        order = [
            sorted(range(depth), key=lambda q: (-abs(q - z), (q < z) != (2 * z >= depth)))
            for z in range(depth)
        ]
        self.sources = [set() for _ in range(depth)]
        arrivals = []
        for z in range(depth):
            below, above = ("b", "a") if z % 2 == 0 else ("a", "b")
            ups = [(z - t, (below, t)) for t in range(1, z + 1)]
            downs = [(z + t, (above, t)) for t in range(1, depth - z)]
            arrivals.append(downs + ups if 2 * z < depth else ups + downs)
            for j, (_, source) in enumerate(arrivals[z], 1):
                self.sources[j].add(source)
        self.sources = [sorted(s) for s in self.sources]
        for device in range(n_rep * n):
            replica, i = divmod(device, n)
            z, x = divmod(i, 2)
            put = functools.partial(self._put, device)
            put("replica", replica)
            put("own", i)
            for k in range(depth):
                put(f"pack{k}", 2 * order[z][k] + 1 - x)
            for s in range(2, depth + 1):
                up, down = z + 1 + depth - s, z - 1 - depth + s
                for link, q in zip("ab", (up, down) if z % 2 == 0 else (down, up)):
                    add = 0 <= q < depth
                    put(f"add_{link}{s}", int(add))
                    put(f"blk_{link}{s}", 2 * q + x if add else 0)
                    put(f"pos_{link}{s}", order[z].index(q) if add else 0)
            for j in range(depth):
                q, source = (z, None) if j == 0 else arrivals[z][j - 1]
                put(f"mine{j}", 2 * q + x)
                put(f"theirs{j}", 2 * q + 1 - x)
                put(f"piece{j}", order[z].index(q))
                put(f"source{j}", 0 if j == 0 else self.sources[j].index(source))
        self.table = np.asarray(self.rows, np.int32)

    def _put(self, i, name, value):
        column = self.columns.setdefault(name, len(self.columns))
        assert column == len(self.rows[i])
        self.rows[i].append(value)

    def __getitem__(self, name):
        return self.columns[name]


def call(kernel, row, ins, outs, grid=(1,), aliases=None, scratch=(), vmem=16):
    scalars = row if isinstance(row, tuple) else (row,)
    return pl.pallas_call(
        kernel,
        grid_spec=pltpu.PrefetchScalarGridSpec(
            num_scalar_prefetch=len(scalars),
            grid=grid,
            in_specs=[spec for _, spec in ins],
            out_specs=[spec for _, spec in outs],
            scratch_shapes=list(scratch),
        ),
        out_shape=[shape for shape, _ in outs],
        input_output_aliases=aliases or {},
        compiler_params=pltpu.CompilerParams(vmem_limit_bytes=vmem * MIB),
        cost_estimate=pl.CostEstimate(flops=0, bytes_accessed=0, transcendentals=0),
    )(*scalars, *[array for array, _ in ins])


def whole(array):
    rank = array.ndim
    return pl.BlockSpec(array.shape, lambda g, row: (0,) * rank)


def block(shape, column, scale=1, offset=0):
    return pl.BlockSpec(shape, lambda g, row: (0, row[column] * scale + offset))


def struct(shape, dtype):
    return jax.ShapeDtypeStruct(shape, dtype)


class View:
    def __init__(self, array, start, count):
        assert start % count == 0
        self.array, self.start, self.count = array, start, count
        self.shape = (array.shape[0], count)

    def operand(self):
        at = self.start // self.count
        return self.array, pl.BlockSpec(self.shape, lambda g, row: (0, at))


def pack(plan, row, width, views, act=None, turns=(), after=()):
    count = len(views) + len(turns)
    ins = [v.operand() for v in views]
    tokens = views[0].shape[0] if views else act.shape[0]
    ins += [(act, block((tokens, width), plan[f"pack{k}"])) for k in turns]
    sizes = [v.count for v in views] + [width] * len(turns)

    def kernel(row_ref, *refs):
        at = 0
        for ref, size in zip(refs[:count], sizes):
            refs[-1][:, at : at + size] = ref[...]
            at += size

    out = struct((tokens, sum(sizes)), jnp.bfloat16)
    return call(
        kernel,
        row,
        ins + [(a, ANY) for a in after],
        [(out, whole(out))],
    )[0]


def relay(plan, row, s, got, act, pieces, cot_own, cot_oth, after=()):
    (tokens, columns), rows = cot_own.shape, got["a"].shape[0]
    count = len(pieces)

    def kernel(row_ref, *refs):
        got_refs, act_refs = refs[0:2], refs[2:4]
        piece_refs = refs[4 : 4 + count]
        own_ref, oth_ref = refs[4 + count : 6 + count]
        out_refs, held = refs[-3:-1], refs[-1]
        for d, link in enumerate("ab"):
            add = row_ref[plan[f"add_{link}{s}"]]
            pos = row_ref[plan[f"pos_{link}{s}"]]

            @pl.when(add == 0)
            def _():
                out_refs[d][...] = got_refs[d][...]

            @pl.when(add == 1)
            def _():
                for j in range(count):

                    @pl.when(pos == j)
                    def _():
                        held[...] = piece_refs[j][...]

                total = dot(act_refs[d][...], own_ref[...], TN)
                total = total + dot(held[...], oth_ref[...], TN)
                out_refs[d][...] = (total + got_refs[d][...].astype(jnp.float32)).astype(jnp.bfloat16)

    ins = [got[link].operand() for link in "ba"]
    ins += [(act, block((tokens, rows), plan[f"blk_{link}{s}"])) for link in "ab"]
    ins += [view.operand() for view in (*pieces, cot_own, cot_oth)]
    ins += [(a, ANY) for a in after]
    out = struct((rows, columns), jnp.bfloat16)
    a, b = call(
        kernel,
        row,
        ins,
        [(out, whole(out)), (out, whole(out))],
        scratch=[pltpu.VMEM((tokens, rows), jnp.bfloat16)],
    )
    return {"a": a, "b": b}


def own_gradient(plan, row, act, piece, cot, cot_oth):
    tokens, columns = cot.shape
    rows = piece.shape[1]

    def kernel(row_ref, act_ref, piece_ref, own_ref, *refs):
        out_ref = refs[-1]
        at = 0
        for ref, view in zip(refs, cot_oth):
            part = slice(at, at + view.count)
            total = dot(act_ref[...], own_ref[:, part], TN)
            out_ref[:, part] = total + dot(piece_ref[...], ref[...], TN)
            at += view.count

    out = struct((rows, columns), jnp.float32)
    return call(
        kernel,
        row,
        [(act, block((tokens, rows), plan["own"])), piece.operand(), (cot, whole(cot))]
        + [view.operand() for view in cot_oth],
        [(out, whole(out))],
    )[0]


def project(plan, row, j, candidates, act, cot, cot_oth, xg_before):
    (tokens, columns), rows = cot.shape, candidates[0][0].shape[0]
    flat = [c for candidate in candidates for c in candidate]
    starts = np.cumsum([0] + [len(candidate) for candidate in candidates])
    parts = max(len(candidate) for candidate in candidates)
    n_w, n_c = len(flat), len(cot_oth)

    def kernel(row_ref, *refs):
        w_refs, cot_refs = refs[:n_w], refs[n_w : n_w + n_c]
        own_ref = refs[n_w + n_c]
        xg_own, xg_oth, w_out, sems = refs[-4:]
        for c in range(len(candidates)):

            @pl.when(row_ref[plan[f"source{j}"]] == c)
            def _():
                copies, at = [], 0
                for p in range(starts[c], starts[c + 1]):
                    to = w_out.at[:, pl.ds(at, flat[p].shape[1])]
                    copies.append(pltpu.make_async_copy(w_refs[p], to, sems.at[len(copies)]))
                    at += flat[p].shape[1]
                for copy in copies:
                    copy.start()
                for copy in copies:
                    copy.wait()

        total, at = 0.0, 0
        for ref, view in zip(cot_refs, cot_oth):
            total = total + dot(ref[...], w_out[:, at : at + view.count], NT)
            at += view.count
        xg_oth[...] = total.astype(jnp.bfloat16)
        xg_own[...] = dot(own_ref[...], w_out[...], NT).astype(jnp.bfloat16)

    ins = [(w, ANY) for w in flat] + [view.operand() for view in cot_oth] + [(cot, whole(cot))]
    aliases = {}
    if xg_before is not None:
        aliases = {1 + len(ins): 0}
        ins.append((xg_before, HBM))
    other = struct((tokens, rows), jnp.bfloat16)
    shard = struct((rows, columns), jnp.bfloat16)
    return call(
        kernel,
        row,
        ins,
        [
            (struct(act.shape, jnp.bfloat16), block((tokens, rows), plan[f"mine{j}"])),
            (other, whole(other)),
            (shard, whole(shard)),
        ],
        aliases=aliases,
        scratch=[pltpu.SemaphoreType.DMA((parts,))],
        vmem=20,
    )


def values(plan, row, turns, shards, act, pieces, kept, behind=None):
    rows, columns = shards[0].shape
    tokens = act.shape[0]
    count, n_p = len(turns), len(pieces)
    extra = 0 if behind is None else behind.count

    def kernel(row_ref, *refs):
        w_refs, act_refs = refs[:count], refs[count : 2 * count]
        piece_refs = refs[2 * count : 2 * count + n_p]
        rest = list(refs[2 * count + n_p : -3])
        own_out, oth_out, held = refs[-3:]
        own = oth = 0.0
        if kept is not None:
            own, oth = rest.pop(0)[...], rest.pop(0)[...]
        for t, j in enumerate(turns):
            for p in range(n_p):

                @pl.when(row_ref[plan[f"piece{j}"]] == p)
                def _():
                    held[...] = piece_refs[p][...]

            oth = oth + dot(held[...], w_refs[t][...])
            own = own + dot(act_refs[t][...], w_refs[t][...])
        oth_out[:, :columns] = oth.astype(oth_out.dtype)
        if behind is not None:
            oth_out[:, columns:] = rest.pop(0)[...]
        own_out[...] = own

    ins = [(w, whole(w)) for w in shards]
    ins += [(act, block((tokens, rows), plan[f"mine{j}"])) for j in turns]
    ins += [p.operand() for p in pieces]
    if kept is not None:
        ins += [(k, whole(k)) for k in kept]
    if behind is not None:
        ins.append(behind.operand())
    own = struct((tokens, columns), jnp.float32)
    oth = struct((tokens, columns + extra), jnp.float32 if behind is None else jnp.bfloat16)
    return call(
        kernel,
        row,
        ins,
        [(own, whole(own)), (oth, whole(oth))],
        scratch=[pltpu.VMEM((tokens, rows), jnp.bfloat16)],
        vmem=28,
    )


def place(plan, row, xg, arrived, first, sums=None, after=()):
    count = len(arrived)
    tokens, width = arrived[0].shape
    table = [plan[f"theirs{first + j}"] for j in range(count)]

    def kernel(row_ref, *refs):
        g = pl.program_id(0)
        out_ref = refs[-2]
        for j in range(count):

            @pl.when(g == j)
            def _():
                out_ref[...] = refs[j][...]

        if sums is None:
            refs[-1][...] = jnp.zeros_like(refs[-1])
        else:
            total = refs[count][...] + refs[count + 1][...].astype(jnp.float32)
            refs[-1][...] = total.astype(jnp.bfloat16)

    def column(g, row):
        at = row[table[0]]
        for j in range(1, count):
            at = jnp.where(g == j, row[table[j]], at)
        return (0, at)

    ins = [view.operand() for view in arrived]
    outs = [(struct(xg.shape, xg.dtype), pl.BlockSpec((tokens, width), column))]
    if sums is None:
        tile = struct((8, 128), jnp.float32)
        outs.append((tile, whole(tile)))
    else:
        own, other = sums
        kv_block = pl.BlockSpec((tokens // count, own.shape[1]), lambda g, row: (g, 0))
        assert other.start == 0
        ins += [(own, kv_block), (other.array, kv_block)]
        outs.append((struct(own.shape, jnp.bfloat16), kv_block))
    aliases = {1 + len(ins): 0}
    return call(
        kernel,
        row,
        ins + [(xg, HBM)] + [(a, ANY) for a in after],
        outs,
        grid=(count,),
        aliases=aliases,
    )


def adam(row, h, got, grad, weights, first, second, kept, after=()):
    rows, columns = got["a"].shape
    assert got["a"].start == 0
    steps = 4 if rows % 64 == 0 else 1
    size = rows // steps

    def kernel(row_ref, up_ref, dn_ref, grad_ref, w_ref, a_ref, b_ref, *refs):
        a_out, b_out, stepped = refs[-3:]
        gradient = grad_ref[...] + up_ref[...].astype(jnp.float32) + dn_ref[...].astype(jnp.float32)
        moment_a = beta_one * a_ref[...] + (1.0 - beta_one) * gradient
        moment_b = beta_two * b_ref[...] + (1.0 - beta_two) * gradient * gradient
        old = w_ref[...].astype(jnp.float32)
        update = moment_a / corr_one / (jnp.sqrt(moment_b / corr_two) + adam_eps) + weight_decay * old
        a_out[...] = moment_a
        b_out[...] = moment_b
        stepped[...] = (old - learn_rate * update).astype(jnp.bfloat16)

    local = pl.BlockSpec((size, columns), lambda g, row: (g, 0))
    part = pl.BlockSpec((size, columns), lambda g, row: (g, h))
    ins = [(got["a"].array, local), (got["b"].array, local)]
    ins += [(a, part) for a in (grad, weights, first, second)]
    aliases = {}
    if kept is not None:
        aliases = {1 + len(ins): 0, 2 + len(ins): 1}
        ins += [(a, HBM) for a in kept]
    ins += after
    return call(
        kernel,
        row,
        ins,
        [
            (struct(first.shape, jnp.float32), part),
            (struct(second.shape, jnp.float32), part),
            (struct((rows, columns), jnp.bfloat16), local),
        ],
        grid=(steps,),
        aliases=aliases,
    )


def average(plan, scalars, h, stepped, others, kept, width, after=()):
    rows, columns = stepped.shape
    steps = 2 if rows % 32 == 0 else 1
    size = rows // steps
    count = len(others)

    def kernel(row_ref, numerator_ref, partner_ref, stepped_ref, *refs):
        mix = numerator_ref[row_ref[plan["replica"]]].astype(jnp.float32) / mix_denom
        for j in range(count):

            @pl.when((partner_ref[0] == j + 1) | (count == 1))
            def _():
                refs[-2][...] = (
                    (1.0 - mix) * stepped_ref[...].astype(jnp.float32)
                    + mix * refs[j][...].astype(jnp.float32)
                ).astype(jnp.bfloat16)

        refs[-1][...] = jnp.zeros_like(refs[-1])

    tile = struct((8, 128), jnp.float32)
    local = pl.BlockSpec((size, columns), lambda g, *scalars: (g, 0))
    part = pl.BlockSpec((size, columns), lambda g, *scalars: (g, h))
    ins = [(a, local) for a in (stepped, *others)]
    if kept is not None:
        ins.append((kept, HBM))
    ins += [(a, ANY) for a in after]
    return call(
        kernel,
        scalars,
        ins,
        [
            (struct((rows, width), jnp.bfloat16), part),
            (tile, pl.BlockSpec(tile.shape, lambda g, *scalars: (0, 0))),
        ],
        grid=(steps,),
        aliases={} if kept is None else {count + 4: 0},
    )


def partner_rows(stepped, partner, replica, n_rep):
    if n_rep != 4:
        gathered = lax.all_gather(stepped, "rep", axis=0, tiled=False)
        return [lax.dynamic_index_in_dim(gathered, partner[replica], 0, keepdims=False)]
    far = lax.ppermute(stepped, "rep", [(r, r ^ 2) for r in range(4)])
    core = [(r, r ^ 1) for r in range(4)]
    return [lax.ppermute(stepped, "rep", core), far, lax.ppermute(far, "rep", core)]


def per_device(
    n_rep, n, activations, kv_weight, kv_cotangent, first_moment, second_moment, partner, mix_numerator
):
    act, weights, cot = activations[0], kv_weight[0], kv_cotangent[0]
    first, second = first_moment[0], second_moment[0]
    plan = Plan(n_rep, n)
    depth = plan.depth
    rows, columns = weights.shape
    size = columns // CHUNKS
    row = lax.dynamic_index_in_dim(
        jnp.asarray(plan.table), lax.axis_index(("rep", "fsdp")), 0, keepdims=False
    )
    links = {
        "a": [(i, i + 2 if i // 2 % 2 == 0 else i - 2) for i in range(n)],
        "b": [(i, i - 2 if i // 2 % 2 == 0 else i + 2) for i in range(n)],
    }
    links = {name: [p for p in pairs if 0 <= p[1] < n] for name, pairs in links.items()}
    swap = functools.partial(lax.ppermute, axis_name="fsdp", perm=[(i, i ^ 1) for i in range(n)])

    def exchange(bufs):
        return {name: lax.ppermute(bufs[name], "fsdp", links[name]) for name in links}

    def part(array, h):
        return View(array, h * size, size)

    opening = exchange({"a": weights, "b": weights})
    got = {(1, h): {link: part(opening[link], h) for link in links} for h in range(CHUNKS)}

    def arrivals(link, slot):
        if slot == 1:
            return [opening[link]]
        return [got[slot, h][link].array for h in range(CHUNKS)]

    def send(*turns, after=()):
        return swap(pack(plan, row, rows, [], act, turns, after))

    parcel = swap(cot)
    cot_oth = [part(parcel, h) for h in range(CHUNKS)]
    pieces = [View(send(0), 0, rows)]

    parcel = send(*range(1, depth - 1), after=[parcel, pieces[0].array])
    pieces += [View(parcel, k * rows, rows) for k in range(depth - 2)]

    arrived, shards, parts = [], [], []

    def shard_step(j, xg):
        candidates = [[weights]]
        if j > 0:
            candidates = [arrivals(*source) for source in plan.sources[j]]
        xg, parcel, shard = project(plan, row, j, candidates, act, cot, cot_oth, xg)
        shards.append(shard)
        parts.append(View(parcel, 0, rows))
        return xg

    def send_parts(views, turns, after):
        parcel = swap(pack(plan, row, rows, views, act, turns, after))
        arrived.extend(View(parcel, t * rows, rows) for t in range(len(views)))
        return parcel

    xg = shard_step(0, None)
    parcel = send_parts(parts, [depth - 1], [parcel])
    pieces.append(View(parcel, rows, rows))
    bufs = {}
    for s in range(2, depth + 1):
        if s == depth:
            for j in range(2, depth - 1):
                xg = shard_step(j, xg)
            send_parts(parts[1:], [], [parcel])
            grad = own_gradient(plan, row, act, pieces[depth - 1], cot, cot_oth)
            sums = values(plan, row, list(range(depth - 1)), shards, act, pieces, None)
        for h in range(CHUNKS):
            after = list(bufs.values())[:1]
            if s == 3 and h == 0:
                xg = shard_step(1, xg)
                after.append(parts[1].array)
            if s == depth and h == CHUNKS - 1:
                after.append(sums[0])
            bufs = relay(
                plan, row, s, got[s - 1, h], act, pieces[: s - 1], part(cot, h), cot_oth[h], after
            )
            got[s, h] = {link: part(array, 0) for link, array in exchange(bufs).items()}
    xg = shard_step(depth - 1, xg)
    kv_own, parcel = values(plan, row, [depth - 1], shards[-1:], act, pieces, sums, parts[-1])
    final = swap(parcel)

    scalars = (row, mix_numerator, partner)
    moments, averaged, placed = None, None, None
    for h in range(CHUNKS):
        last = h == CHUNKS - 1
        after = [] if h == 0 else [(placed_tile, ANY)]
        *moments, stepped = adam(
            row, h, got[depth, h], grad, weights, first, second, moments, after + [(parcel, ANY)]
        )
        if placed is None:
            placed, placed_tile = place(plan, row, xg, arrived, 0)
        others = partner_rows(stepped, partner, row[plan["replica"]], n_rep)
        if last:
            views = [View(final, columns, rows)]
            kv_views = (kv_own, View(final, 0, columns))
            x_grad, kv_out = place(plan, row, placed, views, depth - 1, kv_views, [tile])
        averaged, tile = average(
            plan, scalars, h, stepped, others, averaged, columns, [kv_out] if last else []
        )
    return (
        kv_out[None],
        x_grad[None],
        averaged[None],
        moments[0][None],
        moments[1][None],
    )


def solution(mesh):
    placed = P("rep", "fsdp", None)
    return jax.shard_map(
        functools.partial(per_device, mesh.shape["rep"], mesh.shape["fsdp"]),
        mesh=mesh,
        in_specs=(placed,) * 5 + (P(), P()),
        out_specs=(placed,) * 5,
        check_vma=False,
    )
```

```python
import functools

import jax
import jax.numpy as jnp
import numpy as np
from jax import lax
from jax.experimental import pallas as pl
from jax.experimental.pallas import tpu as pltpu
from jax.sharding import PartitionSpec as P

beta_one = 0.9
beta_two = 0.999
learn_rate = 0.02
weight_decay = 0.1
adam_eps = 1e-08
corr_one = 1.0 - beta_one**10
corr_two = 1.0 - beta_two**10
mix_denom = 64.0

CHUNKS = 2
MIB = 1 << 20
ANY = pl.BlockSpec(memory_space=pl.ANY)
HBM = pl.BlockSpec(memory_space=pltpu.HBM)

TN = (((0,), (0,)), ((), ()))
NT = (((1,), (1,)), ((), ()))


def dot(a, b, dims=(((1,), (0,)), ((), ()))):
    return lax.dot_general(a, b, dims, preferred_element_type=jnp.float32)


class Plan:
    def __init__(self, n_rep, n):
        self.depth = depth = n // 2
        self.columns = {}
        self.rows = [[] for _ in range(n_rep * n)]
        order = [
            sorted(range(depth), key=lambda q: (-abs(q - z), (q < z) != (2 * z >= depth)))
            for z in range(depth)
        ]
        self.sources = [set() for _ in range(depth)]
        arrivals = []
        for z in range(depth):
            below, above = ("b", "a") if z % 2 == 0 else ("a", "b")
            ups = [(z - t, (below, t)) for t in range(1, z + 1)]
            downs = [(z + t, (above, t)) for t in range(1, depth - z)]
            arrivals.append(downs + ups if 2 * z < depth else ups + downs)
            for j, (_, source) in enumerate(arrivals[z], 1):
                self.sources[j].add(source)
        self.sources = [sorted(s) for s in self.sources]
        for device in range(n_rep * n):
            replica, i = divmod(device, n)
            z, x = divmod(i, 2)
            put = functools.partial(self._put, device)
            put("replica", replica)
            put("own", i)
            for k in range(depth):
                put(f"pack{k}", 2 * order[z][k] + 1 - x)
            for s in range(2, depth + 1):
                up, down = z + 1 + depth - s, z - 1 - depth + s
                for link, q in zip("ab", (up, down) if z % 2 == 0 else (down, up)):
                    add = 0 <= q < depth
                    put(f"add_{link}{s}", int(add))
                    put(f"blk_{link}{s}", 2 * q + x if add else 0)
                    put(f"pos_{link}{s}", order[z].index(q) if add else 0)
            for j in range(depth):
                q, source = (z, None) if j == 0 else arrivals[z][j - 1]
                put(f"mine{j}", 2 * q + x)
                put(f"theirs{j}", 2 * q + 1 - x)
                put(f"piece{j}", order[z].index(q))
                put(f"source{j}", 0 if j == 0 else self.sources[j].index(source))
        self.table = np.asarray(self.rows, np.int32)

    def _put(self, i, name, value):
        column = self.columns.setdefault(name, len(self.columns))
        assert column == len(self.rows[i])
        self.rows[i].append(value)

    def __getitem__(self, name):
        return self.columns[name]


def call(kernel, row, ins, outs, grid=(1,), aliases=None, scratch=(), vmem=16):
    scalars = row if isinstance(row, tuple) else (row,)
    return pl.pallas_call(
        kernel,
        grid_spec=pltpu.PrefetchScalarGridSpec(
            num_scalar_prefetch=len(scalars),
            grid=grid,
            in_specs=[spec for _, spec in ins],
            out_specs=[spec for _, spec in outs],
            scratch_shapes=list(scratch),
        ),
        out_shape=[shape for shape, _ in outs],
        input_output_aliases=aliases or {},
        compiler_params=pltpu.CompilerParams(vmem_limit_bytes=vmem * MIB),
        cost_estimate=pl.CostEstimate(flops=0, bytes_accessed=0, transcendentals=0),
    )(*scalars, *[array for array, _ in ins])


def whole(array):
    rank = array.ndim
    return pl.BlockSpec(array.shape, lambda g, row: (0,) * rank)


def block(shape, column, scale=1, offset=0):
    return pl.BlockSpec(shape, lambda g, row: (0, row[column] * scale + offset))


def struct(shape, dtype):
    return jax.ShapeDtypeStruct(shape, dtype)


class View:
    def __init__(self, array, start, count):
        assert start % count == 0
        self.array, self.start, self.count = array, start, count
        self.shape = (array.shape[0], count)

    def operand(self):
        at = self.start // self.count
        return self.array, pl.BlockSpec(self.shape, lambda g, row: (0, at))


def pack(plan, row, width, views, act=None, turns=(), after=()):
    count = len(views) + len(turns)
    ins = [v.operand() for v in views]
    tokens = views[0].shape[0] if views else act.shape[0]
    ins += [(act, block((tokens, width), plan[f"pack{k}"])) for k in turns]
    sizes = [v.count for v in views] + [width] * len(turns)

    def kernel(row_ref, *refs):
        at = 0
        for ref, size in zip(refs[:count], sizes):
            refs[-1][:, at : at + size] = ref[...]
            at += size

    out = struct((tokens, sum(sizes)), jnp.bfloat16)
    return call(
        kernel,
        row,
        ins + [(a, ANY) for a in after],
        [(out, whole(out))],
    )[0]


def relay(plan, row, s, got, act, pieces, cot_own, cot_oth, after=()):
    (tokens, columns), rows = cot_own.shape, got["a"].shape[0]
    count = len(pieces)

    def kernel(row_ref, *refs):
        got_refs, act_refs = refs[0:2], refs[2:4]
        piece_refs = refs[4 : 4 + count]
        own_ref, oth_ref = refs[4 + count : 6 + count]
        out_refs, held = refs[-3:-1], refs[-1]
        for d, link in enumerate("ab"):
            add = row_ref[plan[f"add_{link}{s}"]]
            pos = row_ref[plan[f"pos_{link}{s}"]]

            @pl.when(add == 0)
            def _():
                out_refs[d][...] = got_refs[d][...]

            @pl.when(add == 1)
            def _():
                for j in range(count):

                    @pl.when(pos == j)
                    def _():
                        held[...] = piece_refs[j][...]

                total = dot(act_refs[d][...], own_ref[...], TN)
                total = total + dot(held[...], oth_ref[...], TN)
                out_refs[d][...] = (total + got_refs[d][...].astype(jnp.float32)).astype(jnp.bfloat16)

    ins = [got[link].operand() for link in "ba"]
    ins += [(act, block((tokens, rows), plan[f"blk_{link}{s}"])) for link in "ab"]
    ins += [view.operand() for view in (*pieces, cot_own, cot_oth)]
    ins += [(a, ANY) for a in after]
    out = struct((rows, columns), jnp.bfloat16)
    a, b = call(
        kernel,
        row,
        ins,
        [(out, whole(out)), (out, whole(out))],
        scratch=[pltpu.VMEM((tokens, rows), jnp.bfloat16)],
    )
    return {"a": a, "b": b}


def own_gradient(plan, row, act, piece, cot, cot_oth):
    tokens, columns = cot.shape
    rows = piece.shape[1]

    def kernel(row_ref, act_ref, piece_ref, own_ref, *refs):
        out_ref = refs[-1]
        at = 0
        for ref, view in zip(refs, cot_oth):
            part = slice(at, at + view.count)
            total = dot(act_ref[...], own_ref[:, part], TN)
            out_ref[:, part] = total + dot(piece_ref[...], ref[...], TN)
            at += view.count

    out = struct((rows, columns), jnp.float32)
    return call(
        kernel,
        row,
        [(act, block((tokens, rows), plan["own"])), piece.operand(), (cot, whole(cot))]
        + [view.operand() for view in cot_oth],
        [(out, whole(out))],
    )[0]


def project(plan, row, j, candidates, act, cot, cot_oth, xg_before):
    (tokens, columns), rows = cot.shape, candidates[0][0].shape[0]
    flat = [c for candidate in candidates for c in candidate]
    starts = np.cumsum([0] + [len(candidate) for candidate in candidates])
    parts = max(len(candidate) for candidate in candidates)
    n_w, n_c = len(flat), len(cot_oth)

    def kernel(row_ref, *refs):
        w_refs, cot_refs = refs[:n_w], refs[n_w : n_w + n_c]
        own_ref = refs[n_w + n_c]
        xg_own, xg_oth, w_out, sems = refs[-4:]
        for c in range(len(candidates)):

            @pl.when(row_ref[plan[f"source{j}"]] == c)
            def _():
                copies, at = [], 0
                for p in range(starts[c], starts[c + 1]):
                    to = w_out.at[:, pl.ds(at, flat[p].shape[1])]
                    copies.append(pltpu.make_async_copy(w_refs[p], to, sems.at[len(copies)]))
                    at += flat[p].shape[1]
                for copy in copies:
                    copy.start()
                for copy in copies:
                    copy.wait()

        total, at = 0.0, 0
        for ref, view in zip(cot_refs, cot_oth):
            total = total + dot(ref[...], w_out[:, at : at + view.count], NT)
            at += view.count
        xg_oth[...] = total.astype(jnp.bfloat16)
        xg_own[...] = dot(own_ref[...], w_out[...], NT).astype(jnp.bfloat16)

    ins = [(w, ANY) for w in flat] + [view.operand() for view in cot_oth] + [(cot, whole(cot))]
    aliases = {}
    if xg_before is not None:
        aliases = {1 + len(ins): 0}
        ins.append((xg_before, HBM))
    other = struct((tokens, rows), jnp.bfloat16)
    shard = struct((rows, columns), jnp.bfloat16)
    return call(
        kernel,
        row,
        ins,
        [
            (struct(act.shape, jnp.bfloat16), block((tokens, rows), plan[f"mine{j}"])),
            (other, whole(other)),
            (shard, whole(shard)),
        ],
        aliases=aliases,
        scratch=[pltpu.SemaphoreType.DMA((parts,))],
        vmem=20,
    )


def values(plan, row, turns, shards, act, pieces, kept, behind=None):
    rows, columns = shards[0].shape
    tokens = act.shape[0]
    count, n_p = len(turns), len(pieces)
    extra = 0 if behind is None else behind.count

    def kernel(row_ref, *refs):
        w_refs, act_refs = refs[:count], refs[count : 2 * count]
        piece_refs = refs[2 * count : 2 * count + n_p]
        rest = list(refs[2 * count + n_p : -3])
        own_out, oth_out, held = refs[-3:]
        own = oth = 0.0
        if kept is not None:
            own, oth = rest.pop(0)[...], rest.pop(0)[...]
        for t, j in enumerate(turns):
            for p in range(n_p):

                @pl.when(row_ref[plan[f"piece{j}"]] == p)
                def _():
                    held[...] = piece_refs[p][...]

            oth = oth + dot(held[...], w_refs[t][...])
            own = own + dot(act_refs[t][...], w_refs[t][...])
        oth_out[:, :columns] = oth.astype(oth_out.dtype)
        if behind is not None:
            oth_out[:, columns:] = rest.pop(0)[...]
        own_out[...] = own

    ins = [(w, whole(w)) for w in shards]
    ins += [(act, block((tokens, rows), plan[f"mine{j}"])) for j in turns]
    ins += [p.operand() for p in pieces]
    if kept is not None:
        ins += [(k, whole(k)) for k in kept]
    if behind is not None:
        ins.append(behind.operand())
    own = struct((tokens, columns), jnp.float32)
    oth = struct((tokens, columns + extra), jnp.float32 if behind is None else jnp.bfloat16)
    return call(
        kernel,
        row,
        ins,
        [(own, whole(own)), (oth, whole(oth))],
        scratch=[pltpu.VMEM((tokens, rows), jnp.bfloat16)],
        vmem=28,
    )


def place(plan, row, xg, arrived, first, sums=None):
    count = len(arrived)
    tokens, width = arrived[0].shape
    table = [plan[f"theirs{first + j}"] for j in range(count)]

    def kernel(row_ref, *refs):
        g = pl.program_id(0)
        out_ref, tile_ref = refs[-2:] if sums is None else refs[-3:-1]
        for j in range(count):

            @pl.when(g == j)
            def _():
                out_ref[...] = refs[j][...]

        tile_ref[...] = jnp.zeros_like(tile_ref)
        if sums is not None:
            total = refs[count][...] + refs[count + 1][...].astype(jnp.float32)
            refs[-1][...] = total.astype(jnp.bfloat16)

    def column(g, row):
        at = row[table[0]]
        for j in range(1, count):
            at = jnp.where(g == j, row[table[j]], at)
        return (0, at)

    ins = [view.operand() for view in arrived]
    outs = [(struct(xg.shape, xg.dtype), pl.BlockSpec((tokens, width), column))]
    tile = struct((8, 128), jnp.float32)
    outs.append((tile, whole(tile)))
    if sums is not None:
        own, other = sums
        kv_block = pl.BlockSpec((tokens // count, own.shape[1]), lambda g, row: (g, 0))
        assert other.start == 0
        ins += [(own, kv_block), (other.array, kv_block)]
        outs.append((struct(own.shape, jnp.bfloat16), kv_block))
    aliases = {1 + len(ins): 0}
    return call(
        kernel,
        row,
        ins + [(xg, HBM)],
        outs,
        grid=(count,),
        aliases=aliases,
    )


def adam(row, h, got, grad, weights, first, second, kept, after=()):
    rows, columns = got["a"].shape
    assert got["a"].start == 0
    steps = 4 if rows % 64 == 0 else 1
    size = rows // steps

    def kernel(row_ref, up_ref, dn_ref, grad_ref, w_ref, a_ref, b_ref, *refs):
        a_out, b_out, stepped = refs[-3:]
        gradient = grad_ref[...] + up_ref[...].astype(jnp.float32) + dn_ref[...].astype(jnp.float32)
        moment_a = beta_one * a_ref[...] + (1.0 - beta_one) * gradient
        moment_b = beta_two * b_ref[...] + (1.0 - beta_two) * gradient * gradient
        old = w_ref[...].astype(jnp.float32)
        update = moment_a / corr_one / (jnp.sqrt(moment_b / corr_two) + adam_eps) + weight_decay * old
        a_out[...] = moment_a
        b_out[...] = moment_b
        stepped[...] = (old - learn_rate * update).astype(jnp.bfloat16)

    local = pl.BlockSpec((size, columns), lambda g, row: (g, 0))
    part = pl.BlockSpec((size, columns), lambda g, row: (g, h))
    ins = [(got["a"].array, local), (got["b"].array, local)]
    ins += [(a, part) for a in (grad, weights, first, second)]
    aliases = {}
    if kept is not None:
        aliases = {1 + len(ins): 0, 2 + len(ins): 1}
        ins += [(a, HBM) for a in kept]
    ins += after
    return call(
        kernel,
        row,
        ins,
        [
            (struct(first.shape, jnp.float32), part),
            (struct(second.shape, jnp.float32), part),
            (struct((rows, columns), jnp.bfloat16), local),
        ],
        grid=(steps,),
        aliases=aliases,
    )


def average(plan, scalars, stepped, others, after):
    rows, columns = stepped[0].shape
    chunks, count = len(stepped), len(others[0])
    steps = 4 if rows % 64 == 0 else 1
    size = rows // steps

    def kernel(row_ref, numerator_ref, partner_ref, *refs):
        mix = numerator_ref[row_ref[plan["replica"]]].astype(jnp.float32) / mix_denom
        for j in range(count):

            @pl.when((partner_ref[0] == j + 1) | (count == 1))
            def _():
                for h in range(chunks):
                    own, other = refs[h * (count + 1)], refs[h * (count + 1) + 1 + j]
                    refs[-1][:, h * columns : (h + 1) * columns] = (
                        (1.0 - mix) * own[...].astype(jnp.float32)
                        + mix * other[...].astype(jnp.float32)
                    ).astype(jnp.bfloat16)

    local = pl.BlockSpec((size, columns), lambda g, *scalars: (g, 0))
    full = pl.BlockSpec((size, chunks * columns), lambda g, *scalars: (g, 0))
    ins = [(a, local) for h in range(chunks) for a in (stepped[h], *others[h])]
    return call(
        kernel,
        scalars,
        ins + [(a, ANY) for a in after],
        [(struct((rows, chunks * columns), jnp.bfloat16), full)],
        grid=(steps,),
    )[0]


def partner_rows(stepped, partner, replica, n_rep):
    if n_rep != 4:
        gathered = lax.all_gather(stepped, "rep", axis=0, tiled=False)
        return [lax.dynamic_index_in_dim(gathered, partner[replica], 0, keepdims=False)]
    far = lax.ppermute(stepped, "rep", [(r, r ^ 2) for r in range(4)])
    core = [(r, r ^ 1) for r in range(4)]
    return [lax.ppermute(stepped, "rep", core), far, lax.ppermute(far, "rep", core)]


def per_device(
    n_rep, n, activations, kv_weight, kv_cotangent, first_moment, second_moment, partner, mix_numerator
):
    act, weights, cot = activations[0], kv_weight[0], kv_cotangent[0]
    first, second = first_moment[0], second_moment[0]
    plan = Plan(n_rep, n)
    depth = plan.depth
    rows, columns = weights.shape
    size = columns // CHUNKS
    row = lax.dynamic_index_in_dim(
        jnp.asarray(plan.table), lax.axis_index(("rep", "fsdp")), 0, keepdims=False
    )
    links = {
        "a": [(i, i + 2 if i // 2 % 2 == 0 else i - 2) for i in range(n)],
        "b": [(i, i - 2 if i // 2 % 2 == 0 else i + 2) for i in range(n)],
    }
    links = {name: [p for p in pairs if 0 <= p[1] < n] for name, pairs in links.items()}
    swap = functools.partial(lax.ppermute, axis_name="fsdp", perm=[(i, i ^ 1) for i in range(n)])

    def exchange(bufs):
        return {name: lax.ppermute(bufs[name], "fsdp", links[name]) for name in links}

    def part(array, h):
        return View(array, h * size, size)

    opening = exchange({"a": weights, "b": weights})
    got = {(1, h): {link: part(opening[link], h) for link in links} for h in range(CHUNKS)}

    def arrivals(link, slot):
        if slot == 1:
            return [opening[link]]
        return [got[slot, h][link].array for h in range(CHUNKS)]

    def send(*turns, after=()):
        return swap(pack(plan, row, rows, [], act, turns, after))

    parcel = swap(cot)
    cot_oth = [part(parcel, h) for h in range(CHUNKS)]
    pieces = [View(send(0), 0, rows)]

    parcel = send(*range(1, depth - 1), after=[parcel, pieces[0].array])
    pieces += [View(parcel, k * rows, rows) for k in range(depth - 2)]

    arrived, shards, parts = [], [], []

    def shard_step(j, xg):
        candidates = [[weights]]
        if j > 0:
            candidates = [arrivals(*source) for source in plan.sources[j]]
        xg, parcel, shard = project(plan, row, j, candidates, act, cot, cot_oth, xg)
        shards.append(shard)
        parts.append(View(parcel, 0, rows))
        return xg

    def send_parts(views, turns, after):
        parcel = swap(pack(plan, row, rows, views, act, turns, after))
        arrived.extend(View(parcel, t * rows, rows) for t in range(len(views)))
        return parcel

    xg = shard_step(0, None)
    parcel = send_parts(parts, [depth - 1], [parcel])
    pieces.append(View(parcel, rows, rows))
    bufs = {}
    for s in range(2, depth + 1):
        if s == depth:
            for j in range(2, depth - 1):
                xg = shard_step(j, xg)
            send_parts(parts[1:], [], [parcel])
            grad = own_gradient(plan, row, act, pieces[depth - 1], cot, cot_oth)
            sums = values(plan, row, list(range(depth - 1)), shards, act, pieces, None)
        for h in range(CHUNKS):
            after = list(bufs.values())[:1]
            if s == 3 and h == 0:
                xg = shard_step(1, xg)
                after.append(parts[1].array)
            if s == depth and h == CHUNKS - 1:
                xg = shard_step(depth - 1, xg)
                kv_own, parcel = values(
                    plan, row, [depth - 1], shards[-1:], act, pieces, sums, parts[-1]
                )
                final = swap(parcel)
                after += [sums[0], grad]
            bufs = relay(
                plan, row, s, got[s - 1, h], act, pieces[: s - 1], part(cot, h), cot_oth[h], after
            )
            got[s, h] = {link: part(array, 0) for link, array in exchange(bufs).items()}
    scalars = (row, mix_numerator, partner)
    moments, placed = None, None
    stepped, others = [], []
    for h in range(CHUNKS):
        after = [] if h == 0 else [(placed_tile, ANY)]
        *moments, rows_now = adam(
            row, h, got[depth, h], grad, weights, first, second, moments, after
        )
        if placed is None:
            placed, placed_tile = place(plan, row, xg, arrived, 0)
        stepped.append(rows_now)
        others.append(partner_rows(rows_now, partner, row[plan["replica"]], n_rep))
    views = [View(final, columns, rows)]
    kv_views = (kv_own, View(final, 0, columns))
    x_grad, tile, kv_out = place(plan, row, placed, views, depth - 1, kv_views)
    averaged = average(plan, scalars, stepped, others, [tile])
    return (
        kv_out[None],
        x_grad[None],
        averaged[None],
        moments[0][None],
        moments[1][None],
    )


def solution(mesh):
    placed = P("rep", "fsdp", None)
    return jax.shard_map(
        functools.partial(per_device, mesh.shape["rep"], mesh.shape["fsdp"]),
        mesh=mesh,
        in_specs=(placed,) * 5 + (P(), P()),
        out_specs=(placed,) * 5,
        check_vma=False,
    )
```

```python
import functools

import jax
import jax.numpy as jnp
import numpy as np
from jax import lax
from jax.experimental import pallas as pl
from jax.experimental.pallas import tpu as pltpu
from jax.sharding import PartitionSpec as P

beta_one = 0.9
beta_two = 0.999
learn_rate = 0.02
weight_decay = 0.1
adam_eps = 1e-08
corr_one = 1.0 - beta_one**10
corr_two = 1.0 - beta_two**10
mix_denom = 64.0

CHUNKS = 2
MIB = 1 << 20
ANY = pl.BlockSpec(memory_space=pl.ANY)
HBM = pl.BlockSpec(memory_space=pltpu.HBM)

TN = (((0,), (0,)), ((), ()))
NT = (((1,), (1,)), ((), ()))


def dot(a, b, dims=(((1,), (0,)), ((), ()))):
    return lax.dot_general(a, b, dims, preferred_element_type=jnp.float32)


class Plan:
    def __init__(self, n_rep, n):
        self.depth = depth = n // 2
        self.columns = {}
        self.rows = [[] for _ in range(n_rep * n)]
        order = [
            sorted(range(depth), key=lambda q: (-abs(q - z), (q < z) != (2 * z >= depth)))
            for z in range(depth)
        ]
        self.sources = [set() for _ in range(depth)]
        arrivals = []
        for z in range(depth):
            below, above = ("b", "a") if z % 2 == 0 else ("a", "b")
            ups = [(z - t, (below, t)) for t in range(1, z + 1)]
            downs = [(z + t, (above, t)) for t in range(1, depth - z)]
            arrivals.append(downs + ups if 2 * z < depth else ups + downs)
            for j, (_, source) in enumerate(arrivals[z], 1):
                self.sources[j].add(source)
        self.sources = [sorted(s) for s in self.sources]
        for device in range(n_rep * n):
            replica, i = divmod(device, n)
            z, x = divmod(i, 2)
            put = functools.partial(self._put, device)
            put("replica", replica)
            put("own", i)
            for k in range(depth):
                put(f"pack{k}", 2 * order[z][k] + 1 - x)
            for s in range(2, depth + 1):
                up, down = z + 1 + depth - s, z - 1 - depth + s
                for link, q in zip("ab", (up, down) if z % 2 == 0 else (down, up)):
                    add = 0 <= q < depth
                    put(f"add_{link}{s}", int(add))
                    put(f"blk_{link}{s}", 2 * q + x if add else 0)
                    put(f"pos_{link}{s}", order[z].index(q) if add else 0)
            for j in range(depth):
                q, source = (z, None) if j == 0 else arrivals[z][j - 1]
                put(f"mine{j}", 2 * q + x)
                put(f"theirs{j}", 2 * q + 1 - x)
                put(f"piece{j}", order[z].index(q))
                put(f"source{j}", 0 if j == 0 else self.sources[j].index(source))
        self.table = np.asarray(self.rows, np.int32)

    def _put(self, i, name, value):
        column = self.columns.setdefault(name, len(self.columns))
        assert column == len(self.rows[i])
        self.rows[i].append(value)

    def __getitem__(self, name):
        return self.columns[name]


def call(kernel, row, ins, outs, grid=(1,), aliases=None, scratch=(), vmem=16):
    scalars = row if isinstance(row, tuple) else (row,)
    return pl.pallas_call(
        kernel,
        grid_spec=pltpu.PrefetchScalarGridSpec(
            num_scalar_prefetch=len(scalars),
            grid=grid,
            in_specs=[spec for _, spec in ins],
            out_specs=[spec for _, spec in outs],
            scratch_shapes=list(scratch),
        ),
        out_shape=[shape for shape, _ in outs],
        input_output_aliases=aliases or {},
        compiler_params=pltpu.CompilerParams(vmem_limit_bytes=vmem * MIB),
        cost_estimate=pl.CostEstimate(flops=0, bytes_accessed=0, transcendentals=0),
    )(*scalars, *[array for array, _ in ins])


def whole(array):
    rank = array.ndim
    return pl.BlockSpec(array.shape, lambda g, row: (0,) * rank)


def block(shape, column, scale=1, offset=0):
    return pl.BlockSpec(shape, lambda g, row: (0, row[column] * scale + offset))


def struct(shape, dtype):
    return jax.ShapeDtypeStruct(shape, dtype)


class View:
    def __init__(self, array, start, count):
        assert start % count == 0
        self.array, self.start, self.count = array, start, count
        self.shape = (array.shape[0], count)

    def operand(self):
        at = self.start // self.count
        return self.array, pl.BlockSpec(self.shape, lambda g, row: (0, at))


def pack(plan, row, width, views, act=None, turns=(), after=()):
    count = len(views) + len(turns)
    ins = [v.operand() for v in views]
    tokens = views[0].shape[0] if views else act.shape[0]
    ins += [(act, block((tokens, width), plan[f"pack{k}"])) for k in turns]
    sizes = [v.count for v in views] + [width] * len(turns)

    def kernel(row_ref, *refs):
        at = 0
        for ref, size in zip(refs[:count], sizes):
            refs[-1][:, at : at + size] = ref[...]
            at += size

    out = struct((tokens, sum(sizes)), jnp.bfloat16)
    return call(
        kernel,
        row,
        ins + [(a, ANY) for a in after],
        [(out, whole(out))],
    )[0]


def relay(plan, row, s, got, act, pieces, cot_own, cot_oth, after=()):
    (tokens, columns), rows = cot_own.shape, got["a"].shape[0]
    count = len(pieces)

    def kernel(row_ref, *refs):
        got_refs, act_refs = refs[0:2], refs[2:4]
        piece_refs = refs[4 : 4 + count]
        own_ref, oth_ref = refs[4 + count : 6 + count]
        out_refs, held = refs[-3:-1], refs[-1]
        for d, link in enumerate("ab"):
            add = row_ref[plan[f"add_{link}{s}"]]
            pos = row_ref[plan[f"pos_{link}{s}"]]

            @pl.when(add == 0)
            def _():
                out_refs[d][...] = got_refs[d][...]

            @pl.when(add == 1)
            def _():
                for j in range(count):

                    @pl.when(pos == j)
                    def _():
                        held[...] = piece_refs[j][...]

                total = dot(act_refs[d][...], own_ref[...], TN)
                total = total + dot(held[...], oth_ref[...], TN)
                out_refs[d][...] = (total + got_refs[d][...].astype(jnp.float32)).astype(jnp.bfloat16)

    ins = [got[link].operand() for link in "ba"]
    ins += [(act, block((tokens, rows), plan[f"blk_{link}{s}"])) for link in "ab"]
    ins += [view.operand() for view in (*pieces, cot_own, cot_oth)]
    ins += [(a, ANY) for a in after]
    out = struct((rows, columns), jnp.bfloat16)
    a, b = call(
        kernel,
        row,
        ins,
        [(out, whole(out)), (out, whole(out))],
        scratch=[pltpu.VMEM((tokens, rows), jnp.bfloat16)],
    )
    return {"a": a, "b": b}


def own_gradient(plan, row, act, piece, cot, cot_oth):
    tokens, columns = cot.shape
    rows = piece.shape[1]

    def kernel(row_ref, act_ref, piece_ref, own_ref, *refs):
        out_ref = refs[-1]
        at = 0
        for ref, view in zip(refs, cot_oth):
            part = slice(at, at + view.count)
            total = dot(act_ref[...], own_ref[:, part], TN)
            out_ref[:, part] = total + dot(piece_ref[...], ref[...], TN)
            at += view.count

    out = struct((rows, columns), jnp.float32)
    return call(
        kernel,
        row,
        [(act, block((tokens, rows), plan["own"])), piece.operand(), (cot, whole(cot))]
        + [view.operand() for view in cot_oth],
        [(out, whole(out))],
    )[0]


def project(plan, row, j, candidates, act, cot, cot_oth, xg_before):
    (tokens, columns), rows = cot.shape, candidates[0][0].shape[0]
    flat = [c for candidate in candidates for c in candidate]
    starts = np.cumsum([0] + [len(candidate) for candidate in candidates])
    parts = max(len(candidate) for candidate in candidates)
    n_w, n_c = len(flat), len(cot_oth)

    def kernel(row_ref, *refs):
        w_refs, cot_refs = refs[:n_w], refs[n_w : n_w + n_c]
        own_ref = refs[n_w + n_c]
        xg_own, xg_oth, w_out, sems = refs[-4:]
        for c in range(len(candidates)):

            @pl.when(row_ref[plan[f"source{j}"]] == c)
            def _():
                copies, at = [], 0
                for p in range(starts[c], starts[c + 1]):
                    to = w_out.at[:, pl.ds(at, flat[p].shape[1])]
                    copies.append(pltpu.make_async_copy(w_refs[p], to, sems.at[len(copies)]))
                    at += flat[p].shape[1]
                for copy in copies:
                    copy.start()
                for copy in copies:
                    copy.wait()

        total, at = 0.0, 0
        for ref, view in zip(cot_refs, cot_oth):
            total = total + dot(ref[...], w_out[:, at : at + view.count], NT)
            at += view.count
        xg_oth[...] = total.astype(jnp.bfloat16)
        xg_own[...] = dot(own_ref[...], w_out[...], NT).astype(jnp.bfloat16)

    ins = [(w, ANY) for w in flat] + [view.operand() for view in cot_oth] + [(cot, whole(cot))]
    aliases = {}
    if xg_before is not None:
        aliases = {1 + len(ins): 0}
        ins.append((xg_before, HBM))
    other = struct((tokens, rows), jnp.bfloat16)
    shard = struct((rows, columns), jnp.bfloat16)
    return call(
        kernel,
        row,
        ins,
        [
            (struct(act.shape, jnp.bfloat16), block((tokens, rows), plan[f"mine{j}"])),
            (other, whole(other)),
            (shard, whole(shard)),
        ],
        aliases=aliases,
        scratch=[pltpu.SemaphoreType.DMA((parts,))],
        vmem=20,
    )


def values(plan, row, turns, shards, act, pieces, kept, behind=None):
    rows, columns = shards[0].shape
    tokens = act.shape[0]
    count, n_p = len(turns), len(pieces)
    extra = 0 if behind is None else behind.count

    def kernel(row_ref, *refs):
        w_refs, act_refs = refs[:count], refs[count : 2 * count]
        piece_refs = refs[2 * count : 2 * count + n_p]
        rest = list(refs[2 * count + n_p : -3])
        own_out, oth_out, held = refs[-3:]
        own = oth = 0.0
        if kept is not None:
            own, oth = rest.pop(0)[...], rest.pop(0)[...]
        for t, j in enumerate(turns):
            for p in range(n_p):

                @pl.when(row_ref[plan[f"piece{j}"]] == p)
                def _():
                    held[...] = piece_refs[p][...]

            oth = oth + dot(held[...], w_refs[t][...])
            own = own + dot(act_refs[t][...], w_refs[t][...])
        oth_out[:, :columns] = oth.astype(oth_out.dtype)
        if behind is not None:
            oth_out[:, columns:] = rest.pop(0)[...]
        own_out[...] = own

    ins = [(w, whole(w)) for w in shards]
    ins += [(act, block((tokens, rows), plan[f"mine{j}"])) for j in turns]
    ins += [p.operand() for p in pieces]
    if kept is not None:
        ins += [(k, whole(k)) for k in kept]
    if behind is not None:
        ins.append(behind.operand())
    own = struct((tokens, columns), jnp.float32)
    oth = struct((tokens, columns + extra), jnp.float32 if behind is None else jnp.bfloat16)
    return call(
        kernel,
        row,
        ins,
        [(own, whole(own)), (oth, whole(oth))],
        scratch=[pltpu.VMEM((tokens, rows), jnp.bfloat16)],
        vmem=28,
    )


def place(plan, row, xg, arrived, first, sums=None):
    count = len(arrived)
    tokens, width = arrived[0].shape
    table = [plan[f"theirs{first + j}"] for j in range(count)]

    def kernel(row_ref, *refs):
        g = pl.program_id(0)
        out_ref, tile_ref = refs[-2:] if sums is None else refs[-3:-1]
        for j in range(count):

            @pl.when(g == j)
            def _():
                out_ref[...] = refs[j][...]

        tile_ref[...] = jnp.zeros_like(tile_ref)
        if sums is not None:
            total = refs[count][...] + refs[count + 1][...].astype(jnp.float32)
            refs[-1][...] = total.astype(jnp.bfloat16)

    def column(g, row):
        at = row[table[0]]
        for j in range(1, count):
            at = jnp.where(g == j, row[table[j]], at)
        return (0, at)

    ins = [view.operand() for view in arrived]
    outs = [(struct(xg.shape, xg.dtype), pl.BlockSpec((tokens, width), column))]
    tile = struct((8, 128), jnp.float32)
    outs.append((tile, whole(tile)))
    if sums is not None:
        own, other = sums
        kv_block = pl.BlockSpec((tokens // count, own.shape[1]), lambda g, row: (g, 0))
        assert other.start == 0
        ins += [(own, kv_block), (other.array, kv_block)]
        outs.append((struct(own.shape, jnp.bfloat16), kv_block))
    aliases = {1 + len(ins): 0}
    return call(
        kernel,
        row,
        ins + [(xg, HBM)],
        outs,
        grid=(count,),
        aliases=aliases,
    )


def adam(row, h, got, grad, weights, first, second, kept, after=()):
    rows, columns = got["a"].shape
    assert got["a"].start == 0
    steps = 4 if rows % 64 == 0 else 1
    size = rows // steps

    def kernel(row_ref, up_ref, dn_ref, grad_ref, w_ref, a_ref, b_ref, *refs):
        a_out, b_out, stepped = refs[-3:]
        gradient = grad_ref[...] + up_ref[...].astype(jnp.float32) + dn_ref[...].astype(jnp.float32)
        moment_a = beta_one * a_ref[...] + (1.0 - beta_one) * gradient
        moment_b = beta_two * b_ref[...] + (1.0 - beta_two) * gradient * gradient
        old = w_ref[...].astype(jnp.float32)
        update = moment_a * (1.0 / corr_one) / (jnp.sqrt(moment_b * (1.0 / corr_two)) + adam_eps)
        update = update + weight_decay * old
        a_out[...] = moment_a
        b_out[...] = moment_b
        stepped[...] = (old - learn_rate * update).astype(jnp.bfloat16)

    local = pl.BlockSpec((size, columns), lambda g, row: (g, 0))
    part = pl.BlockSpec((size, columns), lambda g, row: (g, h))
    ins = [(got["a"].array, local), (got["b"].array, local)]
    ins += [(a, part) for a in (grad, weights, first, second)]
    aliases = {}
    if kept is not None:
        aliases = {1 + len(ins): 0, 2 + len(ins): 1}
        ins += [(a, HBM) for a in kept]
    ins += after
    return call(
        kernel,
        row,
        ins,
        [
            (struct(first.shape, jnp.float32), part),
            (struct(second.shape, jnp.float32), part),
            (struct((rows, columns), jnp.bfloat16), local),
        ],
        grid=(steps,),
        aliases=aliases,
    )


def average(plan, scalars, stepped, others, after):
    rows, columns = stepped[0].shape
    chunks, count = len(stepped), len(others[0])
    steps = 4 if rows % 64 == 0 else 1
    size = rows // steps

    def kernel(row_ref, numerator_ref, partner_ref, *refs):
        mix = numerator_ref[row_ref[plan["replica"]]].astype(jnp.float32) / mix_denom
        for j in range(count):

            @pl.when((partner_ref[0] == j + 1) | (count == 1))
            def _():
                for h in range(chunks):
                    own, other = refs[h * (count + 1)], refs[h * (count + 1) + 1 + j]
                    refs[-1][:, h * columns : (h + 1) * columns] = (
                        (1.0 - mix) * own[...].astype(jnp.float32)
                        + mix * other[...].astype(jnp.float32)
                    ).astype(jnp.bfloat16)

    local = pl.BlockSpec((size, columns), lambda g, *scalars: (g, 0))
    full = pl.BlockSpec((size, chunks * columns), lambda g, *scalars: (g, 0))
    chosen = [
        pl.BlockSpec(
            (size, columns),
            lambda g, row, numerator, partner, j=j: (
                jnp.where((partner[0] == j + 1) | (count == 1), g, 0),
                0,
            ),
        )
        for j in range(count)
    ]
    ins = []
    for h in range(chunks):
        ins += [(stepped[h], local), *zip(others[h], chosen)]
    return call(
        kernel,
        scalars,
        ins + [(a, ANY) for a in after],
        [(struct((rows, chunks * columns), jnp.bfloat16), full)],
        grid=(steps,),
    )[0]


def partner_rows(stepped, partner, replica, n_rep):
    if n_rep != 4:
        gathered = lax.all_gather(stepped, "rep", axis=0, tiled=False)
        return [lax.dynamic_index_in_dim(gathered, partner[replica], 0, keepdims=False)]
    far = lax.ppermute(stepped, "rep", [(r, r ^ 2) for r in range(4)])
    core = [(r, r ^ 1) for r in range(4)]
    return [lax.ppermute(stepped, "rep", core), far, lax.ppermute(far, "rep", core)]


def per_device(
    n_rep, n, activations, kv_weight, kv_cotangent, first_moment, second_moment, partner, mix_numerator
):
    act, weights, cot = activations[0], kv_weight[0], kv_cotangent[0]
    first, second = first_moment[0], second_moment[0]
    plan = Plan(n_rep, n)
    depth = plan.depth
    rows, columns = weights.shape
    size = columns // CHUNKS
    row = lax.dynamic_index_in_dim(
        jnp.asarray(plan.table), lax.axis_index(("rep", "fsdp")), 0, keepdims=False
    )
    links = {
        "a": [(i, i + 2 if i // 2 % 2 == 0 else i - 2) for i in range(n)],
        "b": [(i, i - 2 if i // 2 % 2 == 0 else i + 2) for i in range(n)],
    }
    links = {name: [p for p in pairs if 0 <= p[1] < n] for name, pairs in links.items()}
    swap = functools.partial(lax.ppermute, axis_name="fsdp", perm=[(i, i ^ 1) for i in range(n)])

    def exchange(bufs):
        return {name: lax.ppermute(bufs[name], "fsdp", links[name]) for name in links}

    def part(array, h):
        return View(array, h * size, size)

    opening = exchange({"a": weights, "b": weights})
    got = {(1, h): {link: part(opening[link], h) for link in links} for h in range(CHUNKS)}

    def arrivals(link, slot):
        if slot == 1:
            return [opening[link]]
        return [got[slot, h][link].array for h in range(CHUNKS)]

    def send(*turns, after=()):
        return swap(pack(plan, row, rows, [], act, turns, after))

    parcel = swap(cot)
    cot_oth = [part(parcel, h) for h in range(CHUNKS)]
    pieces = [View(send(0), 0, rows)]

    parcel = send(*range(1, depth - 1), after=[parcel, pieces[0].array])
    pieces += [View(parcel, k * rows, rows) for k in range(depth - 2)]

    arrived, shards, parts = [], [], []

    def shard_step(j, xg):
        candidates = [[weights]]
        if j > 0:
            candidates = [arrivals(*source) for source in plan.sources[j]]
        xg, parcel, shard = project(plan, row, j, candidates, act, cot, cot_oth, xg)
        shards.append(shard)
        parts.append(View(parcel, 0, rows))
        return xg

    def send_parts(views, turns, after):
        parcel = swap(pack(plan, row, rows, views, act, turns, after))
        arrived.extend(View(parcel, t * rows, rows) for t in range(len(views)))
        return parcel

    xg = shard_step(0, None)
    parcel = send_parts(parts, [depth - 1], [parcel])
    pieces.append(View(parcel, rows, rows))
    bufs = {}
    for s in range(2, depth + 1):
        if s == depth:
            for j in range(2, depth - 1):
                xg = shard_step(j, xg)
            send_parts(parts[1:], [], [parcel])
            grad = own_gradient(plan, row, act, pieces[depth - 1], cot, cot_oth)
            sums = values(plan, row, list(range(depth - 1)), shards, act, pieces, None)
        for h in range(CHUNKS):
            after = list(bufs.values())[:1]
            if s == 3 and h == 0:
                xg = shard_step(1, xg)
                after.append(parts[1].array)
            if s == depth and h == CHUNKS - 1:
                xg = shard_step(depth - 1, xg)
                kv_own, parcel = values(
                    plan, row, [depth - 1], shards[-1:], act, pieces, sums, parts[-1]
                )
                final = swap(parcel)
                after += [sums[0], grad]
            bufs = relay(
                plan, row, s, got[s - 1, h], act, pieces[: s - 1], part(cot, h), cot_oth[h], after
            )
            got[s, h] = {link: part(array, 0) for link, array in exchange(bufs).items()}
    scalars = (row, mix_numerator, partner)
    moments, placed = None, None
    stepped, others = [], []
    for h in range(CHUNKS):
        after = [] if h == 0 else [(placed_tile, ANY)]
        *moments, rows_now = adam(
            row, h, got[depth, h], grad, weights, first, second, moments, after
        )
        if placed is None:
            placed, placed_tile = place(plan, row, xg, arrived, 0)
        stepped.append(rows_now)
        others.append(partner_rows(rows_now, partner, row[plan["replica"]], n_rep))
    views = [View(final, columns, rows)]
    kv_views = (kv_own, View(final, 0, columns))
    x_grad, tile, kv_out = place(plan, row, placed, views, depth - 1, kv_views)
    averaged = average(plan, scalars, stepped, others, [tile])
    return (
        kv_out[None],
        x_grad[None],
        averaged[None],
        moments[0][None],
        moments[1][None],
    )


def solution(mesh):
    placed = P("rep", "fsdp", None)
    return jax.shard_map(
        functools.partial(per_device, mesh.shape["rep"], mesh.shape["fsdp"]),
        mesh=mesh,
        in_specs=(placed,) * 5 + (P(), P()),
        out_specs=(placed,) * 5,
        check_vma=False,
    )
```

```python
import functools

import jax
import jax.numpy as jnp
import numpy as np
from jax import lax
from jax.experimental import pallas as pl
from jax.experimental.pallas import tpu as pltpu
from jax.sharding import PartitionSpec as P

beta_one = 0.9
beta_two = 0.999
learn_rate = 0.02
weight_decay = 0.1
adam_eps = 1e-08
corr_one = 1.0 - beta_one**10
corr_two = 1.0 - beta_two**10
mix_denom = 64.0

CHUNKS = 2
MIB = 1 << 20
ANY = pl.BlockSpec(memory_space=pl.ANY)
HBM = pl.BlockSpec(memory_space=pltpu.HBM)

TN = (((0,), (0,)), ((), ()))
NT = (((1,), (1,)), ((), ()))


def dot(a, b, dims=(((1,), (0,)), ((), ()))):
    return lax.dot_general(a, b, dims, preferred_element_type=jnp.float32)


class Plan:
    def __init__(self, n_rep, n):
        self.depth = depth = n // 2
        self.columns = {}
        self.rows = [[] for _ in range(n_rep * n)]
        order = [
            sorted(range(depth), key=lambda q: (-abs(q - z), (q < z) != (2 * z >= depth)))
            for z in range(depth)
        ]
        self.sources = [set() for _ in range(depth)]
        arrivals = []
        for z in range(depth):
            below, above = ("b", "a") if z % 2 == 0 else ("a", "b")
            ups = [(z - t, (below, t)) for t in range(1, z + 1)]
            downs = [(z + t, (above, t)) for t in range(1, depth - z)]
            arrivals.append(downs + ups if 2 * z < depth else ups + downs)
            for j, (_, source) in enumerate(arrivals[z], 1):
                self.sources[j].add(source)
        self.sources = [sorted(s) for s in self.sources]
        for device in range(n_rep * n):
            replica, i = divmod(device, n)
            z, x = divmod(i, 2)
            put = functools.partial(self._put, device)
            put("replica", replica)
            put("own", i)
            for k in range(depth):
                put(f"pack{k}", 2 * order[z][k] + 1 - x)
            for s in range(2, depth + 1):
                up, down = z + 1 + depth - s, z - 1 - depth + s
                for link, q in zip("ab", (up, down) if z % 2 == 0 else (down, up)):
                    add = 0 <= q < depth
                    put(f"add_{link}{s}", int(add))
                    put(f"blk_{link}{s}", 2 * q + x if add else 0)
                    put(f"pos_{link}{s}", order[z].index(q) if add else 0)
            for j in range(depth):
                q, source = (z, None) if j == 0 else arrivals[z][j - 1]
                put(f"mine{j}", 2 * q + x)
                put(f"theirs{j}", 2 * q + 1 - x)
                put(f"piece{j}", order[z].index(q))
                put(f"source{j}", 0 if j == 0 else self.sources[j].index(source))
        self.table = np.asarray(self.rows, np.int32)

    def _put(self, i, name, value):
        column = self.columns.setdefault(name, len(self.columns))
        assert column == len(self.rows[i])
        self.rows[i].append(value)

    def __getitem__(self, name):
        return self.columns[name]


def call(kernel, row, ins, outs, grid=(1,), aliases=None, scratch=(), vmem=16):
    scalars = row if isinstance(row, tuple) else (row,)
    return pl.pallas_call(
        kernel,
        grid_spec=pltpu.PrefetchScalarGridSpec(
            num_scalar_prefetch=len(scalars),
            grid=grid,
            in_specs=[spec for _, spec in ins],
            out_specs=[spec for _, spec in outs],
            scratch_shapes=list(scratch),
        ),
        out_shape=[shape for shape, _ in outs],
        input_output_aliases=aliases or {},
        compiler_params=pltpu.CompilerParams(vmem_limit_bytes=vmem * MIB),
        cost_estimate=pl.CostEstimate(flops=0, bytes_accessed=0, transcendentals=0),
    )(*scalars, *[array for array, _ in ins])


def whole(array):
    rank = array.ndim
    return pl.BlockSpec(array.shape, lambda g, row: (0,) * rank)


def block(shape, column, scale=1, offset=0):
    return pl.BlockSpec(shape, lambda g, row: (0, row[column] * scale + offset))


def struct(shape, dtype):
    return jax.ShapeDtypeStruct(shape, dtype)


class View:
    def __init__(self, array, start, count):
        assert start % count == 0
        self.array, self.start, self.count = array, start, count
        self.shape = (array.shape[0], count)

    def operand(self):
        at = self.start // self.count
        return self.array, pl.BlockSpec(self.shape, lambda g, row: (0, at))


def pack(plan, row, width, views, act=None, turns=(), after=()):
    count = len(views) + len(turns)
    ins = [v.operand() for v in views]
    tokens = views[0].shape[0] if views else act.shape[0]
    ins += [(act, block((tokens, width), plan[f"pack{k}"])) for k in turns]
    sizes = [v.count for v in views] + [width] * len(turns)

    def kernel(row_ref, *refs):
        at = 0
        for ref, size in zip(refs[:count], sizes):
            refs[-1][:, at : at + size] = ref[...]
            at += size

    out = struct((tokens, sum(sizes)), jnp.bfloat16)
    return call(
        kernel,
        row,
        ins + [(a, ANY) for a in after],
        [(out, whole(out))],
    )[0]


def relay(plan, row, s, got, act, pieces, cot_own, cot_oth, after=()):
    (tokens, columns), rows = cot_own.shape, got["a"].shape[0]
    count = len(pieces)

    def kernel(row_ref, *refs):
        got_refs, act_refs = refs[0:2], refs[2:4]
        piece_refs = refs[4 : 4 + count]
        own_ref, oth_ref = refs[4 + count : 6 + count]
        out_refs, held = refs[-3:-1], refs[-1]
        for d, link in enumerate("ab"):
            add = row_ref[plan[f"add_{link}{s}"]]
            pos = row_ref[plan[f"pos_{link}{s}"]]

            @pl.when(add == 0)
            def _():
                out_refs[d][...] = got_refs[d][...]

            @pl.when(add == 1)
            def _():
                for j in range(count):

                    @pl.when(pos == j)
                    def _():
                        held[...] = piece_refs[j][...]

                total = dot(act_refs[d][...], own_ref[...], TN)
                total = total + dot(held[...], oth_ref[...], TN)
                out_refs[d][...] = (total + got_refs[d][...].astype(jnp.float32)).astype(jnp.bfloat16)

    ins = [got[link].operand() for link in "ba"]
    ins += [(act, block((tokens, rows), plan[f"blk_{link}{s}"])) for link in "ab"]
    ins += [view.operand() for view in (*pieces, cot_own, cot_oth)]
    ins += [(a, ANY) for a in after]
    out = struct((rows, columns), jnp.bfloat16)
    a, b = call(
        kernel,
        row,
        ins,
        [(out, whole(out)), (out, whole(out))],
        scratch=[pltpu.VMEM((tokens, rows), jnp.bfloat16)],
    )
    return {"a": a, "b": b}


def own_gradient(plan, row, act, piece, cot, cot_oth):
    tokens, columns = cot.shape
    rows = piece.shape[1]

    def kernel(row_ref, act_ref, piece_ref, own_ref, *refs):
        out_ref = refs[-1]
        at = 0
        for ref, view in zip(refs, cot_oth):
            part = slice(at, at + view.count)
            total = dot(act_ref[...], own_ref[:, part], TN)
            out_ref[:, part] = total + dot(piece_ref[...], ref[...], TN)
            at += view.count

    out = struct((rows, columns), jnp.float32)
    return call(
        kernel,
        row,
        [(act, block((tokens, rows), plan["own"])), piece.operand(), (cot, whole(cot))]
        + [view.operand() for view in cot_oth],
        [(out, whole(out))],
    )[0]


def project(plan, row, j, candidates, act, cot, cot_oth, xg_before):
    (tokens, columns), rows = cot.shape, candidates[0][0].shape[0]
    flat = [c for candidate in candidates for c in candidate]
    starts = np.cumsum([0] + [len(candidate) for candidate in candidates])
    parts = max(len(candidate) for candidate in candidates)
    n_w, n_c = len(flat), len(cot_oth)

    def kernel(row_ref, *refs):
        w_refs, cot_refs = refs[:n_w], refs[n_w : n_w + n_c]
        own_ref = refs[n_w + n_c]
        xg_own, xg_oth, w_out, sems = refs[-4:]
        for c in range(len(candidates)):

            @pl.when(row_ref[plan[f"source{j}"]] == c)
            def _():
                copies, at = [], 0
                for p in range(starts[c], starts[c + 1]):
                    to = w_out.at[:, pl.ds(at, flat[p].shape[1])]
                    copies.append(pltpu.make_async_copy(w_refs[p], to, sems.at[len(copies)]))
                    at += flat[p].shape[1]
                for copy in copies:
                    copy.start()
                for copy in copies:
                    copy.wait()

        total, at = 0.0, 0
        for ref, view in zip(cot_refs, cot_oth):
            total = total + dot(ref[...], w_out[:, at : at + view.count], NT)
            at += view.count
        xg_oth[...] = total.astype(jnp.bfloat16)
        xg_own[...] = dot(own_ref[...], w_out[...], NT).astype(jnp.bfloat16)

    ins = [(w, ANY) for w in flat] + [view.operand() for view in cot_oth] + [(cot, whole(cot))]
    aliases = {}
    if xg_before is not None:
        aliases = {1 + len(ins): 0}
        ins.append((xg_before, HBM))
    other = struct((tokens, rows), jnp.bfloat16)
    shard = struct((rows, columns), jnp.bfloat16)
    return call(
        kernel,
        row,
        ins,
        [
            (struct(act.shape, jnp.bfloat16), block((tokens, rows), plan[f"mine{j}"])),
            (other, whole(other)),
            (shard, whole(shard)),
        ],
        aliases=aliases,
        scratch=[pltpu.SemaphoreType.DMA((parts,))],
        vmem=20,
    )


def values(plan, row, turns, shards, act, pieces, kept, behind=None):
    rows, columns = shards[0].shape
    tokens = act.shape[0]
    count, n_p = len(turns), len(pieces)
    extra = 0 if behind is None else behind.count

    def kernel(row_ref, *refs):
        w_refs, act_refs = refs[:count], refs[count : 2 * count]
        piece_refs = refs[2 * count : 2 * count + n_p]
        rest = list(refs[2 * count + n_p : -3])
        own_out, oth_out, held = refs[-3:]
        own = oth = 0.0
        if kept is not None:
            own, oth = rest.pop(0)[...], rest.pop(0)[...]
        for t, j in enumerate(turns):
            for p in range(n_p):

                @pl.when(row_ref[plan[f"piece{j}"]] == p)
                def _():
                    held[...] = piece_refs[p][...]

            oth = oth + dot(held[...], w_refs[t][...])
            own = own + dot(act_refs[t][...], w_refs[t][...])
        oth_out[:, :columns] = oth.astype(oth_out.dtype)
        if behind is not None:
            oth_out[:, columns:] = rest.pop(0)[...]
        own_out[...] = own

    ins = [(w, whole(w)) for w in shards]
    ins += [(act, block((tokens, rows), plan[f"mine{j}"])) for j in turns]
    ins += [p.operand() for p in pieces]
    if kept is not None:
        ins += [(k, whole(k)) for k in kept]
    if behind is not None:
        ins.append(behind.operand())
    own = struct((tokens, columns), jnp.float32)
    oth = struct((tokens, columns + extra), jnp.float32 if behind is None else jnp.bfloat16)
    return call(
        kernel,
        row,
        ins,
        [(own, whole(own)), (oth, whole(oth))],
        scratch=[pltpu.VMEM((tokens, rows), jnp.bfloat16)],
        vmem=28,
    )


def place(plan, row, xg, arrived):
    count = len(arrived)
    tokens, width = arrived[0].shape
    table = [plan[f"theirs{j}"] for j in range(count)]

    def kernel(row_ref, *refs):
        g = pl.program_id(0)
        out_ref, tile_ref = refs[-2:]
        tile_ref[...] = jnp.zeros_like(tile_ref)
        for j in range(count):

            @pl.when(g == j)
            def _():
                out_ref[...] = refs[j][...]

    def column(g, row):
        at = row[table[0]]
        for j in range(1, count):
            at = jnp.where(g == j, row[table[j]], at)
        return (0, at)

    tile = struct((8, 128), jnp.float32)
    ins = [view.operand() for view in arrived]
    return call(
        kernel,
        row,
        ins + [(xg, HBM)],
        [
            (struct(xg.shape, xg.dtype), pl.BlockSpec((tokens, width), column)),
            (tile, whole(tile)),
        ],
        grid=(count,),
        aliases={1 + len(ins): 0},
    )


def adam(row, h, got, grad, weights, first, second, kept, after=()):
    rows, columns = got["a"].shape
    assert got["a"].start == 0
    steps = 4 if rows % 64 == 0 else 1
    size = rows // steps

    def kernel(row_ref, up_ref, dn_ref, grad_ref, w_ref, a_ref, b_ref, *refs):
        a_out, b_out, stepped = refs[-3:]
        gradient = grad_ref[...] + up_ref[...].astype(jnp.float32) + dn_ref[...].astype(jnp.float32)
        moment_a = beta_one * a_ref[...] + (1.0 - beta_one) * gradient
        moment_b = beta_two * b_ref[...] + (1.0 - beta_two) * gradient * gradient
        old = w_ref[...].astype(jnp.float32)
        update = moment_a * (1.0 / corr_one) / (jnp.sqrt(moment_b * (1.0 / corr_two)) + adam_eps)
        update = update + weight_decay * old
        a_out[...] = moment_a
        b_out[...] = moment_b
        stepped[...] = (old - learn_rate * update).astype(jnp.bfloat16)

    local = pl.BlockSpec((size, columns), lambda g, row: (g, 0))
    part = pl.BlockSpec((size, columns), lambda g, row: (g, h))
    ins = [(got["a"].array, local), (got["b"].array, local)]
    ins += [(a, part) for a in (grad, weights, first, second)]
    aliases = {}
    if kept is not None:
        aliases = {1 + len(ins): 0, 2 + len(ins): 1}
        ins += [(a, HBM) for a in kept]
    ins += after
    return call(
        kernel,
        row,
        ins,
        [
            (struct(first.shape, jnp.float32), part),
            (struct(second.shape, jnp.float32), part),
            (struct((rows, columns), jnp.bfloat16), local),
        ],
        grid=(steps,),
        aliases=aliases,
    )


def finish(plan, scalars, stepped, others, xg, piece, sums):
    rows, columns = stepped[0].shape
    tokens, width = piece.shape
    own, other = sums
    chunks, count = len(stepped), len(others[0])
    steps = 4 if rows % 64 == 0 and tokens % 64 == 0 else 1
    size, part = rows // steps, tokens // steps

    def kernel(row_ref, numerator_ref, partner_ref, *refs):
        piece_ref, own_ref, other_ref = refs[-7:-4]
        averaged_ref, xg_ref, kv_ref = refs[-3:]
        mix = numerator_ref[row_ref[plan["replica"]]].astype(jnp.float32) / mix_denom
        xg_ref[...] = piece_ref[...]
        kv_ref[...] = (own_ref[...] + other_ref[...].astype(jnp.float32)).astype(jnp.bfloat16)
        for j in range(count):

            @pl.when((partner_ref[0] == j + 1) | (count == 1))
            def _():
                for h in range(chunks):
                    mine, theirs = refs[h * (count + 1)], refs[h * (count + 1) + 1 + j]
                    averaged_ref[:, h * columns : (h + 1) * columns] = (
                        (1.0 - mix) * mine[...].astype(jnp.float32)
                        + mix * theirs[...].astype(jnp.float32)
                    ).astype(jnp.bfloat16)

    def lines(shape, at=0):
        return pl.BlockSpec(shape, lambda g, *scalars: (g, at))

    chosen = [
        pl.BlockSpec(
            (size, columns),
            lambda g, row, numerator, partner, j=j: (
                jnp.where((partner[0] == j + 1) | (count == 1), g, 0),
                0,
            ),
        )
        for j in range(count)
    ]
    theirs = plan[f"theirs{plan.depth - 1}"]
    ins = []
    for h in range(chunks):
        ins += [(stepped[h], lines((size, columns))), *zip(others[h], chosen)]
    ins += [
        (piece.array, lines((part, width), piece.start // width)),
        (own, lines((part, own.shape[1]))),
        (other.array, lines((part, other.count), other.start // other.count)),
        (xg, HBM),
    ]
    return call(
        kernel,
        scalars,
        ins,
        [
            (struct((rows, chunks * columns), jnp.bfloat16), lines((size, chunks * columns))),
            (
                struct(xg.shape, xg.dtype),
                pl.BlockSpec((part, width), lambda g, row, *scalars: (g, row[theirs])),
            ),
            (struct(own.shape, jnp.bfloat16), lines((part, own.shape[1]))),
        ],
        grid=(steps,),
        aliases={len(scalars) + len(ins) - 1: 1},
    )


def partner_rows(stepped, partner, replica, n_rep):
    if n_rep != 4:
        gathered = lax.all_gather(stepped, "rep", axis=0, tiled=False)
        return [lax.dynamic_index_in_dim(gathered, partner[replica], 0, keepdims=False)]
    far = lax.ppermute(stepped, "rep", [(r, r ^ 2) for r in range(4)])
    core = [(r, r ^ 1) for r in range(4)]
    return [lax.ppermute(stepped, "rep", core), far, lax.ppermute(far, "rep", core)]


def per_device(
    n_rep, n, activations, kv_weight, kv_cotangent, first_moment, second_moment, partner, mix_numerator
):
    act, weights, cot = activations[0], kv_weight[0], kv_cotangent[0]
    first, second = first_moment[0], second_moment[0]
    plan = Plan(n_rep, n)
    depth = plan.depth
    rows, columns = weights.shape
    size = columns // CHUNKS
    row = lax.dynamic_index_in_dim(
        jnp.asarray(plan.table), lax.axis_index(("rep", "fsdp")), 0, keepdims=False
    )
    links = {
        "a": [(i, i + 2 if i // 2 % 2 == 0 else i - 2) for i in range(n)],
        "b": [(i, i - 2 if i // 2 % 2 == 0 else i + 2) for i in range(n)],
    }
    links = {name: [p for p in pairs if 0 <= p[1] < n] for name, pairs in links.items()}
    swap = functools.partial(lax.ppermute, axis_name="fsdp", perm=[(i, i ^ 1) for i in range(n)])

    def exchange(bufs):
        return {name: lax.ppermute(bufs[name], "fsdp", links[name]) for name in links}

    def part(array, h):
        return View(array, h * size, size)

    opening = exchange({"a": weights, "b": weights})
    got = {(1, h): {link: part(opening[link], h) for link in links} for h in range(CHUNKS)}

    def arrivals(link, slot):
        if slot == 1:
            return [opening[link]]
        return [got[slot, h][link].array for h in range(CHUNKS)]

    def send(*turns, after=()):
        return swap(pack(plan, row, rows, [], act, turns, after))

    parcel = swap(cot)
    cot_oth = [part(parcel, h) for h in range(CHUNKS)]
    pieces = [View(send(0), 0, rows)]

    parcel = send(*range(1, depth - 1), after=[parcel, pieces[0].array])
    pieces += [View(parcel, k * rows, rows) for k in range(depth - 2)]

    arrived, shards, parts = [], [], []

    def shard_step(j, xg):
        candidates = [[weights]]
        if j > 0:
            candidates = [arrivals(*source) for source in plan.sources[j]]
        xg, parcel, shard = project(plan, row, j, candidates, act, cot, cot_oth, xg)
        shards.append(shard)
        parts.append(View(parcel, 0, rows))
        return xg

    def send_parts(views, turns, after):
        parcel = swap(pack(plan, row, rows, views, act, turns, after))
        arrived.extend(View(parcel, t * rows, rows) for t in range(len(views)))
        return parcel

    xg = shard_step(0, None)
    parcel = send_parts(parts, [depth - 1], [parcel])
    pieces.append(View(parcel, rows, rows))
    bufs = {}
    for s in range(2, depth + 1):
        if s == depth:
            for j in range(2, depth - 1):
                xg = shard_step(j, xg)
            send_parts(parts[1:], [], [parcel])
            grad = own_gradient(plan, row, act, pieces[depth - 1], cot, cot_oth)
            sums = values(plan, row, list(range(depth - 1)), shards, act, pieces, None)
        for h in range(CHUNKS):
            after = list(bufs.values())[:1]
            if s == 3 and h == 0:
                xg = shard_step(1, xg)
                after.append(parts[1].array)
            if s == depth and h == CHUNKS - 1:
                xg = shard_step(depth - 1, xg)
                kv_own, parcel = values(
                    plan, row, [depth - 1], shards[-1:], act, pieces, sums, parts[-1]
                )
                final = swap(parcel)
                after += [sums[0], grad]
            bufs = relay(
                plan, row, s, got[s - 1, h], act, pieces[: s - 1], part(cot, h), cot_oth[h], after
            )
            got[s, h] = {link: part(array, 0) for link, array in exchange(bufs).items()}
    scalars = (row, mix_numerator, partner)
    moments, placed = None, None
    stepped, others = [], []
    for h in range(CHUNKS):
        after = [] if h == 0 else [(placed_tile, ANY)]
        *moments, rows_now = adam(
            row, h, got[depth, h], grad, weights, first, second, moments, after
        )
        if placed is None:
            placed, placed_tile = place(plan, row, xg, arrived)
        stepped.append(rows_now)
        others.append(partner_rows(rows_now, partner, row[plan["replica"]], n_rep))
    averaged, x_grad, kv_out = finish(
        plan,
        scalars,
        stepped,
        others,
        placed,
        View(final, columns, rows),
        (kv_own, View(final, 0, columns)),
    )
    return (
        kv_out[None],
        x_grad[None],
        averaged[None],
        moments[0][None],
        moments[1][None],
    )


def solution(mesh):
    placed = P("rep", "fsdp", None)
    return jax.shard_map(
        functools.partial(per_device, mesh.shape["rep"], mesh.shape["fsdp"]),
        mesh=mesh,
        in_specs=(placed,) * 5 + (P(), P()),
        out_specs=(placed,) * 5,
        check_vma=False,
    )
```

```python
import functools

import jax
import jax.numpy as jnp
import numpy as np
from jax import lax
from jax.experimental import pallas as pl
from jax.experimental.pallas import tpu as pltpu
from jax.sharding import PartitionSpec as P

beta_one = 0.9
beta_two = 0.999
learn_rate = 0.02
weight_decay = 0.1
adam_eps = 1e-08
corr_one = 1.0 - beta_one**10
corr_two = 1.0 - beta_two**10
mix_denom = 64.0

CHUNKS = 2
MIB = 1 << 20
ANY = pl.BlockSpec(memory_space=pl.ANY)
HBM = pl.BlockSpec(memory_space=pltpu.HBM)

TN = (((0,), (0,)), ((), ()))
NT = (((1,), (1,)), ((), ()))


def dot(a, b, dims=(((1,), (0,)), ((), ()))):
    return lax.dot_general(a, b, dims, preferred_element_type=jnp.float32)


class Plan:
    def __init__(self, n_rep, n):
        self.depth = depth = n // 2
        self.columns = {}
        self.rows = [[] for _ in range(n_rep * n)]
        order = [
            sorted(range(depth), key=lambda q: (-abs(q - z), (q < z) != (2 * z >= depth)))
            for z in range(depth)
        ]
        self.sources = [set() for _ in range(depth)]
        arrivals = []
        for z in range(depth):
            below, above = ("b", "a") if z % 2 == 0 else ("a", "b")
            ups = [(z - t, (below, t)) for t in range(1, z + 1)]
            downs = [(z + t, (above, t)) for t in range(1, depth - z)]
            arrivals.append(downs + ups if 2 * z < depth else ups + downs)
            for j, (_, source) in enumerate(arrivals[z], 1):
                self.sources[j].add(source)
        self.sources = [sorted(s) for s in self.sources]
        for device in range(n_rep * n):
            replica, i = divmod(device, n)
            z, x = divmod(i, 2)
            put = functools.partial(self._put, device)
            put("replica", replica)
            put("own", i)
            for k in range(depth):
                put(f"pack{k}", 2 * order[z][k] + 1 - x)
            for s in range(2, depth + 1):
                up, down = z + 1 + depth - s, z - 1 - depth + s
                for link, q in zip("ab", (up, down) if z % 2 == 0 else (down, up)):
                    add = 0 <= q < depth
                    put(f"add_{link}{s}", int(add))
                    put(f"blk_{link}{s}", 2 * q + x if add else 0)
                    put(f"pos_{link}{s}", order[z].index(q) if add else 0)
            for j in range(depth):
                q, source = (z, None) if j == 0 else arrivals[z][j - 1]
                put(f"mine{j}", 2 * q + x)
                put(f"theirs{j}", 2 * q + 1 - x)
                put(f"piece{j}", order[z].index(q))
                put(f"source{j}", 0 if j == 0 else self.sources[j].index(source))
        self.table = np.asarray(self.rows, np.int32)

    def _put(self, i, name, value):
        column = self.columns.setdefault(name, len(self.columns))
        assert column == len(self.rows[i])
        self.rows[i].append(value)

    def __getitem__(self, name):
        return self.columns[name]


def call(kernel, row, ins, outs, grid=(1,), aliases=None, scratch=(), vmem=16):
    scalars = row if isinstance(row, tuple) else (row,)
    return pl.pallas_call(
        kernel,
        grid_spec=pltpu.PrefetchScalarGridSpec(
            num_scalar_prefetch=len(scalars),
            grid=grid,
            in_specs=[spec for _, spec in ins],
            out_specs=[spec for _, spec in outs],
            scratch_shapes=list(scratch),
        ),
        out_shape=[shape for shape, _ in outs],
        input_output_aliases=aliases or {},
        compiler_params=pltpu.CompilerParams(vmem_limit_bytes=vmem * MIB),
        cost_estimate=pl.CostEstimate(flops=0, bytes_accessed=0, transcendentals=0),
    )(*scalars, *[array for array, _ in ins])


def whole(array):
    rank = array.ndim
    return pl.BlockSpec(array.shape, lambda g, row: (0,) * rank)


def block(shape, column, scale=1, offset=0):
    return pl.BlockSpec(shape, lambda g, row: (0, row[column] * scale + offset))


def struct(shape, dtype):
    return jax.ShapeDtypeStruct(shape, dtype)


class View:
    def __init__(self, array, start, count):
        assert start % count == 0
        self.array, self.start, self.count = array, start, count
        self.shape = (array.shape[0], count)

    def operand(self):
        at = self.start // self.count
        return self.array, pl.BlockSpec(self.shape, lambda g, row: (0, at))


def pack(plan, row, width, views, act=None, turns=(), after=()):
    count = len(views) + len(turns)
    ins = [v.operand() for v in views]
    tokens = views[0].shape[0] if views else act.shape[0]
    ins += [(act, block((tokens, width), plan[f"pack{k}"])) for k in turns]
    sizes = [v.count for v in views] + [width] * len(turns)

    def kernel(row_ref, *refs):
        at = 0
        for ref, size in zip(refs[:count], sizes):
            refs[-1][:, at : at + size] = ref[...]
            at += size

    out = struct((tokens, sum(sizes)), jnp.bfloat16)
    return call(
        kernel,
        row,
        ins + [(a, ANY) for a in after],
        [(out, whole(out))],
    )[0]


def relay(plan, row, s, got, act, pieces, cot_own, cot_oth, after=()):
    (tokens, columns), rows = cot_own.shape, got["a"].shape[0]
    count = len(pieces)

    def kernel(row_ref, *refs):
        got_refs, act_refs = refs[0:2], refs[2:4]
        piece_refs = refs[4 : 4 + count]
        own_ref, oth_ref = refs[4 + count : 6 + count]
        out_refs, held = refs[-3:-1], refs[-1]
        for d, link in enumerate("ab"):
            add = row_ref[plan[f"add_{link}{s}"]]
            pos = row_ref[plan[f"pos_{link}{s}"]]

            @pl.when(add == 0)
            def _():
                out_refs[d][...] = got_refs[d][...]

            @pl.when(add == 1)
            def _():
                for j in range(count):

                    @pl.when(pos == j)
                    def _():
                        held[...] = piece_refs[j][...]

                total = dot(act_refs[d][...], own_ref[...], TN)
                total = total + dot(held[...], oth_ref[...], TN)
                out_refs[d][...] = (total + got_refs[d][...].astype(jnp.float32)).astype(jnp.bfloat16)

    ins = [got[link].operand() for link in "ba"]
    ins += [(act, block((tokens, rows), plan[f"blk_{link}{s}"])) for link in "ab"]
    ins += [view.operand() for view in (*pieces, cot_own, cot_oth)]
    ins += [(a, ANY) for a in after]
    out = struct((rows, columns), jnp.bfloat16)
    a, b = call(
        kernel,
        row,
        ins,
        [(out, whole(out)), (out, whole(out))],
        scratch=[pltpu.VMEM((tokens, rows), jnp.bfloat16)],
    )
    return {"a": a, "b": b}


def own_gradient(plan, row, act, piece, cot, cot_oth):
    tokens, columns = cot.shape
    rows = piece.shape[1]

    def kernel(row_ref, act_ref, piece_ref, own_ref, *refs):
        out_ref = refs[-1]
        at = 0
        for ref, view in zip(refs, cot_oth):
            part = slice(at, at + view.count)
            total = dot(act_ref[...], own_ref[:, part], TN)
            out_ref[:, part] = total + dot(piece_ref[...], ref[...], TN)
            at += view.count

    out = struct((rows, columns), jnp.float32)
    return call(
        kernel,
        row,
        [(act, block((tokens, rows), plan["own"])), piece.operand(), (cot, whole(cot))]
        + [view.operand() for view in cot_oth],
        [(out, whole(out))],
    )[0]


def project(plan, row, j, candidates, act, cot, cot_oth, xg_before):
    (tokens, columns), rows = cot.shape, candidates[0][0].shape[0]
    flat = [c for candidate in candidates for c in candidate]
    starts = np.cumsum([0] + [len(candidate) for candidate in candidates])
    parts = max(len(candidate) for candidate in candidates)
    n_w, n_c = len(flat), len(cot_oth)

    def kernel(row_ref, *refs):
        w_refs, cot_refs = refs[:n_w], refs[n_w : n_w + n_c]
        own_ref = refs[n_w + n_c]
        xg_own, xg_oth, w_out, sems = refs[-4:]
        for c in range(len(candidates)):

            @pl.when(row_ref[plan[f"source{j}"]] == c)
            def _():
                copies, at = [], 0
                for p in range(starts[c], starts[c + 1]):
                    to = w_out.at[:, pl.ds(at, flat[p].shape[1])]
                    copies.append(pltpu.make_async_copy(w_refs[p], to, sems.at[len(copies)]))
                    at += flat[p].shape[1]
                for copy in copies:
                    copy.start()
                for copy in copies:
                    copy.wait()

        total, at = 0.0, 0
        for ref, view in zip(cot_refs, cot_oth):
            total = total + dot(ref[...], w_out[:, at : at + view.count], NT)
            at += view.count
        xg_oth[...] = total.astype(jnp.bfloat16)
        xg_own[...] = dot(own_ref[...], w_out[...], NT).astype(jnp.bfloat16)

    ins = [(w, ANY) for w in flat] + [view.operand() for view in cot_oth] + [(cot, whole(cot))]
    aliases = {}
    if xg_before is not None:
        aliases = {1 + len(ins): 0}
        ins.append((xg_before, HBM))
    other = struct((tokens, rows), jnp.bfloat16)
    shard = struct((rows, columns), jnp.bfloat16)
    return call(
        kernel,
        row,
        ins,
        [
            (struct(act.shape, jnp.bfloat16), block((tokens, rows), plan[f"mine{j}"])),
            (other, whole(other)),
            (shard, whole(shard)),
        ],
        aliases=aliases,
        scratch=[pltpu.SemaphoreType.DMA((parts,))],
        vmem=20,
    )


def values(plan, row, turns, shards, act, pieces, kept, behind=None):
    rows, columns = shards[0].shape
    tokens = act.shape[0]
    count, n_p = len(turns), len(pieces)
    extra = 0 if behind is None else behind.count

    def kernel(row_ref, *refs):
        w_refs, act_refs = refs[:count], refs[count : 2 * count]
        piece_refs = refs[2 * count : 2 * count + n_p]
        rest = list(refs[2 * count + n_p : -3])
        own_out, oth_out, held = refs[-3:]
        own = oth = 0.0
        if kept is not None:
            own, oth = rest.pop(0)[...], rest.pop(0)[...]
        for t, j in enumerate(turns):
            for p in range(n_p):

                @pl.when(row_ref[plan[f"piece{j}"]] == p)
                def _():
                    held[...] = piece_refs[p][...]

            oth = oth + dot(held[...], w_refs[t][...])
            own = own + dot(act_refs[t][...], w_refs[t][...])
        oth_out[:, :columns] = oth.astype(oth_out.dtype)
        if behind is not None:
            oth_out[:, columns:] = rest.pop(0)[...]
        own_out[...] = own

    ins = [(w, whole(w)) for w in shards]
    ins += [(act, block((tokens, rows), plan[f"mine{j}"])) for j in turns]
    ins += [p.operand() for p in pieces]
    if kept is not None:
        ins += [(k, whole(k)) for k in kept]
    if behind is not None:
        ins.append(behind.operand())
    own = struct((tokens, columns), jnp.float32)
    oth = struct((tokens, columns + extra), jnp.float32 if behind is None else jnp.bfloat16)
    return call(
        kernel,
        row,
        ins,
        [(own, whole(own)), (oth, whole(oth))],
        scratch=[pltpu.VMEM((tokens, rows), jnp.bfloat16)],
        vmem=28,
    )


def place(plan, row, xg, arrived, first, sums=None):
    count = len(arrived)
    tokens, width = arrived[0].shape
    table = [plan[f"theirs{first + j}"] for j in range(count)]

    def kernel(row_ref, *refs):
        g = pl.program_id(0)
        out_ref, tile_ref = refs[-2:] if sums is None else refs[-3:-1]
        for j in range(count):

            @pl.when(g == j)
            def _():
                out_ref[...] = refs[j][...]

        tile_ref[...] = jnp.zeros_like(tile_ref)
        if sums is not None:
            total = refs[count][...] + refs[count + 1][...].astype(jnp.float32)
            refs[-1][...] = total.astype(jnp.bfloat16)

    def column(g, row):
        at = row[table[0]]
        for j in range(1, count):
            at = jnp.where(g == j, row[table[j]], at)
        return (0, at)

    ins = [view.operand() for view in arrived]
    outs = [(struct(xg.shape, xg.dtype), pl.BlockSpec((tokens, width), column))]
    tile = struct((8, 128), jnp.float32)
    outs.append((tile, whole(tile)))
    if sums is not None:
        own, other = sums
        kv_block = pl.BlockSpec((tokens // count, own.shape[1]), lambda g, row: (g, 0))
        assert other.start == 0
        ins += [(own, kv_block), (other.array, kv_block)]
        outs.append((struct(own.shape, jnp.bfloat16), kv_block))
    aliases = {1 + len(ins): 0}
    return call(
        kernel,
        row,
        ins + [(xg, HBM)],
        outs,
        grid=(count,),
        aliases=aliases,
    )


def adam(row, h, got, grad, weights, first, second, kept, after=()):
    rows, columns = got["a"].shape
    assert got["a"].start == 0
    steps = 2 if rows % 32 == 0 else 1
    size = rows // steps

    def kernel(row_ref, up_ref, dn_ref, grad_ref, w_ref, a_ref, b_ref, *refs):
        a_out, b_out, stepped = refs[-3:]
        gradient = grad_ref[...] + up_ref[...].astype(jnp.float32) + dn_ref[...].astype(jnp.float32)
        moment_a = beta_one * a_ref[...] + (1.0 - beta_one) * gradient
        moment_b = beta_two * b_ref[...] + (1.0 - beta_two) * gradient * gradient
        old = w_ref[...].astype(jnp.float32)
        update = moment_a * (1.0 / corr_one) / (jnp.sqrt(moment_b * (1.0 / corr_two)) + adam_eps)
        update = update + weight_decay * old
        a_out[...] = moment_a
        b_out[...] = moment_b
        stepped[...] = (old - learn_rate * update).astype(jnp.bfloat16)

    local = pl.BlockSpec((size, columns), lambda g, row: (g, 0))
    part = pl.BlockSpec((size, columns), lambda g, row: (g, h))
    ins = [(got["a"].array, local), (got["b"].array, local)]
    ins += [(a, part) for a in (grad, weights, first, second)]
    aliases = {}
    if kept is not None:
        aliases = {1 + len(ins): 0, 2 + len(ins): 1}
        ins += [(a, HBM) for a in kept]
    ins += after
    return call(
        kernel,
        row,
        ins,
        [
            (struct(first.shape, jnp.float32), part),
            (struct(second.shape, jnp.float32), part),
            (struct((rows, columns), jnp.bfloat16), local),
        ],
        grid=(steps,),
        aliases=aliases,
    )


def average(plan, scalars, stepped, others, after):
    rows, columns = stepped[0].shape
    chunks, count = len(stepped), len(others[0])
    steps = 2 if rows % 32 == 0 else 1
    size = rows // steps

    def kernel(row_ref, numerator_ref, partner_ref, *refs):
        mix = numerator_ref[row_ref[plan["replica"]]].astype(jnp.float32) / mix_denom
        for j in range(count):

            @pl.when((partner_ref[0] == j + 1) | (count == 1))
            def _():
                for h in range(chunks):
                    own, other = refs[h * (count + 1)], refs[h * (count + 1) + 1 + j]
                    refs[-1][:, h * columns : (h + 1) * columns] = (
                        (1.0 - mix) * own[...].astype(jnp.float32)
                        + mix * other[...].astype(jnp.float32)
                    ).astype(jnp.bfloat16)

    local = pl.BlockSpec((size, columns), lambda g, *scalars: (g, 0))
    full = pl.BlockSpec((size, chunks * columns), lambda g, *scalars: (g, 0))
    chosen = [
        pl.BlockSpec(
            (size, columns),
            lambda g, row, numerator, partner, j=j: (
                jnp.where((partner[0] == j + 1) | (count == 1), g, 0),
                0,
            ),
        )
        for j in range(count)
    ]
    ins = []
    for h in range(chunks):
        ins += [(stepped[h], local), *zip(others[h], chosen)]
    return call(
        kernel,
        scalars,
        ins + [(a, ANY) for a in after],
        [(struct((rows, chunks * columns), jnp.bfloat16), full)],
        grid=(steps,),
    )[0]


def partner_rows(stepped, partner, replica, n_rep):
    if n_rep != 4:
        gathered = lax.all_gather(stepped, "rep", axis=0, tiled=False)
        return [lax.dynamic_index_in_dim(gathered, partner[replica], 0, keepdims=False)]
    far = lax.ppermute(stepped, "rep", [(r, r ^ 2) for r in range(4)])
    core = [(r, r ^ 1) for r in range(4)]
    return [lax.ppermute(stepped, "rep", core), far, lax.ppermute(far, "rep", core)]


def per_device(
    n_rep, n, activations, kv_weight, kv_cotangent, first_moment, second_moment, partner, mix_numerator
):
    act, weights, cot = activations[0], kv_weight[0], kv_cotangent[0]
    first, second = first_moment[0], second_moment[0]
    plan = Plan(n_rep, n)
    depth = plan.depth
    rows, columns = weights.shape
    size = columns // CHUNKS
    row = lax.dynamic_index_in_dim(
        jnp.asarray(plan.table), lax.axis_index(("rep", "fsdp")), 0, keepdims=False
    )
    links = {
        "a": [(i, i + 2 if i // 2 % 2 == 0 else i - 2) for i in range(n)],
        "b": [(i, i - 2 if i // 2 % 2 == 0 else i + 2) for i in range(n)],
    }
    links = {name: [p for p in pairs if 0 <= p[1] < n] for name, pairs in links.items()}
    swap = functools.partial(lax.ppermute, axis_name="fsdp", perm=[(i, i ^ 1) for i in range(n)])

    def exchange(bufs):
        return {name: lax.ppermute(bufs[name], "fsdp", links[name]) for name in links}

    def part(array, h):
        return View(array, h * size, size)

    opening = exchange({"a": weights, "b": weights})
    got = {(1, h): {link: part(opening[link], h) for link in links} for h in range(CHUNKS)}

    def arrivals(link, slot):
        if slot == 1:
            return [opening[link]]
        return [got[slot, h][link].array for h in range(CHUNKS)]

    def send(*turns, after=()):
        return swap(pack(plan, row, rows, [], act, turns, after))

    parcel = swap(cot)
    cot_oth = [part(parcel, h) for h in range(CHUNKS)]
    pieces = [View(send(0), 0, rows)]

    parcel = send(*range(1, depth - 1), after=[parcel, pieces[0].array])
    pieces += [View(parcel, k * rows, rows) for k in range(depth - 2)]

    arrived, shards, parts = [], [], []

    def shard_step(j, xg):
        candidates = [[weights]]
        if j > 0:
            candidates = [arrivals(*source) for source in plan.sources[j]]
        xg, parcel, shard = project(plan, row, j, candidates, act, cot, cot_oth, xg)
        shards.append(shard)
        parts.append(View(parcel, 0, rows))
        return xg

    def send_parts(views, turns, after):
        parcel = swap(pack(plan, row, rows, views, act, turns, after))
        arrived.extend(View(parcel, t * rows, rows) for t in range(len(views)))
        return parcel

    xg = shard_step(0, None)
    parcel = send_parts(parts, [depth - 1], [parcel])
    pieces.append(View(parcel, rows, rows))
    bufs = {}
    for s in range(2, depth + 1):
        if s == depth:
            for j in range(2, depth - 1):
                xg = shard_step(j, xg)
            send_parts(parts[1:], [], [parcel])
            grad = own_gradient(plan, row, act, pieces[depth - 1], cot, cot_oth)
            sums = values(plan, row, list(range(depth - 1)), shards, act, pieces, None)
        for h in range(CHUNKS):
            after = list(bufs.values())[:1]
            if s == 3 and h == 0:
                xg = shard_step(1, xg)
                after.append(parts[1].array)
            if s == depth and h == CHUNKS - 1:
                xg = shard_step(depth - 1, xg)
                kv_own, parcel = values(
                    plan, row, [depth - 1], shards[-1:], act, pieces, sums, parts[-1]
                )
                final = swap(parcel)
                after += [sums[0], grad]
            bufs = relay(
                plan, row, s, got[s - 1, h], act, pieces[: s - 1], part(cot, h), cot_oth[h], after
            )
            got[s, h] = {link: part(array, 0) for link, array in exchange(bufs).items()}
    scalars = (row, mix_numerator, partner)
    moments, placed = None, None
    stepped, others = [], []
    for h in range(CHUNKS):
        after = [] if h == 0 else [(placed_tile, ANY)]
        *moments, rows_now = adam(
            row, h, got[depth, h], grad, weights, first, second, moments, after
        )
        if placed is None:
            placed, placed_tile = place(plan, row, xg, arrived, 0)
        stepped.append(rows_now)
        others.append(partner_rows(rows_now, partner, row[plan["replica"]], n_rep))
    views = [View(final, columns, rows)]
    kv_views = (kv_own, View(final, 0, columns))
    x_grad, tile, kv_out = place(plan, row, placed, views, depth - 1, kv_views)
    averaged = average(plan, scalars, stepped, others, [tile])
    return (
        kv_out[None],
        x_grad[None],
        averaged[None],
        moments[0][None],
        moments[1][None],
    )


def solution(mesh):
    placed = P("rep", "fsdp", None)
    return jax.shard_map(
        functools.partial(per_device, mesh.shape["rep"], mesh.shape["fsdp"]),
        mesh=mesh,
        in_specs=(placed,) * 5 + (P(), P()),
        out_specs=(placed,) * 5,
        check_vma=False,
    )
```

```python
import functools

import jax
import jax.numpy as jnp
import numpy as np
from jax import lax
from jax.experimental import pallas as pl
from jax.experimental.pallas import tpu as pltpu
from jax.sharding import PartitionSpec as P

beta_one = 0.9
beta_two = 0.999
learn_rate = 0.02
weight_decay = 0.1
adam_eps = 1e-08
corr_one = 1.0 - beta_one**10
corr_two = 1.0 - beta_two**10
mix_denom = 64.0

CHUNKS = 2
MIB = 1 << 20
ANY = pl.BlockSpec(memory_space=pl.ANY)
HBM = pl.BlockSpec(memory_space=pltpu.HBM)

TN = (((0,), (0,)), ((), ()))
NT = (((1,), (1,)), ((), ()))


def dot(a, b, dims=(((1,), (0,)), ((), ()))):
    return lax.dot_general(a, b, dims, preferred_element_type=jnp.float32)


class Plan:
    def __init__(self, n_rep, n):
        self.depth = depth = n // 2
        self.columns = {}
        self.rows = [[] for _ in range(n_rep * n)]
        order = [
            sorted(range(depth), key=lambda q: (-abs(q - z), (q < z) != (2 * z >= depth)))
            for z in range(depth)
        ]
        self.sources = [set() for _ in range(depth)]
        arrivals = []
        for z in range(depth):
            below, above = ("b", "a") if z % 2 == 0 else ("a", "b")
            ups = [(z - t, (below, t)) for t in range(1, z + 1)]
            downs = [(z + t, (above, t)) for t in range(1, depth - z)]
            arrivals.append(downs + ups if 2 * z < depth else ups + downs)
            for j, (_, source) in enumerate(arrivals[z], 1):
                self.sources[j].add(source)
        self.sources = [sorted(s) for s in self.sources]
        for device in range(n_rep * n):
            replica, i = divmod(device, n)
            z, x = divmod(i, 2)
            put = functools.partial(self._put, device)
            put("replica", replica)
            put("own", i)
            for k in range(depth):
                put(f"pack{k}", 2 * order[z][k] + 1 - x)
            for s in range(2, depth + 1):
                up, down = z + 1 + depth - s, z - 1 - depth + s
                for link, q in zip("ab", (up, down) if z % 2 == 0 else (down, up)):
                    add = 0 <= q < depth
                    put(f"add_{link}{s}", int(add))
                    put(f"blk_{link}{s}", 2 * q + x if add else 0)
                    put(f"pos_{link}{s}", order[z].index(q) if add else 0)
            for j in range(depth):
                q, source = (z, None) if j == 0 else arrivals[z][j - 1]
                put(f"mine{j}", 2 * q + x)
                put(f"theirs{j}", 2 * q + 1 - x)
                put(f"piece{j}", order[z].index(q))
                put(f"source{j}", 0 if j == 0 else self.sources[j].index(source))
        self.table = np.asarray(self.rows, np.int32)

    def _put(self, i, name, value):
        column = self.columns.setdefault(name, len(self.columns))
        assert column == len(self.rows[i])
        self.rows[i].append(value)

    def __getitem__(self, name):
        return self.columns[name]


def call(kernel, row, ins, outs, grid=(1,), aliases=None, scratch=(), vmem=16):
    scalars = row if isinstance(row, tuple) else (row,)
    return pl.pallas_call(
        kernel,
        grid_spec=pltpu.PrefetchScalarGridSpec(
            num_scalar_prefetch=len(scalars),
            grid=grid,
            in_specs=[spec for _, spec in ins],
            out_specs=[spec for _, spec in outs],
            scratch_shapes=list(scratch),
        ),
        out_shape=[shape for shape, _ in outs],
        input_output_aliases=aliases or {},
        compiler_params=pltpu.CompilerParams(vmem_limit_bytes=vmem * MIB),
        cost_estimate=pl.CostEstimate(flops=0, bytes_accessed=0, transcendentals=0),
    )(*scalars, *[array for array, _ in ins])


def whole(array):
    rank = array.ndim
    return pl.BlockSpec(array.shape, lambda g, row: (0,) * rank)


def block(shape, column, scale=1, offset=0):
    return pl.BlockSpec(shape, lambda g, row: (0, row[column] * scale + offset))


def struct(shape, dtype):
    return jax.ShapeDtypeStruct(shape, dtype)


class View:
    def __init__(self, array, start, count):
        assert start % count == 0
        self.array, self.start, self.count = array, start, count
        self.shape = (array.shape[0], count)

    def operand(self):
        at = self.start // self.count
        return self.array, pl.BlockSpec(self.shape, lambda g, row: (0, at))


def pack(plan, row, width, views, act=None, turns=(), after=()):
    count = len(views) + len(turns)
    ins = [v.operand() for v in views]
    tokens = views[0].shape[0] if views else act.shape[0]
    ins += [(act, block((tokens, width), plan[f"pack{k}"])) for k in turns]
    sizes = [v.count for v in views] + [width] * len(turns)

    def kernel(row_ref, *refs):
        at = 0
        for ref, size in zip(refs[:count], sizes):
            refs[-1][:, at : at + size] = ref[...]
            at += size

    out = struct((tokens, sum(sizes)), jnp.bfloat16)
    return call(
        kernel,
        row,
        ins + [(a, ANY) for a in after],
        [(out, whole(out))],
    )[0]


def relay(plan, row, s, got, act, pieces, cot_own, cot_oth, after=()):
    (tokens, columns), rows = cot_own.shape, got["a"].shape[0]
    count = len(pieces)

    def kernel(row_ref, *refs):
        got_refs, act_refs = refs[0:2], refs[2:4]
        piece_refs = refs[4 : 4 + count]
        own_ref, oth_ref = refs[4 + count : 6 + count]
        out_refs, held = refs[-3:-1], refs[-1]
        for d, link in enumerate("ab"):
            add = row_ref[plan[f"add_{link}{s}"]]
            pos = row_ref[plan[f"pos_{link}{s}"]]

            @pl.when(add == 0)
            def _():
                out_refs[d][...] = got_refs[d][...]

            @pl.when(add == 1)
            def _():
                for j in range(count):

                    @pl.when(pos == j)
                    def _():
                        held[...] = piece_refs[j][...]

                total = dot(act_refs[d][...], own_ref[...], TN)
                total = total + dot(held[...], oth_ref[...], TN)
                out_refs[d][...] = (total + got_refs[d][...].astype(jnp.float32)).astype(jnp.bfloat16)

    ins = [got[link].operand() for link in "ba"]
    ins += [(act, block((tokens, rows), plan[f"blk_{link}{s}"])) for link in "ab"]
    ins += [view.operand() for view in (*pieces, cot_own, cot_oth)]
    ins += [(a, ANY) for a in after]
    out = struct((rows, columns), jnp.bfloat16)
    a, b = call(
        kernel,
        row,
        ins,
        [(out, whole(out)), (out, whole(out))],
        scratch=[pltpu.VMEM((tokens, rows), jnp.bfloat16)],
    )
    return {"a": a, "b": b}


def own_gradient(plan, row, act, piece, cot, cot_oth):
    tokens, columns = cot.shape
    rows = piece.shape[1]

    def kernel(row_ref, act_ref, piece_ref, own_ref, *refs):
        out_ref = refs[-1]
        at = 0
        for ref, view in zip(refs, cot_oth):
            part = slice(at, at + view.count)
            total = dot(act_ref[...], own_ref[:, part], TN)
            out_ref[:, part] = total + dot(piece_ref[...], ref[...], TN)
            at += view.count

    out = struct((rows, columns), jnp.float32)
    return call(
        kernel,
        row,
        [(act, block((tokens, rows), plan["own"])), piece.operand(), (cot, whole(cot))]
        + [view.operand() for view in cot_oth],
        [(out, whole(out))],
    )[0]


def project(plan, row, j, candidates, act, cot, cot_oth, xg_before):
    (tokens, columns), rows = cot.shape, candidates[0][0].shape[0]
    flat = [c for candidate in candidates for c in candidate]
    starts = np.cumsum([0] + [len(candidate) for candidate in candidates])
    parts = max(len(candidate) for candidate in candidates)
    n_w, n_c = len(flat), len(cot_oth)

    def kernel(row_ref, *refs):
        w_refs, cot_refs = refs[:n_w], refs[n_w : n_w + n_c]
        own_ref = refs[n_w + n_c]
        xg_own, xg_oth, w_out, sems = refs[-4:]
        for c in range(len(candidates)):

            @pl.when(row_ref[plan[f"source{j}"]] == c)
            def _():
                copies, at = [], 0
                for p in range(starts[c], starts[c + 1]):
                    to = w_out.at[:, pl.ds(at, flat[p].shape[1])]
                    copies.append(pltpu.make_async_copy(w_refs[p], to, sems.at[len(copies)]))
                    at += flat[p].shape[1]
                for copy in copies:
                    copy.start()
                for copy in copies:
                    copy.wait()

        total, at = 0.0, 0
        for ref, view in zip(cot_refs, cot_oth):
            total = total + dot(ref[...], w_out[:, at : at + view.count], NT)
            at += view.count
        xg_oth[...] = total.astype(jnp.bfloat16)
        xg_own[...] = dot(own_ref[...], w_out[...], NT).astype(jnp.bfloat16)

    ins = [(w, ANY) for w in flat] + [view.operand() for view in cot_oth] + [(cot, whole(cot))]
    aliases = {}
    if xg_before is not None:
        aliases = {1 + len(ins): 0}
        ins.append((xg_before, HBM))
    other = struct((tokens, rows), jnp.bfloat16)
    shard = struct((rows, columns), jnp.bfloat16)
    return call(
        kernel,
        row,
        ins,
        [
            (struct(act.shape, jnp.bfloat16), block((tokens, rows), plan[f"mine{j}"])),
            (other, whole(other)),
            (shard, whole(shard)),
        ],
        aliases=aliases,
        scratch=[pltpu.SemaphoreType.DMA((parts,))],
        vmem=20,
    )


def values(plan, row, turns, shards, act, pieces, kept, behind=None):
    rows, columns = shards[0].shape
    tokens = act.shape[0]
    count, n_p = len(turns), len(pieces)
    extra = 0 if behind is None else behind.count

    def kernel(row_ref, *refs):
        w_refs, act_refs = refs[:count], refs[count : 2 * count]
        piece_refs = refs[2 * count : 2 * count + n_p]
        rest = list(refs[2 * count + n_p : -3])
        own_out, oth_out, held = refs[-3:]
        own = oth = 0.0
        if kept is not None:
            own, oth = rest.pop(0)[...], rest.pop(0)[...]
        for t, j in enumerate(turns):
            for p in range(n_p):

                @pl.when(row_ref[plan[f"piece{j}"]] == p)
                def _():
                    held[...] = piece_refs[p][...]

            oth = oth + dot(held[...], w_refs[t][...])
            own = own + dot(act_refs[t][...], w_refs[t][...])
        oth_out[:, :columns] = oth.astype(oth_out.dtype)
        if behind is not None:
            oth_out[:, columns:] = rest.pop(0)[...]
        own_out[...] = own

    ins = [(w, whole(w)) for w in shards]
    ins += [(act, block((tokens, rows), plan[f"mine{j}"])) for j in turns]
    ins += [p.operand() for p in pieces]
    if kept is not None:
        ins += [(k, whole(k)) for k in kept]
    if behind is not None:
        ins.append(behind.operand())
    own = struct((tokens, columns), jnp.float32)
    oth = struct((tokens, columns + extra), jnp.float32 if behind is None else jnp.bfloat16)
    return call(
        kernel,
        row,
        ins,
        [(own, whole(own)), (oth, whole(oth))],
        scratch=[pltpu.VMEM((tokens, rows), jnp.bfloat16)],
        vmem=28,
    )


def place(plan, row, xg, arrived, first, sums=None):
    count = len(arrived)
    tokens, width = arrived[0].shape
    table = [plan[f"theirs{first + j}"] for j in range(count)]

    def kernel(row_ref, *refs):
        g = pl.program_id(0)
        out_ref, tile_ref = refs[-2:] if sums is None else refs[-3:-1]
        for j in range(count):

            @pl.when(g == j)
            def _():
                out_ref[...] = refs[j][...]

        tile_ref[...] = jnp.zeros_like(tile_ref)
        if sums is not None:
            total = refs[count][...] + refs[count + 1][...].astype(jnp.float32)
            refs[-1][...] = total.astype(jnp.bfloat16)

    def column(g, row):
        at = row[table[0]]
        for j in range(1, count):
            at = jnp.where(g == j, row[table[j]], at)
        return (0, at)

    ins = [view.operand() for view in arrived]
    outs = [(struct(xg.shape, xg.dtype), pl.BlockSpec((tokens, width), column))]
    tile = struct((8, 128), jnp.float32)
    outs.append((tile, whole(tile)))
    if sums is not None:
        own, other = sums
        kv_block = pl.BlockSpec((tokens // count, own.shape[1]), lambda g, row: (g, 0))
        assert other.start == 0
        ins += [(own, kv_block), (other.array, kv_block)]
        outs.append((struct(own.shape, jnp.bfloat16), kv_block))
    aliases = {1 + len(ins): 0}
    return call(
        kernel,
        row,
        ins + [(xg, HBM)],
        outs,
        grid=(count,),
        aliases=aliases,
    )


def adam(row, h, got, grad, weights, first, second, kept, after=()):
    rows, columns = got["a"].shape
    assert got["a"].start == 0
    steps = 2 if rows % 32 == 0 else 1
    size = rows // steps

    def kernel(row_ref, up_ref, dn_ref, grad_ref, w_ref, a_ref, b_ref, *refs):
        a_out, b_out, stepped = refs[-3:]
        gradient = grad_ref[...] + up_ref[...].astype(jnp.float32) + dn_ref[...].astype(jnp.float32)
        moment_a = beta_one * a_ref[...] + (1.0 - beta_one) * gradient
        moment_b = beta_two * b_ref[...] + (1.0 - beta_two) * gradient * gradient
        old = w_ref[...].astype(jnp.float32)
        update = moment_a * (1.0 / corr_one) / (jnp.sqrt(moment_b * (1.0 / corr_two)) + adam_eps)
        update = update + weight_decay * old
        a_out[...] = moment_a
        b_out[...] = moment_b
        stepped[...] = (old - learn_rate * update).astype(jnp.bfloat16)

    local = pl.BlockSpec((size, columns), lambda g, row: (g, 0))
    part = pl.BlockSpec((size, columns), lambda g, row: (g, h))
    ins = [(got["a"].array, local), (got["b"].array, local)]
    ins += [(a, part) for a in (grad, weights, first, second)]
    aliases = {}
    if kept is not None:
        aliases = {1 + len(ins): 0, 2 + len(ins): 1}
        ins += [(a, HBM) for a in kept]
    ins += after
    return call(
        kernel,
        row,
        ins,
        [
            (struct(first.shape, jnp.float32), part),
            (struct(second.shape, jnp.float32), part),
            (struct((rows, columns), jnp.bfloat16), local),
        ],
        grid=(steps,),
        aliases=aliases,
    )


def average(plan, scalars, stepped, others, after):
    rows, columns = stepped[0].shape
    chunks, count = len(stepped), len(others[0])
    size = rows

    def kernel(row_ref, numerator_ref, partner_ref, *refs):
        mix = numerator_ref[row_ref[plan["replica"]]].astype(jnp.float32) / mix_denom
        for j in range(count):

            @pl.when((partner_ref[0] == j + 1) | (count == 1))
            def _():
                for h in range(chunks):
                    own, other = refs[h * (count + 1)], refs[h * (count + 1) + 1 + j]
                    refs[-1][:, h * columns : (h + 1) * columns] = (
                        (1.0 - mix) * own[...].astype(jnp.float32)
                        + mix * other[...].astype(jnp.float32)
                    ).astype(jnp.bfloat16)

    local = pl.BlockSpec((size, columns), lambda g, *scalars: (g, 0))
    full = pl.BlockSpec((size, chunks * columns), lambda g, *scalars: (g, 0))
    chosen = [
        pl.BlockSpec(
            (size, columns),
            lambda g, row, numerator, partner, j=j: (
                jnp.where((partner[0] == j + 1) | (count == 1), g, 0),
                0,
            ),
        )
        for j in range(count)
    ]
    ins = []
    for h in range(chunks):
        ins += [(stepped[h], local), *zip(others[h], chosen)]
    return call(
        kernel,
        scalars,
        ins + [(a, ANY) for a in after],
        [(struct((rows, chunks * columns), jnp.bfloat16), full)],
        vmem=24,
    )[0]


def partner_rows(stepped, partner, replica, n_rep):
    if n_rep != 4:
        gathered = lax.all_gather(stepped, "rep", axis=0, tiled=False)
        return [lax.dynamic_index_in_dim(gathered, partner[replica], 0, keepdims=False)]
    far = lax.ppermute(stepped, "rep", [(r, r ^ 2) for r in range(4)])
    core = [(r, r ^ 1) for r in range(4)]
    return [lax.ppermute(stepped, "rep", core), far, lax.ppermute(far, "rep", core)]


def per_device(
    n_rep, n, activations, kv_weight, kv_cotangent, first_moment, second_moment, partner, mix_numerator
):
    act, weights, cot = activations[0], kv_weight[0], kv_cotangent[0]
    first, second = first_moment[0], second_moment[0]
    plan = Plan(n_rep, n)
    depth = plan.depth
    rows, columns = weights.shape
    size = columns // CHUNKS
    row = lax.dynamic_index_in_dim(
        jnp.asarray(plan.table), lax.axis_index(("rep", "fsdp")), 0, keepdims=False
    )
    links = {
        "a": [(i, i + 2 if i // 2 % 2 == 0 else i - 2) for i in range(n)],
        "b": [(i, i - 2 if i // 2 % 2 == 0 else i + 2) for i in range(n)],
    }
    links = {name: [p for p in pairs if 0 <= p[1] < n] for name, pairs in links.items()}
    swap = functools.partial(lax.ppermute, axis_name="fsdp", perm=[(i, i ^ 1) for i in range(n)])

    def exchange(bufs):
        return {name: lax.ppermute(bufs[name], "fsdp", links[name]) for name in links}

    def part(array, h):
        return View(array, h * size, size)

    opening = exchange({"a": weights, "b": weights})
    got = {(1, h): {link: part(opening[link], h) for link in links} for h in range(CHUNKS)}

    def arrivals(link, slot):
        if slot == 1:
            return [opening[link]]
        return [got[slot, h][link].array for h in range(CHUNKS)]

    def send(*turns, after=()):
        return swap(pack(plan, row, rows, [], act, turns, after))

    parcel = swap(cot)
    cot_oth = [part(parcel, h) for h in range(CHUNKS)]
    pieces = [View(send(0), 0, rows)]

    parcel = send(*range(1, depth - 1), after=[parcel, pieces[0].array])
    pieces += [View(parcel, k * rows, rows) for k in range(depth - 2)]

    arrived, shards, parts = [], [], []

    def shard_step(j, xg):
        candidates = [[weights]]
        if j > 0:
            candidates = [arrivals(*source) for source in plan.sources[j]]
        xg, parcel, shard = project(plan, row, j, candidates, act, cot, cot_oth, xg)
        shards.append(shard)
        parts.append(View(parcel, 0, rows))
        return xg

    def send_parts(views, turns, after):
        parcel = swap(pack(plan, row, rows, views, act, turns, after))
        arrived.extend(View(parcel, t * rows, rows) for t in range(len(views)))
        return parcel

    xg = shard_step(0, None)
    parcel = send_parts(parts, [depth - 1], [parcel])
    pieces.append(View(parcel, rows, rows))
    bufs = {}
    for s in range(2, depth + 1):
        if s == depth:
            for j in range(2, depth - 1):
                xg = shard_step(j, xg)
            send_parts(parts[1:], [], [parcel])
            grad = own_gradient(plan, row, act, pieces[depth - 1], cot, cot_oth)
            sums = values(plan, row, list(range(depth - 1)), shards, act, pieces, None)
        for h in range(CHUNKS):
            after = list(bufs.values())[:1]
            if s == 3 and h == 0:
                xg = shard_step(1, xg)
                after.append(parts[1].array)
            if s == depth and h == CHUNKS - 1:
                xg = shard_step(depth - 1, xg)
                kv_own, parcel = values(
                    plan, row, [depth - 1], shards[-1:], act, pieces, sums, parts[-1]
                )
                final = swap(parcel)
                after += [sums[0], grad]
            bufs = relay(
                plan, row, s, got[s - 1, h], act, pieces[: s - 1], part(cot, h), cot_oth[h], after
            )
            got[s, h] = {link: part(array, 0) for link, array in exchange(bufs).items()}
    scalars = (row, mix_numerator, partner)
    moments, placed = None, None
    stepped, others = [], []
    for h in range(CHUNKS):
        after = [] if h == 0 else [(placed_tile, ANY)]
        *moments, rows_now = adam(
            row, h, got[depth, h], grad, weights, first, second, moments, after
        )
        if placed is None:
            placed, placed_tile = place(plan, row, xg, arrived, 0)
        stepped.append(rows_now)
        others.append(partner_rows(rows_now, partner, row[plan["replica"]], n_rep))
    views = [View(final, columns, rows)]
    kv_views = (kv_own, View(final, 0, columns))
    x_grad, tile, kv_out = place(plan, row, placed, views, depth - 1, kv_views)
    averaged = average(plan, scalars, stepped, others, [tile])
    return (
        kv_out[None],
        x_grad[None],
        averaged[None],
        moments[0][None],
        moments[1][None],
    )


def solution(mesh):
    placed = P("rep", "fsdp", None)
    return jax.shard_map(
        functools.partial(per_device, mesh.shape["rep"], mesh.shape["fsdp"]),
        mesh=mesh,
        in_specs=(placed,) * 5 + (P(), P()),
        out_specs=(placed,) * 5,
        check_vma=False,
    )
```
